32 devices in a mesh: section: 4 (over x, core), dp: 8 (over z, y).
Axes of the slice: x: 2, y: 2, z: 4, core: 2. Of those that a mesh axis runs over, the one named last changes fastest.
Arguments:
- global_rows: bfloat16 [16, 2, 197, 384], P('dp'), may hold values from -6 to 6
- local_rows: bfloat16 [16, 10, 37, 384], P('dp'), may hold values from -6 to 6
- patch_rank: int32 [16, 2, 196], P('dp'), may hold values from 0 to 195, as said below
- ratio_bin: int32 [16], P('dp'), may hold values from 0 to 4
- mask_token: bfloat16 [1, 384], replicated, may hold values from -4 to 4
- attend_gain: bfloat16 [2, 384], replicated, may hold values from 0.099609375 to 1.8984375
- attend_shift: bfloat16 [2, 384], replicated, may hold values from -2 to 2
- triple_weight: bfloat16 [2, 384, 1152], replicated, may hold values from -0.3125 to 0.3125
- pair_bias: bfloat16 [2, 768], replicated, may hold values from -3 to 3
- output_weight: bfloat16 [2, 384, 384], replicated, may hold values from -2.5 to 2.5
- output_bias: bfloat16 [2, 384], replicated, may hold values from -2 to 2
- expand_gain: bfloat16 [2, 384], replicated, may hold values from 0.099609375 to 1.8984375
- expand_shift: bfloat16 [2, 384], replicated, may hold values from -2 to 2
- up_weight: bfloat16 [2, 384, 1536], replicated, may hold values from -0.3125 to 0.3125
- up_bias: bfloat16 [2, 1536], replicated, may hold values from -3 to 3
- down_weight: bfloat16 [2, 1536, 384], replicated, may hold values from -0.15625 to 0.15625
- down_bias: bfloat16 [2, 384], replicated, may hold values from -2 to 2
- grad_global: bfloat16 [16, 2, 197, 384], P('dp'), may hold values from -6 to 6
- grad_local: bfloat16 [16, 10, 37, 384], P('dp'), may hold values from -6 to 6
Outputs:
- out_global: float32 [16, 2, 197, 384], P('dp', None, None, 'section')
- out_local: float32 [16, 10, 37, 384], P('dp', None, None, 'section')
- input_grad_global: float32 [16, 2, 197, 384], P('dp', None, None, 'section')
- input_grad_local: float32 [16, 10, 37, 384], P('dp', None, None, 'section')
- token_grad: float32 [1, 384], P(None, 'section')
- attend_gain_grad: float32 [2, 384], P(None, 'section')
- attend_shift_grad: float32 [2, 384], P(None, 'section')
- triple_weight_grad: float32 [2, 384, 1152], P(None, 'section')
- pair_bias_grad: float32 [2, 768], P(None, 'section')
- output_weight_grad: float32 [2, 384, 384], P(None, 'section')
- output_bias_grad: float32 [2, 384], P(None, 'section')
- expand_gain_grad: float32 [2, 384], P(None, 'section')
- expand_shift_grad: float32 [2, 384], P(None, 'section')
- up_weight_grad: float32 [2, 384, 1536], P(None, 'section')
- up_bias_grad: float32 [2, 1536], P(None, 'section')
- down_weight_grad: float32 [2, 1536, 384], P(None, 'section')
- down_bias_grad: float32 [2, 384], P(None, 'section')
The draws below stay inside these ranges and needn't reach their ends.
Inputs may be any that keep to these rules, and one draw needn't show every extreme that they name: In each global crop, patch_rank holds every number from 0 to 195 once; the four patches of each aligned 2 x 2 square of the crop's 14 x 14 grid of patches (row-major) hold four consecutive ranks that start at a multiple of 4.
All inputs are finite; a program needn't handle non-finite values.
Results may differ from the reference program's by a relative error of at most 0.015.
Values may be sent and summed in bfloat16 or wider, within the bound.
No kernel may reach another device: no remote copies, remote signals or barrier semaphores. Data moves between devices by JAX's collectives and lax.ppermute only.
A program may use at most 320 MiB of HBM per device.

```python
import math
import jax
import jax.numpy as jnp
from jax import lax

D = 384
HEADS = 6
FF = 1536
HEAD = 64
LAYERS = 2
GLOBAL_LEN = 197
LOCAL_LEN = 37
GLOBAL_CROPS = 2
LOCAL_CROPS = 10
PATCHES = 196
IMAGES = 16


def draw_patch_rank(key, part):
    key = jax.random.fold_in(key, 7)
    grid_side = math.isqrt(PATCHES)
    half_side = grid_side // 2
    blocks = half_side * half_side
    subkeys = jax.random.split(key, IMAGES * GLOBAL_CROPS)
    orders = jax.vmap(lambda subkey: jax.random.permutation(subkey, blocks))(subkeys)
    places = jnp.argsort(orders, axis=-1, stable=True)
    patch_index = jnp.arange(PATCHES)
    row_index = patch_index // grid_side
    column_index = patch_index % grid_side
    block_index = row_index // 2 * half_side + column_index // 2
    inside = row_index % 2 * 2 + column_index % 2
    rank_table = places[:, block_index] * 4 + inside[None, :]
    return rank_table.reshape(IMAGES, GLOBAL_CROPS, PATCHES).astype(jnp.int32)


def touch_ends(drawn, own_key, smallest, top_value):
    extent = drawn.shape
    index_at = [jax.random.randint(jax.random.fold_in(own_key, axis), (), 0, extent[axis]) for axis in range(len(extent))]
    drawn = drawn.at[tuple(index_at)].set(smallest)
    longest = extent.index(max(extent))
    index_at[longest] = (index_at[longest] + 1) % extent[longest]
    return drawn.at[tuple(index_at)].set(top_value)


def shard_levels(stream_key, dims, cuts, smallest, largest):
    def one(axis_at, blocks):
        heights = jax.random.uniform(jax.random.fold_in(jax.random.fold_in(stream_key, 6), axis_at), (blocks,), jnp.float32, smallest / len(cuts), largest / len(cuts))
        return jnp.repeat(jnp.exp(heights), dims[axis_at] // blocks).reshape((-1,) + (1,) * (len(dims) - axis_at - 1))

    gain = one(*cuts[0])
    for cut in cuts[1:]:
        gain = gain * one(*cut)
    return gain


def scatter_about(own_key, shape, spread, most, cuts=(), dtype=jnp.bfloat16):
    factor_of = shard_levels(own_key, shape, cuts, -0.22, 0.18) if cuts else 1.0
    drawn = jax.random.normal(own_key, shape, jnp.float32) * spread * factor_of
    return jnp.minimum(jnp.maximum(drawn, -most), most).astype(dtype)


def setup_inputs(seed: int = 0) -> dict:
    key_of = jax.random.split(jax.random.key(seed), 20)
    global_rows = scatter_about(key_of[0], (IMAGES, GLOBAL_CROPS, GLOBAL_LEN, D), 1.0, 6.0, ((0, 8),))
    local_rows = scatter_about(key_of[1], (IMAGES, LOCAL_CROPS, LOCAL_LEN, D), 1.0, 6.0, ((0, 8),))
    patch_rank = draw_patch_rank(jax.random.fold_in(key_of[19], 71), 0)
    ratio_bin = touch_ends(jax.random.randint(key_of[3], (IMAGES,), 0, 5), jax.random.fold_in(key_of[3], 1), 0, 4).astype(jnp.int32)
    mask_token = scatter_about(key_of[4], (1, D), 1.0, 4.0)
    attend_gain = jnp.clip(1.0 + 0.18 * jax.random.normal(key_of[5], (LAYERS, D), jnp.float32), 0.099609375, 1.8984375).astype(jnp.bfloat16)
    attend_shift = scatter_about(key_of[6], (LAYERS, D), 0.3, 2.0)
    triple_weight = scatter_about(key_of[7], (LAYERS, D, 3 * D), D ** -0.5, 0.3125)
    pair_bias = scatter_about(key_of[8], (LAYERS, 2 * D), 0.5, 3.0)
    output_weight = scatter_about(key_of[9], (LAYERS, D, D), (max(D // 64, 1)) ** -0.5, 2.5)
    output_bias = scatter_about(key_of[10], (LAYERS, D), 0.3, 2.0)
    expand_gain = jnp.clip(1.0 + 0.18 * jax.random.normal(key_of[11], (LAYERS, D), jnp.float32), 0.099609375, 1.8984375).astype(jnp.bfloat16)
    expand_shift = scatter_about(key_of[12], (LAYERS, D), 0.3, 2.0)
    up_weight = scatter_about(key_of[13], (LAYERS, D, FF), D ** -0.5, 0.3125)
    up_bias = scatter_about(key_of[14], (LAYERS, FF), 0.5, 3.0)
    down_weight = scatter_about(key_of[15], (LAYERS, FF, D), FF ** -0.5, 0.15625)
    down_bias = scatter_about(key_of[16], (LAYERS, D), 0.3, 2.0)
    grad_global = scatter_about(key_of[17], (IMAGES, GLOBAL_CROPS, GLOBAL_LEN, D), 1.0, 6.0, ((0, 8),))
    grad_local = scatter_about(key_of[18], (IMAGES, LOCAL_CROPS, LOCAL_LEN, D), 1.0, 6.0, ((0, 8),))
    return dict(global_rows=global_rows, local_rows=local_rows, patch_rank=patch_rank, ratio_bin=ratio_bin, mask_token=mask_token, attend_gain=attend_gain, attend_shift=attend_shift, triple_weight=triple_weight, pair_bias=pair_bias, output_weight=output_weight, output_bias=output_bias, expand_gain=expand_gain, expand_shift=expand_shift, up_weight=up_weight, up_bias=up_bias, down_weight=down_weight, down_bias=down_bias, grad_global=grad_global, grad_local=grad_local)


@jax.custom_vjp
def low(v):
    return lax.optimization_barrier(v.astype(jnp.bfloat16)).astype(jnp.float32)

@jax.custom_vjp
def low_back(v):
    return v

def low_keep(v):
    return (low(v), None)

def low_pass(kept, grad):
    return (grad,)

def back_keep(v):
    return (v, None)

def back_low(kept, grad):
    return (low(grad),)
low.defvjp(low_keep, low_pass)
low_back.defvjp(back_keep, back_low)
highest = lax.Precision.HIGHEST
epsilon = 1e-06

def send_both(value):
    return low_back(low(value))

def layer_norm(hidden, norm_gain, norm_shift):
    average = lax.optimization_barrier(jnp.mean(hidden, axis=-1, keepdims=True))
    centred = hidden - average
    variance = lax.optimization_barrier(jnp.mean(centred * centred, axis=-1, keepdims=True))
    return centred * lax.rsqrt(variance + epsilon) * norm_gain + norm_shift

def attend(hidden, layer_index, weights):
    attend_gain, attend_shift, triple_weight, pair_bias, output_weight, output_bias = weights
    normed = low(layer_norm(hidden, attend_gain[layer_index], attend_shift[layer_index]))
    project = jnp.einsum('nld,de->nle', normed, triple_weight[layer_index], precision=highest)
    queries = send_both(project[..., :D] + pair_bias[layer_index, :D])
    key_rows = send_both(project[..., D:2 * D])
    value_rows = send_both(project[..., 2 * D:] + pair_bias[layer_index, D:])
    split_shape = hidden.shape[:2] + (HEADS, HEAD)
    scores = jnp.einsum('nqhd,nkhd->nhqk', queries.reshape(split_shape), key_rows.reshape(split_shape), precision=highest)
    scores = low_back(scores * (1.0 / math.sqrt(HEAD)))
    probable = low(jax.nn.softmax(scores, axis=-1))
    context = jnp.einsum('nhqk,nkhd->nqhd', probable, value_rows.reshape(split_shape), precision=highest)
    context = send_both(context.reshape(hidden.shape))
    return hidden + jnp.einsum('nld,de->nle', context, output_weight[layer_index], precision=highest) + output_bias[layer_index]

def expand(hidden, layer_index, weights):
    expand_gain, expand_shift, up_weight, up_bias, down_weight, down_bias = weights
    normed = low(layer_norm(hidden, expand_gain[layer_index], expand_shift[layer_index]))
    before = low_back(jnp.einsum('nld,df->nlf', normed, up_weight[layer_index], precision=highest) + up_bias[layer_index])
    active = low(jax.nn.gelu(before, approximate=False))
    return hidden + jnp.einsum('nlf,fd->nld', active, down_weight[layer_index], precision=highest) + down_bias[layer_index]

def chain(rows, attend_weights, expand_weights):
    hidden = attend(rows, 0, attend_weights)
    hidden = expand(send_both(hidden), 0, expand_weights)
    hidden = attend(send_both(hidden), 1, attend_weights)
    return expand(send_both(hidden), 1, expand_weights)

def reference(global_rows, local_rows, patch_rank, ratio_bin, mask_token, attend_gain, attend_shift, triple_weight, pair_bias, output_weight, output_bias, expand_gain, expand_shift, up_weight, up_bias, down_weight, down_bias, grad_global, grad_local):
    floats = [tensor.astype(jnp.float32) for tensor in (global_rows, local_rows, mask_token, attend_gain, attend_shift, triple_weight, pair_bias, output_weight, output_bias, expand_gain, expand_shift, up_weight, up_bias, down_weight, down_bias)]

    def forward(global_in, local_in, token, *weights):
        attend_weights = weights[:6]
        expand_weights = weights[6:]

        def one_image(item):
            image_global, image_local, rank_rows, ratio = item
            limit = (ratio + 1) * PATCHES // 10
            masked = rank_rows < limit
            masked = jnp.concatenate([jnp.zeros((GLOBAL_CROPS, 1), jnp.bool_), masked], axis=1)
            start_global = jnp.where(masked[..., None], token[0], image_global)
            return (chain(start_global, attend_weights, expand_weights), chain(image_local, attend_weights, expand_weights))
        return lax.map(jax.checkpoint(one_image), (global_in, local_in, patch_rank, ratio_bin))
    outputs, pull_back = jax.vjp(forward, *floats)
    grads = pull_back((grad_global.astype(jnp.float32), grad_local.astype(jnp.float32)))
    return (outputs[0], outputs[1], grads[0], grads[1], grads[2], grads[3], grads[4], grads[5], grads[6], grads[7], grads[8], grads[9], grads[10], grads[11], grads[12], grads[13], grads[14])
```

```python
import math

import jax
import jax.numpy as jnp
from jax import lax
from jax.experimental import pallas as pl
from jax.experimental.pallas import tpu as pltpu
from jax.sharding import PartitionSpec as P

HEADS = 6
EPS = 1e-06
LANES = 128
VMEM_BYTES = 56 * 1024 * 1024
SMALL_ROWS = 128

f32 = jnp.float32
bf16 = jnp.bfloat16


def up_to(value, step):
    return (value + step - 1) // step * step


class Sizes:
    def __init__(self, global_rows, local_rows, up_weight, sections, replicas):
        images, crops, self.global_len, self.width = global_rows.shape
        _, local_crops, self.local_len, _ = local_rows.shape
        self.hidden = up_weight.shape[2]
        self.sections = sections
        self.replicas = replicas
        self.images = images
        self.all_globals = images * crops
        self.all_locals = images * local_crops
        self.locals = self.all_locals // sections
        self.used = self.global_len + self.locals * self.local_len
        self.rows = up_to(self.used, LANES)
        self.head = self.width // HEADS
        self.cut = self.width // sections
        self.hidden_cut = self.hidden // sections
        self.tiles = self.width // LANES
        self.first_end = up_to(self.global_len, 16)
        self.second_start = self.global_len // 16 * 16
        self.windows = (
            (0, self.first_end),
            (self.second_start, self.rows - self.second_start),
        )
        self.lse_at = (0, self.first_end)
        self.lse_rows = self.first_end + self.rows - self.second_start
        unit = 16 * replicas
        self.attend_full = 4 * self.tiles * self.cut
        self.expand_full = self.hidden // LANES * self.cut + self.tiles * self.hidden_cut
        self.attend_rows = up_to(self.attend_full + 48, unit)
        self.expand_rows = up_to(self.expand_full + 48, unit)
        self.extra = self.cut * self.rows // LANES


def dot(a, b):
    return jnp.dot(a, b, preferred_element_type=f32)


def dot_last(a, b):
    return lax.dot_general(a, b, (((1,), (1,)), ((), ())), preferred_element_type=f32)


def dot_first(a, b):
    return lax.dot_general(a, b, (((0,), (0,)), ((), ())), preferred_element_type=f32)


def normalize(hidden):
    average = jnp.mean(hidden, axis=-1, keepdims=True)
    centred = hidden - average
    inverse = lax.rsqrt(jnp.mean(centred * centred, axis=-1, keepdims=True) + EPS)
    return centred * inverse, inverse


def row_blocks(sz):
    return [slice(i, i + LANES) for i in range(0, sz.rows, LANES)]


def head_mask(sz, rows, which):
    lane = lax.broadcasted_iota(jnp.int32, (rows, 2 * sz.head), 1)
    return lane < sz.head if which == 0 else lane >= sz.head


def window_bias(sz, which):
    start, length = sz.windows[which]

    def group(row):
        if which == 0:
            return jnp.where(row < sz.global_len, 0, 1)
        kind = jnp.where(row + start < sz.global_len, 0, 1)
        for crop in range(1, sz.locals + 1):
            kind = kind + jnp.where(row + start >= sz.global_len + crop * sz.local_len, 1, 0)
        return kind

    left = group(lax.broadcasted_iota(jnp.int32, (length, length), 0))
    right = group(lax.broadcasted_iota(jnp.int32, (length, length), 1))
    return jnp.where(left == right, 0.0, -1e30).astype(f32)


def own_rows(sz, which):
    start, length = sz.windows[which]
    row = lax.broadcasted_iota(jnp.int32, (length, 1), 0) + start
    return row < sz.global_len if which == 0 else row >= sz.global_len


def store_window(sz, which, ref, columns, value):
    start, length = sz.windows[which]
    if which == 0 or sz.first_end == start:
        ref[start : start + length, columns] = value.astype(bf16)
        return
    shared = sz.first_end - start
    row = lax.broadcasted_iota(jnp.int32, (shared, value.shape[1]), 0) + start
    before = ref[start : sz.first_end, columns].astype(f32)
    ref[start : sz.first_end, columns] = jnp.where(
        row < sz.global_len, before, value[:shared]
    ).astype(bf16)
    ref[sz.first_end : start + length, columns] = value[shared:].astype(bf16)


def norm_rows(sz, h_ref, gain, shift, normed_ref):
    for rows in row_blocks(sz):
        scaled, _ = normalize(h_ref[rows, :].astype(f32))
        normed_ref[rows, :] = (scaled * gain + shift).astype(bf16)


def attend_forward(sz, h_ref, weights, out_ref, normed_ref, qkv_ref, lse_ref, ctx_ref, bias_refs):
    gain, shift, triple_ref, pair_bias, output_ref, output_bias = weights
    width = sz.width
    norm_rows(sz, h_ref, gain, shift, normed_ref)
    for part in range(3):
        columns = slice(part * width, (part + 1) * width)
        project = dot(normed_ref[...], triple_ref[:, columns])
        if part == 0:
            project = project + pair_bias[:, :width]
        if part == 2:
            project = project + pair_bias[:, width:]
        qkv_ref[:, columns] = project.astype(bf16)
    scale = 1.0 / math.sqrt(sz.head)
    for which, (start, length) in enumerate(sz.windows):
        rows = slice(start, start + length)
        bias = bias_refs[which]
        lane = lax.broadcasted_iota(jnp.int32, (length, LANES), 1)
        kept = jnp.zeros((length, LANES), f32)
        for pair in range(HEADS // 2):
            at = 2 * sz.head * pair
            queries = qkv_ref[rows, at : at + 2 * sz.head]
            keys = qkv_ref[rows, width + at : width + at + 2 * sz.head]
            values = qkv_ref[rows, 2 * width + at : 2 * width + at + 2 * sz.head]
            both = []
            for which_head in range(2):
                one = jnp.where(head_mask(sz, length, which_head), queries, jnp.zeros_like(queries))
                scores = dot_last(one, keys) * scale + bias[...]
                top = jnp.max(scores, axis=-1, keepdims=True)
                raised = jnp.exp(scores - top)
                total = jnp.sum(raised, axis=-1, keepdims=True)
                kept = jnp.where(lane == 2 * pair + which_head, top + jnp.log(total), kept)
                both.append(dot((raised * (1.0 / total)).astype(bf16), values))
            store_window(
                sz, which, ctx_ref, slice(at, at + 2 * sz.head),
                jnp.where(head_mask(sz, length, 0), both[0], both[1]),
            )
        lse_ref[sz.lse_at[which] : sz.lse_at[which] + length, :] = kept
    moved = dot(ctx_ref[...], output_ref[...]) + output_bias
    out_ref[...] = (h_ref[...].astype(f32) + moved).astype(bf16)


def expand_forward(sz, h_ref, weights, out_ref, normed_ref, active_ref, slope_ref, total_ref):
    gain, shift, up_ref, up_bias, down_ref, down_bias = weights
    norm_rows(sz, h_ref, gain, shift, normed_ref)
    total_ref[...] = h_ref[...].astype(f32) + down_bias
    for at in range(0, sz.hidden, sz.hidden_cut):
        columns = slice(at, at + sz.hidden_cut)
        before = dot(normed_ref[...], up_ref[:, columns]) + up_bias[:, columns]
        share = 0.5 + 0.5 * lax.erf(before * math.sqrt(0.5))
        active_ref[:, columns] = (before * share).astype(bf16)
        density = jnp.exp(before * before * -0.5) * (1.0 / math.sqrt(2.0 * math.pi))
        slope_ref[:, columns] = (share + before * density).astype(bf16)
        total_ref[...] += dot(active_ref[:, columns], down_ref[columns, :])
    out_ref[...] = total_ref[...].astype(bf16)


def turned_blocks(sz, value, me, turned_ref, blocks_ref):
    turned_ref[...] = value.T
    for j in range(sz.sections):
        source = pl.multiple_of((me ^ j) * sz.cut, sz.cut)
        blocks_ref[j * sz.cut : (j + 1) * sz.cut, :] = turned_ref[pl.ds(source, sz.cut), :]


def front_kernel(
    sz, ids_ref, limit_ref, global_ref, local_ref, rank_ref, token_ref, global_grad_ref, local_grad_ref,
    gain_a, shift_a, triple, pair, output, output_b, gain_e, shift_e, up, up_b, down, down_b,
    s0, s1, s2, s3, n0, n1, n2, n3, qkv0, qkv1, lse0, lse1, ctx0, ctx1, act0, act1, slope0, slope1, grad, masked_ref, out_turned,
    row_global, row_local, row_global_grad, row_local_grad, row_rank, wide, bias0, bias1,
    turned, blocks, last, sems,
):
    me = ids_ref[0]
    copies = [
        pltpu.make_async_copy(global_ref.at[me], row_global, sems.at[0]),
        pltpu.make_async_copy(local_ref.at[pl.ds(me * sz.locals, sz.locals)], row_local, sems.at[1]),
        pltpu.make_async_copy(global_grad_ref.at[me], row_global_grad, sems.at[2]),
        pltpu.make_async_copy(local_grad_ref.at[pl.ds(me * sz.locals, sz.locals)], row_local_grad, sems.at[3]),
        pltpu.make_async_copy(rank_ref.at[me], row_rank, sems.at[4]),
    ]
    for copy in copies:
        copy.start()
    bias0[...] = window_bias(sz, 0)
    bias1[...] = window_bias(sz, 1)
    for copy in copies:
        copy.wait()
    patches = sz.global_len - 1
    limit = limit_ref[me]
    ranks = row_rank[...]
    shape = (sz.global_len, patches)
    row = lax.broadcasted_iota(jnp.int32, shape, 0)
    column = lax.broadcasted_iota(jnp.int32, shape, 1)
    chosen = jnp.where((row == column + 1) & (ranks < limit), 1.0, 0.0)
    chosen = jnp.max(chosen, axis=-1, keepdims=True)
    masked_ref[...] = jnp.zeros_like(masked_ref)
    masked_ref[: sz.global_len, :] = jnp.broadcast_to(chosen, (sz.global_len, LANES))
    wide[...] = jnp.zeros_like(wide)
    wide[: sz.global_len, :] = jnp.where(chosen > 0.5, token_ref[...].astype(f32), row_global[...].astype(f32))
    for crop in range(sz.locals):
        at = sz.global_len + crop * sz.local_len
        wide[at : at + sz.local_len, :] = row_local[crop].astype(f32)
    s0[...] = wide[...].astype(bf16)
    wide[: sz.global_len, :] = row_global_grad[...].astype(f32)
    for crop in range(sz.locals):
        at = sz.global_len + crop * sz.local_len
        wide[at : at + sz.local_len, :] = row_local_grad[crop].astype(f32)
    grad[...] = wide[...].astype(bf16)

    def attend_weights(layer):
        one = slice(layer, layer + 1)
        return (
            gain_a[one, :].astype(f32), shift_a[one, :].astype(f32), triple.at[layer],
            pair[one, :].astype(f32), output.at[layer], output_b[one, :].astype(f32),
        )

    def expand_weights(layer):
        one = slice(layer, layer + 1)
        return (
            gain_e[one, :].astype(f32), shift_e[one, :].astype(f32), up.at[layer],
            up_b[one, :].astype(f32), down.at[layer], down_b[one, :].astype(f32),
        )

    attend_forward(sz, s0, attend_weights(0), s1, n0, qkv0, lse0, ctx0, (bias0, bias1))
    expand_forward(sz, s1, expand_weights(0), s2, n1, act0, slope0, wide)
    attend_forward(sz, s2, attend_weights(1), s3, n2, qkv1, lse1, ctx1, (bias0, bias1))
    expand_forward(sz, s3, expand_weights(1), last, n3, act1, slope1, wide)
    turned_blocks(sz, last[...], me, turned, blocks)
    for j in range(sz.sections):
        for tile in range(sz.rows // LANES):
            out_turned[j, tile * sz.cut : (tile + 1) * sz.cut, :] = blocks[
                j * sz.cut : (j + 1) * sz.cut, tile * LANES : (tile + 1) * LANES
            ]


def norm_backward(sz, h_ref, grad_ref, grad_normed_ref, gain, dh_ref):
    gain_sum = jnp.zeros((1, sz.width), f32)
    shift_sum = jnp.zeros((1, sz.width), f32)
    for rows in row_blocks(sz):
        scaled, inverse = normalize(h_ref[rows, :].astype(f32))
        grad_normed = grad_normed_ref[rows, :]
        grad_scaled = grad_normed * gain
        first = jnp.mean(grad_scaled, axis=-1, keepdims=True)
        second = jnp.mean(grad_scaled * scaled, axis=-1, keepdims=True)
        grad_in = inverse * (grad_scaled - first - scaled * second)
        dh_ref[rows, :] = grad_ref[rows, :].astype(f32) + grad_in
        gain_sum += jnp.sum(grad_normed * scaled, axis=0, keepdims=True)
        shift_sum += jnp.sum(grad_normed, axis=0, keepdims=True)
    return gain_sum, shift_sum


def put_vector(small, at, vector):
    for tile in range(vector.shape[1] // LANES):
        small[at + tile : at + tile + 1, :] = vector[:, tile * LANES : (tile + 1) * LANES]
    return at + vector.shape[1] // LANES


def put_tiles(pack, j, at, value):
    r = value.shape[0]
    for tile in range(value.shape[1] // LANES):
        pack[j, pl.ds(at + tile * r, r), :] = value[:, tile * LANES : (tile + 1) * LANES].astype(bf16)


def put_small(sz, pack, small, start, end):
    held = min(end - start, SMALL_ROWS)
    for j in range(sz.sections):
        pack[j, start : start + held, :] = small[:held, :].astype(bf16)
        if start + held < end:
            pack[j, start + held : end, :] = jnp.zeros((end - start - held, LANES), bf16)


def ship(sz, replica, pack, rows, keep, send, sems):
    bits = sz.replicas.bit_length() - 1
    shard = rows // sz.replicas
    copies = []
    for j in range(sz.sections):
        target = (keep, send)[j % 2]
        for place in range(sz.replicas):
            offset = sum(((place >> (bits - 1 - bit)) & 1) << bit for bit in range(bits))
            source = pl.multiple_of((replica ^ offset) * shard, 16)
            copies.append(
                pltpu.make_async_copy(
                    pack.at[j, pl.ds(source, shard), :],
                    target.at[j // 2, pl.ds(place * shard, shard), :],
                    sems.at[0],
                )
            )
    for copy in copies:
        copy.start()
    for copy in copies:
        copy.wait()


def expand_kernel(sz, layer, ids_ref, h_ref, normed, grad_ref, act_ref, slope_ref, gain_e, up, down, *rest):
    if layer == 1:
        extra_ref, dh_ref, keep, send, total, turned, blocks, pack, small, sems = rest
    else:
        dh_ref, keep, send, total, turned, blocks, pack, small, sems = rest
        extra_ref = None
    me = ids_ref[0]
    moves = []
    if extra_ref is not None:
        for j in range(sz.sections):
            target = (keep, send)[j % 2]
            moves.append(
                pltpu.make_async_copy(
                    extra_ref.at[j], target.at[j // 2, pl.ds(sz.expand_rows, sz.extra), :], sems.at[1]
                )
            )
    for move in moves:
        move.start()
    part = sz.hidden_cut
    up_rows = sz.hidden // LANES * sz.cut
    small[...] = jnp.zeros_like(small)
    turned_blocks(sz, normed[...], me, turned, blocks)
    after = 2 * sz.tiles
    for j in range(sz.sections):
        owner = me ^ j
        columns = pl.ds(pl.multiple_of(owner * part, LANES), part)
        active = act_ref[:, columns]
        put_tiles(pack, j, up_rows, dot_first(active, grad_ref[...]))
        grad_active = dot_last(grad_ref[...], down[layer, columns, :])
        grad_before = (grad_active * slope_ref[:, columns].astype(f32)).astype(bf16)
        up_sum = jnp.sum(grad_before.astype(f32), axis=0, keepdims=True)
        for tile in range(part // LANES):
            small[pl.ds(after + owner * (part // LANES) + tile, 1), :] = up_sum[:, tile * LANES : (tile + 1) * LANES]
        up_grad = dot(blocks[...], grad_before)
        at = pl.multiple_of(owner * (part // LANES * sz.cut), 16)
        for other in range(sz.sections):
            put_tiles(pack, other, at, up_grad[other * sz.cut : (other + 1) * sz.cut, :])
        more = dot_last(grad_before, up[layer, :, columns])
        if j == 0:
            total[...] = more
        else:
            total[...] += more
    gain = gain_e[layer : layer + 1, :].astype(f32)
    gain_sum, shift_sum = norm_backward(sz, h_ref, grad_ref, total, gain, total)
    dh_ref[...] = total[...].astype(bf16)
    put_vector(small, 0, gain_sum)
    put_vector(small, sz.tiles, shift_sum)
    put_vector(
        small, after + sz.hidden // LANES, jnp.sum(grad_ref[...].astype(f32), axis=0, keepdims=True)
    )
    put_small(sz, pack, small, sz.expand_full, sz.expand_rows)
    ship(sz, ids_ref[1], pack, sz.expand_rows, keep, send, sems)
    for move in moves:
        move.wait()


def attend_kernel(
    sz, layer, ids_ref, h_ref, normed, grad_ref, qkv_ref, lse_ref, ctx_ref, gain_a, triple, output, *rest
):
    if layer == 0:
        masked_ref, keep, send, total, turned, blocks, pack, small, proj, dctx, bias0, bias1, sems = rest
    else:
        dh_ref, keep, send, total, turned, blocks, pack, small, proj, dctx, bias0, bias1, sems = rest
    me = ids_ref[0]
    width = sz.width
    bias0[...] = window_bias(sz, 0)
    bias1[...] = window_bias(sz, 1)
    small[...] = jnp.zeros_like(small)
    grad = grad_ref[...]
    dctx[...] = dot_last(grad, output[layer]).astype(bf16)
    out_rows = 3 * sz.tiles * sz.cut
    turned_blocks(sz, ctx_ref[...], me, turned, blocks)
    output_grad = dot(blocks[...], grad)
    for j in range(sz.sections):
        put_tiles(pack, j, out_rows, output_grad[j * sz.cut : (j + 1) * sz.cut, :])
    scale = 1.0 / math.sqrt(sz.head)
    for which, (start, length) in enumerate(sz.windows):
        rows = slice(start, start + length)
        bias = (bias0, bias1)[which]
        own = own_rows(sz, which)
        lse_at = sz.lse_at[which]
        for pair in range(HEADS // 2):
            at = 2 * sz.head * pair
            columns = [slice(part * width + at, part * width + at + 2 * sz.head) for part in range(3)]
            queries, keys, values = (qkv_ref[rows, c] for c in columns)
            grad_ctx = jnp.where(own, dctx[rows, columns[0]], jnp.zeros((length, 2 * sz.head), bf16))
            results = []
            for which_head in range(2):
                mask = head_mask(sz, length, which_head)
                one = jnp.where(mask, queries, jnp.zeros_like(queries))
                scores = dot_last(one, keys) * scale + bias[...]
                head = 2 * pair + which_head
                prob = jnp.exp(scores - lse_ref[lse_at : lse_at + length, head : head + 1])
                grad_one = jnp.where(mask, grad_ctx, jnp.zeros_like(grad_ctx))
                grad_prob = dot_last(grad_one, values)
                delta = jnp.sum(prob * grad_prob, axis=-1, keepdims=True)
                grad_scores = (prob * (grad_prob - delta)).astype(bf16)
                results.append(
                    (
                        dot(grad_scores, keys) * scale,
                        dot_first(grad_scores, queries) * scale,
                        dot_first(prob.astype(bf16), grad_ctx),
                    )
                )
            first = head_mask(sz, length, 0)
            for part in range(3):
                store_window(sz, which, proj, columns[part], jnp.where(first, results[0][part], results[1][part]))
    turned_blocks(sz, normed[...], me, turned, blocks)
    after = 2 * sz.tiles
    for part in range(3):
        columns = slice(part * width, (part + 1) * width)
        grad_part = proj[:, columns]
        triple_grad = dot(blocks[...], grad_part)
        for j in range(sz.sections):
            put_tiles(pack, j, part * sz.tiles * sz.cut, triple_grad[j * sz.cut : (j + 1) * sz.cut, :])
        if part != 1:
            after = put_vector(small, after, jnp.sum(grad_part.astype(f32), axis=0, keepdims=True))
        more = dot_last(grad_part, triple[layer, :, columns])
        if part == 0:
            total[...] = more
        else:
            total[...] += more
    gain = gain_a[layer : layer + 1, :].astype(f32)
    gain_sum, shift_sum = norm_backward(sz, h_ref, grad_ref, total, gain, total)
    put_vector(small, 0, gain_sum)
    put_vector(small, sz.tiles, shift_sum)
    after = put_vector(small, after, jnp.sum(grad.astype(f32), axis=0, keepdims=True))
    if layer == 0:
        masked = masked_ref[:, :1] > 0.5
        put_vector(small, after, jnp.sum(jnp.where(masked, total[...], 0.0), axis=0, keepdims=True))
        turned_blocks(sz, jnp.where(masked, 0.0, total[...]).astype(bf16), me, turned, blocks)
        for j in range(sz.sections):
            for tile in range(sz.rows // LANES):
                at = sz.attend_rows + tile * sz.cut
                pack[j, at : at + sz.cut, :] = blocks[
                    j * sz.cut : (j + 1) * sz.cut, tile * LANES : (tile + 1) * LANES
                ]
    else:
        dh_ref[...] = total[...].astype(bf16)
    put_small(sz, pack, small, sz.attend_full, sz.attend_rows)
    moves = []
    if layer == 0:
        for j in range(sz.sections):
            target = (keep, send)[j % 2]
            tail = pl.ds(sz.attend_rows, sz.extra)
            moves.append(pltpu.make_async_copy(pack.at[j, tail, :], target.at[j // 2, tail, :], sems.at[1]))
    for move in moves:
        move.start()
    ship(sz, ids_ref[1], pack, sz.attend_rows, keep, send, sems)
    for move in moves:
        move.wait()


def finish_kernel(sz, ids_ref, *refs):
    parts, (own_out, core_out, x_out, own_in, core_in, x_in) = refs[:4], refs[4:10]
    (
        out_global, out_local, in_global, in_local, token, gain_a, shift_a, triple, pair, output, output_b,
        gain_e, shift_e, up, up_b, down, down_b,
    ) = refs[10:27]
    scratch = refs[27:31]
    row_scratch, vectors, wide, sems = refs[31:]
    me, replica = ids_ref[0], ids_ref[1]
    bits = sz.replicas.bit_length() - 1
    moves = []
    for source, target in zip(parts, scratch):
        shard = target.shape[0] // sz.replicas
        for place in range(sz.replicas):
            offset = sum(((place >> (bits - 1 - bit)) & 1) << bit for bit in range(bits))
            at = pl.multiple_of((replica ^ offset) * shard, 16)
            moves.append(
                pltpu.make_async_copy(
                    source.at[pl.ds(place * shard, shard), :], target.at[pl.ds(at, shard), :], sems.at[0]
                )
            )
    count = len(moves)
    for which, refs_in in enumerate(((own_out, core_out, x_out), (own_in, core_in, x_in))):
        base = (sz.expand_rows, sz.attend_rows)[which]
        for k in range(4):
            if k < 2:
                source = refs_in[k].at[0, pl.ds(base, sz.extra), :]
            else:
                source = refs_in[2].at[pl.ds(base + (k - 2) * sz.extra, sz.extra), :]
            moves.append(pltpu.make_async_copy(source, row_scratch.at[which, k], sems.at[1]))
    for move in moves:
        move.start()
    for move in moves[count:]:
        move.wait()
    for which, (to_global, to_local) in enumerate(((out_global, out_local), (in_global, in_local))):
        for k in range(4):
            section = me ^ k
            turned = jnp.concatenate(
                [
                    row_scratch[which, k, tile * sz.cut : (tile + 1) * sz.cut, :].astype(f32)
                    for tile in range(sz.rows // LANES)
                ],
                axis=1,
            )
            turned = jnp.concatenate([turned, jnp.zeros((LANES - sz.cut, sz.rows), f32)], axis=0)
            wide[...] = turned.T
            to_global[section] = wide[: sz.global_len, : sz.cut]
            for crop in range(sz.locals):
                at = sz.global_len + crop * sz.local_len
                to_local[section * sz.locals + crop] = wide[at : at + sz.local_len, : sz.cut]
    for move in moves[:count]:
        move.wait()
    width = sz.width
    row = lax.broadcasted_iota(jnp.int32, (width, sz.cut), 0)
    column = lax.broadcasted_iota(jnp.int32, (width, sz.cut), 1)
    pick = jnp.where(row == column + me * sz.cut, 1.0, 0.0).astype(bf16)
    row = lax.broadcasted_iota(jnp.int32, (2 * width, 2 * sz.cut), 0)
    column = lax.broadcasted_iota(jnp.int32, (2 * width, 2 * sz.cut), 1)
    pick_pair = jnp.where(row == column + me * 2 * sz.cut, 1.0, 0.0).astype(bf16)
    for layer in range(2):
        one = slice(layer, layer + 1)
        attend, expand = scratch[2 * layer], scratch[2 * layer + 1]
        tiles, cut = sz.tiles, sz.cut

        def tile_row(source, base, tile):
            return source[base + tile * cut : base + (tile + 1) * cut, :].astype(f32)

        for tile in range(3 * tiles):
            triple[layer, :, tile * LANES : (tile + 1) * LANES] = tile_row(attend, 0, tile)
        for tile in range(tiles):
            output[layer, :, tile * LANES : (tile + 1) * LANES] = tile_row(attend, 3 * tiles * cut, tile)
        hidden_tiles = sz.hidden // LANES
        for tile in range(hidden_tiles):
            up[layer, :, tile * LANES : (tile + 1) * LANES] = tile_row(expand, 0, tile)
        for tile in range(tiles):
            base = hidden_tiles * cut + tile * sz.hidden_cut
            down[layer, :, tile * LANES : (tile + 1) * LANES] = expand[base : base + sz.hidden_cut, :].astype(f32)
        vectors[...] = attend[sz.attend_full : sz.attend_full + 48, :].astype(f32)

        def vector(at, tiles_in):
            return jnp.concatenate([vectors[at + t : at + t + 1, :] for t in range(tiles_in)], axis=1)

        def picked(at):
            return dot(vector(at, tiles).astype(bf16), pick)

        gain_a[one, :] = picked(0)
        shift_a[one, :] = picked(tiles)
        pair[one, :] = dot(vector(2 * tiles, 2 * tiles).astype(bf16), pick_pair)
        output_b[one, :] = picked(4 * tiles)
        if layer == 0:
            token[...] = picked(5 * tiles)
        vectors[...] = expand[sz.expand_full : sz.expand_full + 48, :].astype(f32)
        gain_e[one, :] = picked(0)
        shift_e[one, :] = picked(tiles)
        up_tiles = sz.hidden_cut // LANES
        for tile in range(up_tiles):
            up_b[one, tile * LANES : (tile + 1) * LANES] = vectors[pl.ds(2 * tiles + me * up_tiles + tile, 1), :]
        down_b[one, :] = picked(2 * tiles + hidden_tiles)


VMEM = pl.BlockSpec(memory_space=pltpu.VMEM)
ANY = pl.BlockSpec(memory_space=pl.ANY)
SMEM = pl.BlockSpec(memory_space=pltpu.SMEM)


def call(body, name, out_shapes, out_specs, in_specs, scratch, args, flops):
    return pl.pallas_call(
        body,
        name=name,
        out_shape=tuple(jax.ShapeDtypeStruct(shape, kind) for shape, kind in out_shapes),
        in_specs=in_specs,
        out_specs=tuple(out_specs),
        scratch_shapes=scratch,
        compiler_params=pltpu.CompilerParams(vmem_limit_bytes=VMEM_BYTES),
        cost_estimate=pl.CostEstimate(flops=flops, bytes_accessed=4 << 20, transcendentals=0),
    )(*args)


def partner(axis, bit):
    return [(i, i ^ bit) for i in range(lax.axis_size(axis))]


def swap(value, axis, bit):
    return lax.ppermute(value, axis, partner(axis, bit))


def add(a, b):
    return (a.astype(f32) + b.astype(f32)).astype(bf16)


def section_reduce(keep, send, rows, extra):
    core = swap(send, "section", 1)
    out = add(keep[1, :rows], core[1, :rows])
    if extra:
        out = jnp.concatenate([out, keep[1, rows:], core[1, rows:]], axis=0)
    across = swap(out, "section", 2)
    mine = (keep[0, :rows].astype(f32) + core[0, :rows].astype(f32) + across[:rows].astype(f32)).astype(bf16)
    return mine, core, across


def replica_reduce(mine):
    replicas = lax.axis_size("dp")
    bits = replicas.bit_length() - 1
    for bit in range(bits):
        half = mine.shape[0] // 2
        mine = add(mine[:half], swap(mine[half:], "dp", 1 << bit))
    for bit in reversed(range(bits)):
        mine = jnp.concatenate([mine, swap(mine, "dp", 1 << bit)], axis=0)
    return mine


def per_device(
    global_rows, local_rows, patch_rank, ratio_bin, mask_token, attend_gain, attend_shift, triple_weight,
    pair_bias, output_weight, output_bias, expand_gain, expand_shift, up_weight, up_bias, down_weight,
    down_bias, grad_global, grad_local,
):
    sections, replicas = lax.axis_size("section"), lax.axis_size("dp")
    sz = Sizes(global_rows, local_rows, up_weight, sections, replicas)
    width, rows = sz.width, sz.rows
    ids = jnp.stack([lax.axis_index("section"), lax.axis_index("dp")]).astype(jnp.int32)
    patches = patch_rank.shape[-1]
    limit = jnp.repeat((ratio_bin + 1) * patches // 10, patch_rank.shape[1])
    global_in = global_rows.reshape((sz.all_globals,) + global_rows.shape[2:])
    local_in = local_rows.reshape((sz.all_locals,) + local_rows.shape[2:])
    rank_in = patch_rank.reshape(sz.all_globals, 1, patches)
    global_back = grad_global.reshape(global_in.shape)
    local_back = grad_local.reshape(local_in.shape)
    hidden = sz.hidden
    wide = (rows, width)
    lse = ((sz.lse_rows, LANES), f32)
    window_scratch = [pltpu.VMEM((length, length), f32) for _, length in sz.windows]
    turned_scratch = [pltpu.VMEM((width, rows), bf16), pltpu.VMEM((width, rows), bf16)]
    front = call(
        lambda *refs: front_kernel(sz, *refs),
        "front",
        [(wide, bf16)] * 8
        + [((rows, 3 * width), bf16)] * 2
        + [lse] * 2
        + [(wide, bf16)] * 2
        + [((rows, hidden), bf16)] * 4
        + [(wide, bf16), ((rows, LANES), f32), ((sections, sz.extra, LANES), bf16)],
        [VMEM] * 21,
        [SMEM, SMEM, ANY, ANY, ANY, VMEM, ANY, ANY] + [VMEM] * 12,
        [
            pltpu.VMEM(global_in.shape[1:], bf16),
            pltpu.VMEM((sz.locals,) + local_in.shape[1:], bf16),
            pltpu.VMEM(global_in.shape[1:], bf16),
            pltpu.VMEM((sz.locals,) + local_in.shape[1:], bf16),
            pltpu.VMEM((1, patches), jnp.int32),
            pltpu.VMEM(wide, f32),
        ]
        + window_scratch
        + turned_scratch
        + [pltpu.VMEM(wide, bf16), pltpu.SemaphoreType.DMA((5,))],
        (
            ids, limit, global_in, local_in, rank_in, mask_token, global_back, local_back, attend_gain,
            attend_shift, triple_weight, pair_bias, output_weight, output_bias, expand_gain, expand_shift,
            up_weight, up_bias, down_weight, down_bias,
        ),
        4 << 30,
    )
    states, normed = front[:4], front[4:8]
    qkv, lses, contexts = front[8:10], front[10:12], front[12:14]
    actives, slopes = front[14:16], front[16:18]
    grad, masked, out_turned = front[18:]
    reduced = {}
    moved = {}
    for layer in (1, 0):
        total_rows = sz.expand_rows + (sz.extra if layer == 1 else 0)
        grad, keep, send = call(
            lambda *refs, layer=layer: expand_kernel(sz, layer, *refs),
            f"expand_back_{layer}",
            [(wide, bf16)] + [((2, total_rows, LANES), bf16)] * 2,
            [VMEM, ANY, ANY],
            [SMEM] + [VMEM] * 8 + ([ANY] if layer == 1 else []),
            [pltpu.VMEM(wide, f32)]
            + turned_scratch
            + [
                pltpu.VMEM((sections, sz.expand_rows, LANES), bf16),
                pltpu.VMEM((SMALL_ROWS, LANES), f32),
                pltpu.SemaphoreType.DMA((2,)),
            ],
            (ids, states[2 * layer + 1], normed[2 * layer + 1], grad, actives[layer], slopes[layer], expand_gain,
             up_weight, down_weight) + ((out_turned,) if layer == 1 else ()),
            3 << 30,
        )
        mine, core, across = section_reduce(keep, send, sz.expand_rows, layer == 1)
        reduced["expand", layer] = replica_reduce(mine)
        if layer == 1:
            moved["out"] = (keep, core, across)
        total_rows = sz.attend_rows + (sz.extra if layer == 0 else 0)
        results = call(
            lambda *refs, layer=layer: attend_kernel(sz, layer, *refs),
            f"attend_back_{layer}",
            ([(wide, bf16)] if layer == 1 else []) + [((2, total_rows, LANES), bf16)] * 2,
            ([VMEM] if layer == 1 else []) + [ANY, ANY],
            [SMEM] + [VMEM] * (9 + (layer == 0)),
            [pltpu.VMEM(wide, f32)]
            + turned_scratch
            + [
                pltpu.VMEM((sections, total_rows, LANES), bf16),
                pltpu.VMEM((SMALL_ROWS, LANES), f32),
                pltpu.VMEM((rows, 3 * width), bf16),
                pltpu.VMEM(wide, bf16),
            ]
            + window_scratch
            + [pltpu.SemaphoreType.DMA((2,))],
            (ids, states[2 * layer], normed[2 * layer], grad, qkv[layer], lses[layer], contexts[layer], attend_gain,
             triple_weight, output_weight) + ((masked,) if layer == 0 else ()),
            2 << 30,
        )
        if layer == 1:
            grad, keep, send = results
        else:
            keep, send = results
        mine, core, across = section_reduce(keep, send, sz.attend_rows, layer == 0)
        reduced["attend", layer] = replica_reduce(mine)
        if layer == 0:
            moved["in"] = (keep, core, across)
    cut = sz.cut
    outs = [
        ((sz.all_globals, sz.global_len, cut), f32),
        ((sz.all_locals, sz.local_len, cut), f32),
    ] * 2 + [
        ((1, cut), f32),
        ((2, cut), f32),
        ((2, cut), f32),
        ((2, cut, 3 * width), f32),
        ((2, 2 * cut), f32),
        ((2, cut, width), f32),
        ((2, cut), f32),
        ((2, cut), f32),
        ((2, cut), f32),
        ((2, cut, hidden), f32),
        ((2, sz.hidden_cut), f32),
        ((2, sz.hidden_cut, width), f32),
        ((2, cut), f32),
    ]
    final = call(
        lambda *refs: finish_kernel(sz, *refs),
        "finish",
        outs,
        [VMEM] * 17,
        [SMEM] + [ANY] * 10,
        [
            pltpu.VMEM((sz.attend_rows, LANES), bf16),
            pltpu.VMEM((sz.expand_rows, LANES), bf16),
            pltpu.VMEM((sz.attend_rows, LANES), bf16),
            pltpu.VMEM((sz.expand_rows, LANES), bf16),
            pltpu.VMEM((2, 4, sz.extra, LANES), bf16),
            pltpu.VMEM((48, LANES), f32),
            pltpu.VMEM((rows, LANES), f32),
            pltpu.SemaphoreType.DMA((2,)),
        ],
        (
            ids, reduced["attend", 0], reduced["expand", 0], reduced["attend", 1], reduced["expand", 1],
            *moved["out"], *moved["in"],
        ),
        1 << 28,
    )
    return (
        final[0].reshape(global_rows.shape[:3] + (cut,)),
        final[1].reshape(local_rows.shape[:3] + (cut,)),
        final[2].reshape(global_rows.shape[:3] + (cut,)),
        final[3].reshape(local_rows.shape[:3] + (cut,)),
        *final[4:],
    )


def solution(mesh):
    rows, copied = P("dp", None, None, None), P()
    in_specs = (rows, rows, P("dp", None, None), P("dp")) + (copied,) * 13 + (rows, rows)
    wide, flat, deep = P("dp", None, None, "section"), P(None, "section"), P(None, "section", None)
    out_specs = (
        wide, wide, wide, wide, flat, flat, flat, deep, flat, deep, flat, flat, flat, deep, flat, deep, flat,
    )
    return jax.shard_map(per_device, mesh=mesh, in_specs=in_specs, out_specs=out_specs, check_vma=False)
```

```python
import math

import jax
import jax.numpy as jnp
from jax import lax
from jax.experimental import pallas as pl
from jax.experimental.pallas import tpu as pltpu
from jax.sharding import PartitionSpec as P

HEADS = 6
EPS = 1e-06
LANES = 128
VMEM_BYTES = 56 * 1024 * 1024
X_AXIS = -1

f32 = jnp.float32
bf16 = jnp.bfloat16


def up_to(value, step):
    return (value + step - 1) // step * step


class Sizes:
    def __init__(self, global_rows, local_rows, up_weight, sections, replicas):
        images, crops, self.global_len, self.width = global_rows.shape
        _, local_crops, self.local_len, _ = local_rows.shape
        self.hidden = up_weight.shape[2]
        self.sections = sections
        self.replicas = replicas
        self.images = images
        self.all_globals = images * crops
        self.all_locals = images * local_crops
        self.locals = self.all_locals // sections
        self.used = self.global_len + self.locals * self.local_len
        self.rows = up_to(self.used, LANES)
        self.head = self.width // HEADS
        self.cut = self.width // sections
        self.hidden_cut = self.hidden // sections
        self.tiles = self.width // LANES
        self.first_end = up_to(self.global_len, 16)
        self.second_start = self.global_len // 16 * 16
        self.windows = (
            (0, self.first_end),
            (self.second_start, self.rows - self.second_start),
        )
        self.lse_at = (0, self.first_end)
        self.lse_rows = self.first_end + self.rows - self.second_start
        self.attend_full = 4 * self.tiles * self.cut
        self.expand_full = self.hidden // LANES * self.cut + self.tiles * self.hidden_cut
        self.expand_small = 8 * self.tiles
        self.small_rows = up_to(self.expand_small + 3 * self.tiles + self.hidden // LANES, 16)
        self.extra = self.cut * self.rows // LANES
        bits = replicas.bit_length() - 1
        low = list(range(min(bits, 2)))
        self.orders = ([X_AXIS] + low, low[1:] + [X_AXIS] + low[:1])
        self.rest = list(range(len(low), bits))
        self.shards = 1 << len(low)
        self.unit = 16 * self.shards

    def packed(self, full):
        return up_to(full + self.small_rows, self.unit)

    def offset(self, core, place, with_x):
        order = [axis for axis in self.orders[core] if with_x or axis != X_AXIS]
        across, replica = 0, 0
        for at, axis in enumerate(order):
            bit = place >> (len(order) - 1 - at) & 1
            if axis == X_AXIS:
                across = bit
            else:
                replica |= bit << axis
        return across, replica


def dot(a, b):
    return jnp.dot(a, b, preferred_element_type=f32)


def dot_last(a, b):
    return lax.dot_general(a, b, (((1,), (1,)), ((), ())), preferred_element_type=f32)


def dot_first(a, b):
    return lax.dot_general(a, b, (((0,), (0,)), ((), ())), preferred_element_type=f32)


def normalize(hidden):
    average = jnp.mean(hidden, axis=-1, keepdims=True)
    centred = hidden - average
    inverse = lax.rsqrt(jnp.mean(centred * centred, axis=-1, keepdims=True) + EPS)
    return centred * inverse, inverse


def row_blocks(sz):
    return [slice(i, i + LANES) for i in range(0, sz.rows, LANES)]


def head_mask(sz, rows, which):
    lane = lax.broadcasted_iota(jnp.int32, (rows, 2 * sz.head), 1)
    return lane < sz.head if which == 0 else lane >= sz.head


def window_bias(sz, which):
    start, length = sz.windows[which]

    def group(row):
        if which == 0:
            return jnp.where(row < sz.global_len, 0, 1)
        kind = jnp.where(row + start < sz.global_len, 0, 1)
        for crop in range(1, sz.locals + 1):
            kind = kind + jnp.where(row + start >= sz.global_len + crop * sz.local_len, 1, 0)
        return kind

    left = group(lax.broadcasted_iota(jnp.int32, (length, length), 0))
    right = group(lax.broadcasted_iota(jnp.int32, (length, length), 1))
    return jnp.where(left == right, 0.0, -1e30).astype(f32)


def own_rows(sz, which):
    start, length = sz.windows[which]
    row = lax.broadcasted_iota(jnp.int32, (length, 1), 0) + start
    return row < sz.global_len if which == 0 else row >= sz.global_len


def store_window(sz, which, ref, columns, value):
    start, length = sz.windows[which]
    if which == 0 or sz.first_end == start:
        ref[start : start + length, columns] = value.astype(bf16)
        return
    shared = sz.first_end - start
    row = lax.broadcasted_iota(jnp.int32, (shared, value.shape[1]), 0) + start
    before = ref[start : sz.first_end, columns].astype(f32)
    ref[start : sz.first_end, columns] = jnp.where(
        row < sz.global_len, before, value[:shared]
    ).astype(bf16)
    ref[sz.first_end : start + length, columns] = value[shared:].astype(bf16)


def norm_rows(sz, h_ref, gain, shift, normed_ref):
    for rows in row_blocks(sz):
        scaled, _ = normalize(h_ref[rows, :].astype(f32))
        normed_ref[rows, :] = (scaled * gain + shift).astype(bf16)


def attend_forward(sz, h_ref, weights, out_ref, normed_ref, qkv_ref, lse_ref, ctx_ref, bias_refs):
    gain, shift, triple_ref, pair_bias, output_ref, output_bias = weights
    width = sz.width
    norm_rows(sz, h_ref, gain, shift, normed_ref)
    for part in range(3):
        columns = slice(part * width, (part + 1) * width)
        project = dot(normed_ref[...], triple_ref[:, columns])
        if part == 0:
            project = project + pair_bias[:, :width]
        if part == 2:
            project = project + pair_bias[:, width:]
        qkv_ref[:, columns] = project.astype(bf16)
    scale = 1.0 / math.sqrt(sz.head)
    for which, (start, length) in enumerate(sz.windows):
        rows = slice(start, start + length)
        bias = bias_refs[which]
        lane = lax.broadcasted_iota(jnp.int32, (length, LANES), 1)
        kept = jnp.zeros((length, LANES), f32)
        for pair in range(HEADS // 2):
            at = 2 * sz.head * pair
            queries = qkv_ref[rows, at : at + 2 * sz.head]
            keys = qkv_ref[rows, width + at : width + at + 2 * sz.head]
            values = qkv_ref[rows, 2 * width + at : 2 * width + at + 2 * sz.head]
            both = []
            for which_head in range(2):
                one = jnp.where(head_mask(sz, length, which_head), queries, jnp.zeros_like(queries))
                scores = dot_last(one, keys) * scale + bias[...]
                top = jnp.max(scores, axis=-1, keepdims=True)
                raised = jnp.exp(scores - top)
                total = jnp.sum(raised, axis=-1, keepdims=True)
                kept = jnp.where(lane == 2 * pair + which_head, top + jnp.log(total), kept)
                both.append(dot((raised * (1.0 / total)).astype(bf16), values))
            store_window(
                sz, which, ctx_ref, slice(at, at + 2 * sz.head),
                jnp.where(head_mask(sz, length, 0), both[0], both[1]),
            )
        lse_ref[sz.lse_at[which] : sz.lse_at[which] + length, :] = kept
    moved = dot(ctx_ref[...], output_ref[...]) + output_bias
    out_ref[...] = (h_ref[...].astype(f32) + moved).astype(bf16)


def expand_forward(sz, h_ref, weights, out_ref, normed_ref, active_ref, slope_ref, total_ref):
    gain, shift, up_ref, up_bias, down_ref, down_bias = weights
    norm_rows(sz, h_ref, gain, shift, normed_ref)
    total_ref[...] = h_ref[...].astype(f32) + down_bias
    for at in range(0, sz.hidden, sz.hidden_cut):
        columns = slice(at, at + sz.hidden_cut)
        before = dot(normed_ref[...], up_ref[:, columns]) + up_bias[:, columns]
        share = 0.5 + 0.5 * lax.erf(before * math.sqrt(0.5))
        active_ref[:, columns] = (before * share).astype(bf16)
        density = jnp.exp(before * before * -0.5) * (1.0 / math.sqrt(2.0 * math.pi))
        slope_ref[:, columns] = (share + before * density).astype(bf16)
        total_ref[...] += dot(active_ref[:, columns], down_ref[columns, :])
    out_ref[...] = total_ref[...].astype(bf16)


def turned_blocks(sz, value, me, turned_ref, blocks_ref):
    turned_ref[...] = value.T
    for j in range(sz.sections):
        source = pl.multiple_of((me ^ j) * sz.cut, sz.cut)
        blocks_ref[j * sz.cut : (j + 1) * sz.cut, :] = turned_ref[pl.ds(source, sz.cut), :]


def put_vector(small, at, vector):
    for tile in range(vector.shape[1] // LANES):
        small[at + tile : at + tile + 1, :] = vector[:, tile * LANES : (tile + 1) * LANES]
    return at + vector.shape[1] // LANES


def put_tiles(pack, j, at, value):
    r = value.shape[0]
    for tile in range(value.shape[1] // LANES):
        pack[j, pl.ds(at + tile * r, r), :] = value[:, tile * LANES : (tile + 1) * LANES].astype(bf16)


def norm_backward(sz, h_ref, grad_ref, grad_normed_ref, gain, dh_ref):
    gain_sum = jnp.zeros((1, sz.width), f32)
    shift_sum = jnp.zeros((1, sz.width), f32)
    for rows in row_blocks(sz):
        scaled, inverse = normalize(h_ref[rows, :].astype(f32))
        grad_normed = grad_normed_ref[rows, :]
        grad_scaled = grad_normed * gain
        first = jnp.mean(grad_scaled, axis=-1, keepdims=True)
        second = jnp.mean(grad_scaled * scaled, axis=-1, keepdims=True)
        grad_in = inverse * (grad_scaled - first - scaled * second)
        dh_ref[rows, :] = (grad_ref[rows, :].astype(f32) + grad_in).astype(dh_ref.dtype)
        gain_sum += jnp.sum(grad_normed * scaled, axis=0, keepdims=True)
        shift_sum += jnp.sum(grad_normed, axis=0, keepdims=True)
    return gain_sum, shift_sum


def expand_backward(sz, me, h_ref, normed, grad_ref, act_ref, slope_ref, gain, up, down, dh_ref, scratch, pack, base, small):
    total, turned, blocks = scratch
    part = sz.hidden_cut
    up_rows = sz.hidden // LANES * sz.cut
    turned_blocks(sz, normed[...], me, turned, blocks)
    start = sz.expand_small
    after = start + 2 * sz.tiles
    for j in range(sz.sections):
        owner = me ^ j
        columns = pl.ds(pl.multiple_of(owner * part, LANES), part)
        put_tiles(pack, j, base + up_rows, dot_first(act_ref[:, columns], grad_ref[...]))
        grad_active = dot_last(grad_ref[...], down[columns, :])
        grad_before = (grad_active * slope_ref[:, columns].astype(f32)).astype(bf16)
        up_sum = jnp.sum(grad_before.astype(f32), axis=0, keepdims=True)
        for tile in range(part // LANES):
            small[pl.ds(after + owner * (part // LANES) + tile, 1), :] = up_sum[:, tile * LANES : (tile + 1) * LANES]
        up_grad = dot(blocks[...], grad_before)
        at = base + pl.multiple_of(owner * (part // LANES * sz.cut), 16)
        for other in range(sz.sections):
            put_tiles(pack, other, at, up_grad[other * sz.cut : (other + 1) * sz.cut, :])
        more = dot_last(grad_before, up[:, columns])
        if j == 0:
            total[...] = more
        else:
            total[...] += more
    gain_sum, shift_sum = norm_backward(sz, h_ref, grad_ref, total, gain, dh_ref)
    put_vector(small, start, gain_sum)
    put_vector(small, start + sz.tiles, shift_sum)
    put_vector(
        small, after + sz.hidden // LANES, jnp.sum(grad_ref[...].astype(f32), axis=0, keepdims=True)
    )


def attend_backward(
    sz, me, h_ref, normed, grad_ref, qkv_ref, lse_ref, ctx_ref, gain, triple, output, dh_ref, scratch, pack, base, small,
    proj, dctx, bias_refs,
):
    total, turned, blocks = scratch
    width = sz.width
    grad = grad_ref[...]
    dctx[...] = dot_last(grad, output[...]).astype(bf16)
    out_rows = base + 3 * sz.tiles * sz.cut
    turned_blocks(sz, ctx_ref[...], me, turned, blocks)
    output_grad = dot(blocks[...], grad)
    for j in range(sz.sections):
        put_tiles(pack, j, out_rows, output_grad[j * sz.cut : (j + 1) * sz.cut, :])
    scale = 1.0 / math.sqrt(sz.head)
    for which, (start, length) in enumerate(sz.windows):
        rows = slice(start, start + length)
        bias = bias_refs[which]
        own = own_rows(sz, which)
        lse_at = sz.lse_at[which]
        for pair in range(HEADS // 2):
            at = 2 * sz.head * pair
            columns = [slice(part * width + at, part * width + at + 2 * sz.head) for part in range(3)]
            queries, keys, values = (qkv_ref[rows, c] for c in columns)
            grad_ctx = jnp.where(own, dctx[rows, columns[0]], jnp.zeros((length, 2 * sz.head), bf16))
            results = []
            for which_head in range(2):
                mask = head_mask(sz, length, which_head)
                one = jnp.where(mask, queries, jnp.zeros_like(queries))
                scores = dot_last(one, keys) * scale + bias[...]
                head = 2 * pair + which_head
                prob = jnp.exp(scores - lse_ref[lse_at : lse_at + length, head : head + 1])
                grad_one = jnp.where(mask, grad_ctx, jnp.zeros_like(grad_ctx))
                grad_prob = dot_last(grad_one, values)
                delta = jnp.sum(prob * grad_prob, axis=-1, keepdims=True)
                grad_scores = (prob * (grad_prob - delta)).astype(bf16)
                results.append(
                    (
                        dot(grad_scores, keys) * scale,
                        dot_first(grad_scores, queries) * scale,
                        dot_first(prob.astype(bf16), grad_ctx),
                    )
                )
            first = head_mask(sz, length, 0)
            for part in range(3):
                store_window(sz, which, proj, columns[part], jnp.where(first, results[0][part], results[1][part]))
    turned_blocks(sz, normed[...], me, turned, blocks)
    after = 2 * sz.tiles
    for part in range(3):
        columns = slice(part * width, (part + 1) * width)
        grad_part = proj[:, columns]
        triple_grad = dot(blocks[...], grad_part)
        for j in range(sz.sections):
            put_tiles(pack, j, base + part * sz.tiles * sz.cut, triple_grad[j * sz.cut : (j + 1) * sz.cut, :])
        if part != 1:
            after = put_vector(small, after, jnp.sum(grad_part.astype(f32), axis=0, keepdims=True))
        more = dot_last(grad_part, triple[:, columns])
        if part == 0:
            total[...] = more
        else:
            total[...] += more
    gain_sum, shift_sum = norm_backward(sz, h_ref, grad_ref, total, gain, dh_ref)
    put_vector(small, 0, gain_sum)
    put_vector(small, sz.tiles, shift_sum)
    return put_vector(small, after, jnp.sum(grad.astype(f32), axis=0, keepdims=True))


def put_rows(sz, value, me, turned, blocks, stage, keep, send, sem):
    turned_blocks(sz, value, me, turned, blocks)
    moves = []
    for j in range(sz.sections):
        for tile in range(sz.rows // LANES):
            stage[j, tile * sz.cut : (tile + 1) * sz.cut, :] = blocks[
                j * sz.cut : (j + 1) * sz.cut, tile * LANES : (tile + 1) * LANES
            ]
        moves.append(pltpu.make_async_copy(stage.at[j], (keep, send)[j % 2].at[j // 2], sem))
    return moves


def ship(sz, me, replica, pack, rows, keep, send, sem):
    shard = rows // sz.shards
    moves = []
    for core in range(2):
        target = me & 1 ^ core
        for place in range(2 * sz.shards):
            options = [sz.offset(c, place, True) for c in range(2)]
            across = jnp.where(target == 0, options[0][0], options[1][0])
            offset = jnp.where(target == 0, options[0][1], options[1][1])
            source = pl.multiple_of((replica & sz.shards - 1 ^ offset) * shard, 16)
            moves.append(
                pltpu.make_async_copy(
                    pack.at[2 * across + core, pl.ds(source, shard), :],
                    (keep, send)[core].at[pl.ds(place * shard, shard), :],
                    sem,
                )
            )
    return moves


def put_small(pack, start, rows, small):
    held = small.shape[0]
    for j in range(pack.shape[0]):
        pack[j, start : start + held, :] = small[...].astype(bf16)
        if start + held < rows:
            pack[j, start + held : rows, :] = jnp.zeros((rows - start - held, LANES), bf16)


class Loads:
    def __init__(self, pairs, sems):
        self.moves = [pltpu.make_async_copy(source, target, sems.at[i]) for i, (source, target) in enumerate(pairs)]
        for move in self.moves:
            move.start()

    def wait(self, *which):
        for i in which:
            self.moves[i].wait()


def row_of(ref, layer):
    return ref[layer : layer + 1, :].astype(f32)


def pick_row(block, which):
    value = block[:, 0, :].astype(f32)
    for other in range(1, block.shape[1]):
        value = jnp.where(which == other, block[:, other, :].astype(f32), value)
    return value


def gather_rows(sz, of_global, of_local, crop, image, wide):
    wide[: sz.global_len, :] = pick_row(of_global, crop)
    for at in range(sz.locals):
        start = sz.global_len + at * sz.local_len
        wide[start : start + sz.local_len, :] = pick_row(of_local.at[at], image)
    wide[sz.used :, :] = jnp.zeros((sz.rows - sz.used, sz.width), f32)


def front_kernel(
    sz, global_in, local_in, global_back, local_back, rank_ref, ratio_ref, token_ref, gain_a, shift_a, triple_in, pair, output_in, output_b,
    gain_e, shift_e, up_in, up_b, down_in, down_b,
    s0_out, s1_out, n0_out, n1_out, qkv0_out, lse0_out, ctx0_out, act0_out, slope0_out, masked_ref, dh_out,
    out_keep, out_send, keep, send,
    triple, output, up, down, s0, s1, s2, s3, n0, n1, n2, n3, qkv0, qkv1, lse0, lse1, ctx0, ctx1, act0, act1,
    slope0, slope1, wide, bias0, bias1, turned, blocks, last, grad, stage, pack, small, proj, dctx, first_grad,
    own_global, own_local, own_global_back, own_local_back, load_sems, store_sems,
):
    me, replica = lax.axis_index("section"), lax.axis_index("dp")
    per_image = sz.sections // sz.images
    image, crop = me // per_image, me % per_image
    sources = [(triple_in, triple), (output_in, output), (up_in, up), (down_in, down)]
    pairs = [(source.at[layer], target.at[layer]) for layer in range(2) for source, target in sources]
    several = pl.ds(crop * sz.locals, sz.locals)
    rows = [
        (global_in.at[image], own_global), (local_in.at[several], own_local),
        (global_back.at[image], own_global_back), (local_back.at[several], own_local_back),
    ]
    loads = Loads(rows + pairs, load_sems)
    bias0[...] = window_bias(sz, 0)
    bias1[...] = window_bias(sz, 1)
    biases = (bias0, bias1)
    patches = sz.global_len - 1
    limit = lax.div((ratio_ref[image] + 1) * patches, jnp.int32(10))
    both = rank_ref[image]
    places = lax.broadcasted_iota(jnp.int32, both.shape, 0)
    ranks = jnp.sum(jnp.where(places == crop, both, 0), axis=0, keepdims=True)
    shape = (sz.rows, patches)
    row = lax.broadcasted_iota(jnp.int32, shape, 0)
    column = lax.broadcasted_iota(jnp.int32, shape, 1)
    chosen = jnp.where((row == column + 1) & (ranks < limit), 1.0, 0.0)
    chosen = jnp.max(chosen, axis=-1, keepdims=True)
    masked_ref[...] = jnp.broadcast_to(chosen, masked_ref.shape)
    loads.wait(0, 1)
    gather_rows(sz, own_global, own_local, crop, image, wide)
    s0[...] = jnp.where(chosen > 0.5, token_ref[...].astype(f32), wide[...]).astype(bf16)
    loads.wait(2, 3)
    gather_rows(sz, own_global_back, own_local_back, crop, image, wide)
    first_grad[...] = wide[...].astype(bf16)

    def attend_weights(layer):
        return (
            row_of(gain_a, layer), row_of(shift_a, layer), triple.at[layer], row_of(pair, layer), output.at[layer],
            row_of(output_b, layer),
        )

    def expand_weights(layer):
        return (
            row_of(gain_e, layer), row_of(shift_e, layer), up.at[layer], row_of(up_b, layer), down.at[layer],
            row_of(down_b, layer),
        )

    loads.wait(4, 5)
    attend_forward(sz, s0, attend_weights(0), s1, n0, qkv0, lse0, ctx0, biases)
    stores = [
        pltpu.make_async_copy(source, target, store_sems.at[i])
        for i, (source, target) in enumerate(
            [(s0, s0_out), (s1, s1_out), (n0, n0_out), (qkv0, qkv0_out), (lse0, lse0_out), (ctx0, ctx0_out)]
        )
    ]
    for move in stores:
        move.start()
    loads.wait(6, 7)
    expand_forward(sz, s1, expand_weights(0), s2, n1, act0, slope0, wide)
    more = [
        pltpu.make_async_copy(source, target, store_sems.at[len(stores) + i])
        for i, (source, target) in enumerate([(n1, n1_out), (act0, act0_out), (slope0, slope0_out)])
    ]
    for move in more:
        move.start()
    stores += more
    loads.wait(8, 9)
    attend_forward(sz, s2, attend_weights(1), s3, n2, qkv1, lse1, ctx1, biases)
    loads.wait(10, 11)
    expand_forward(sz, s3, expand_weights(1), last, n3, act1, slope1, wide)
    more = put_rows(sz, last[...], me, turned, blocks, stage, out_keep, out_send, store_sems.at[len(stores)])
    for move in more:
        move.start()
    stores += more
    small[...] = jnp.zeros_like(small)
    scratch = (wide, turned, blocks)
    expand_backward(
        sz, me, s3, n3, first_grad, act1, slope1, row_of(gain_e, 1), up.at[1], down.at[1], grad, scratch, pack,
        sz.attend_full, small,
    )
    attend_backward(
        sz, me, s2, n2, grad, qkv1, lse1, ctx1, row_of(gain_a, 1), triple.at[1], output.at[1], dh_out, scratch, pack, 0,
        small, proj, dctx, biases,
    )
    rows = sz.packed(sz.attend_full + sz.expand_full)
    put_small(pack, sz.attend_full + sz.expand_full, rows, small)
    more = ship(sz, me, replica, pack, rows, keep, send, store_sems.at[10])
    for move in more:
        move.start()
    for move in stores + more:
        move.wait()


def expand_kernel(
    sz, h_ref, normed, grad_ref, act_ref, slope_ref, gain_e, up, down, _after, _after_rows,
    dh_ref, keep, send, total, turned, blocks, pack, small, up_v, down_v, sems,
):
    me, replica = lax.axis_index("section"), lax.axis_index("dp")
    small[...] = jnp.zeros_like(small)
    loads = Loads([(up.at[0], up_v), (down.at[0], down_v)], sems)
    loads.wait(0, 1)
    expand_backward(
        sz, me, h_ref, normed, grad_ref, act_ref, slope_ref, row_of(gain_e, 0), up_v, down_v, dh_ref,
        (total, turned, blocks), pack, 0, small,
    )
    rows = sz.packed(sz.expand_full)
    put_small(pack, sz.expand_full, rows, small)
    moves = ship(sz, me, replica, pack, rows, keep, send, sems.at[2])
    for move in moves:
        move.start()
    for move in moves:
        move.wait()


def attend_kernel(
    sz, h_ref, normed, grad_ref, qkv_ref, lse_ref, ctx_ref, gain_a, triple, output, masked_ref,
    _after, _after_rows, _after_other, in_keep, in_send, keep, send, total, turned, blocks, pack, small, proj, dctx, bias0, bias1, stage, triple_v, output_v,
    sems,
):
    me, replica = lax.axis_index("section"), lax.axis_index("dp")
    loads = Loads([(triple.at[0], triple_v), (output.at[0], output_v)], sems)
    bias0[...] = window_bias(sz, 0)
    bias1[...] = window_bias(sz, 1)
    small[...] = jnp.zeros_like(small)
    loads.wait(0, 1)
    after = attend_backward(
        sz, me, h_ref, normed, grad_ref, qkv_ref, lse_ref, ctx_ref, row_of(gain_a, 0), triple_v, output_v, total,
        (total, turned, blocks), pack, 0, small, proj, dctx, (bias0, bias1),
    )
    masked = masked_ref[:, :1] > 0.5
    put_vector(small, after, jnp.sum(jnp.where(masked, total[...], 0.0), axis=0, keepdims=True))
    rows = sz.packed(sz.attend_full)
    put_small(pack, sz.attend_full, rows, small)
    moves = ship(sz, me, replica, pack, rows, keep, send, sems.at[2])
    for move in moves:
        move.start()
    more = put_rows(
        sz, jnp.where(masked, 0.0, total[...]).astype(bf16), me, turned, blocks, stage, in_keep, in_send, sems.at[3]
    )
    for move in more:
        move.start()
    for move in moves + more:
        move.wait()


def finish_kernel(sz, *refs):
    parts, row_parts = refs[:3], (refs[3:6], refs[6:9])
    (
        out_global, out_local, in_global, in_local, token, gain_a, shift_a, triple, pair, output, output_b,
        gain_e, shift_e, up, up_b, down, down_b,
    ) = refs[9:26]
    scratch = refs[26:29]
    row_scratch, vectors, wide, sems = refs[29:]
    me, replica = lax.axis_index("section"), lax.axis_index("dp")
    moves = []
    for source, target in zip(parts, scratch):
        shard = target.shape[0] // sz.shards
        for place in range(sz.shards):
            options = [sz.offset(core, place, False)[1] for core in range(2)]
            offset = jnp.where(me & 1 == 0, options[0], options[1])
            at = pl.multiple_of((replica & sz.shards - 1 ^ offset) * shard, 16)
            moves.append(
                pltpu.make_async_copy(
                    source.at[pl.ds(place * shard, shard), :], target.at[pl.ds(at, shard), :], sems.at[0]
                )
            )
    count = len(moves)
    for which, (own, core, across) in enumerate(row_parts):
        for k, source in enumerate((own.at[0], core.at[0], across.at[0], across.at[1])):
            moves.append(pltpu.make_async_copy(source, row_scratch.at[which, k], sems.at[1]))
    for move in moves:
        move.start()
    for move in moves[count:]:
        move.wait()
    per_image = sz.sections // sz.images
    for which, (to_global, to_local) in enumerate(((out_global, out_local), (in_global, in_local))):
        for k in range(4):
            section = me ^ k
            image, crop = section // per_image, section % per_image
            turned = jnp.concatenate(
                [
                    row_scratch[which, k, tile * sz.cut : (tile + 1) * sz.cut, :].astype(f32)
                    for tile in range(sz.rows // LANES)
                ],
                axis=1,
            )
            to_global[section] = turned[:, : sz.global_len]
            turned = jnp.concatenate([turned, jnp.zeros((LANES - sz.cut, sz.rows), f32)], axis=0)
            wide[...] = turned.T
            for at in range(sz.locals):
                start = sz.global_len + at * sz.local_len
                to_local[crop * sz.locals + at, :, pl.ds(image, 1), :] = wide[
                    start : start + sz.local_len, : sz.cut
                ].reshape(sz.local_len, 1, sz.cut)
    for move in moves[:count]:
        move.wait()
    width, tiles, cut = sz.width, sz.tiles, sz.cut
    row = lax.broadcasted_iota(jnp.int32, (width, cut), 0)
    column = lax.broadcasted_iota(jnp.int32, (width, cut), 1)
    pick = jnp.where(row == column + me * cut, 1.0, 0.0).astype(bf16)
    row = lax.broadcasted_iota(jnp.int32, (2 * width, 2 * cut), 0)
    column = lax.broadcasted_iota(jnp.int32, (2 * width, 2 * cut), 1)
    pick_pair = jnp.where(row == column + me * 2 * cut, 1.0, 0.0).astype(bf16)
    hidden_tiles = sz.hidden // LANES
    places = (
        ((scratch[2], 0, sz.attend_full), (scratch[1], 0, sz.expand_full)),
        (
            (scratch[0], 0, sz.attend_full + sz.expand_full),
            (scratch[0], sz.attend_full, sz.attend_full + sz.expand_full),
        ),
    )
    for layer in range(2):
        one = slice(layer, layer + 1)
        (attend, attend_at, attend_small), (expand, expand_at, expand_small) = places[layer]

        def tile_row(source, base, tile):
            return source[base + tile * cut : base + (tile + 1) * cut, :].astype(f32)

        for tile in range(3 * tiles):
            triple[layer, :, tile * LANES : (tile + 1) * LANES] = tile_row(attend, attend_at, tile)
        for tile in range(tiles):
            output[layer, :, tile * LANES : (tile + 1) * LANES] = tile_row(attend, attend_at + 3 * tiles * cut, tile)
        for tile in range(hidden_tiles):
            up[layer, :, tile * LANES : (tile + 1) * LANES] = tile_row(expand, expand_at, tile)
        for tile in range(tiles):
            base = expand_at + hidden_tiles * cut + tile * sz.hidden_cut
            down[layer, :, tile * LANES : (tile + 1) * LANES] = expand[base : base + sz.hidden_cut, :].astype(f32)

        def vector(at, tiles_in):
            return jnp.concatenate([vectors[at + t : at + t + 1, :] for t in range(tiles_in)], axis=1)

        def picked(at):
            return dot(vector(at, tiles).astype(bf16), pick)

        vectors[...] = attend[attend_small : attend_small + sz.small_rows, :].astype(f32)
        gain_a[one, :] = picked(0)
        shift_a[one, :] = picked(tiles)
        pair[one, :] = dot(vector(2 * tiles, 2 * tiles).astype(bf16), pick_pair)
        output_b[one, :] = picked(4 * tiles)
        if layer == 0:
            token[...] = picked(5 * tiles)
        vectors[...] = expand[expand_small : expand_small + sz.small_rows, :].astype(f32)
        start = sz.expand_small
        gain_e[one, :] = picked(start)
        shift_e[one, :] = picked(start + tiles)
        up_tiles = sz.hidden_cut // LANES
        for tile in range(up_tiles):
            up_b[one, tile * LANES : (tile + 1) * LANES] = vectors[
                pl.ds(start + 2 * tiles + me * up_tiles + tile, 1), :
            ]
        down_b[one, :] = picked(start + 2 * tiles + hidden_tiles)


VMEM = pl.BlockSpec(memory_space=pltpu.VMEM)
ANY = pl.BlockSpec(memory_space=pl.ANY)
SMEM = pl.BlockSpec(memory_space=pltpu.SMEM)
DMA = pltpu.SemaphoreType.DMA


def call(body, name, outs, in_specs, scratch, args, flops):
    return pl.pallas_call(
        body,
        name=name,
        out_shape=tuple(jax.ShapeDtypeStruct(shape, kind) for shape, kind, _ in outs),
        in_specs=in_specs,
        out_specs=tuple(memory for _, _, memory in outs),
        scratch_shapes=[pltpu.VMEM(*item) if isinstance(item, tuple) else item for item in scratch],
        compiler_params=pltpu.CompilerParams(vmem_limit_bytes=VMEM_BYTES),
        cost_estimate=pl.CostEstimate(flops=flops, bytes_accessed=1 << 20, transcendentals=0),
    )(*args)


def add(a, b):
    return lax.reduce_precision(a.astype(f32) + b.astype(f32), 8, 7).astype(bf16)


def swap(value, partner_of):
    sections, replicas = lax.axis_size("section"), lax.axis_size("dp")
    route = []
    for section in range(sections):
        for replica in range(replicas):
            to_section, to_replica = partner_of(section, replica)
            route.append((section * replicas + replica, to_section * replicas + to_replica))
    return lax.ppermute(value, ("section", "dp"), route)


def other_core(section, replica):
    return section ^ 1, replica


def other_x(section, replica):
    return section ^ 2, replica


def along(orders, step):
    def partner_of(section, replica):
        axis = orders[section & 1][step]
        return (section ^ 2, replica) if axis == X_AXIS else (section, replica ^ (1 << axis))

    return partner_of


def reduce_steps(sz, keep, send):
    mine = add(keep, swap(send, other_core))
    yield mine
    for step in range(len(sz.orders[0])):
        half = mine.shape[0] // 2
        mine = add(mine[:half], swap(mine[half:], along(sz.orders, step)))
        yield mine
    for axis in sz.rest:
        mine = add(mine, swap(mine, along(([axis], [axis]), 0)))
        yield mine
    back = [[axis for axis in order if axis != X_AXIS] for order in sz.orders]
    for step in reversed(range(len(back[0]))):
        mine = jnp.concatenate([mine, swap(mine, along(back, step))], axis=0)
        yield mine


def finished(steps, value):
    for value in steps:
        pass
    return value


def per_device(
    global_rows, local_rows, patch_rank, ratio_bin, mask_token, attend_gain, attend_shift, triple_weight,
    pair_bias, output_weight, output_bias, expand_gain, expand_shift, up_weight, up_bias, down_weight,
    down_bias, grad_global, grad_local,
):
    sections, replicas = lax.axis_size("section"), lax.axis_size("dp")
    sz = Sizes(global_rows, local_rows, up_weight, sections, replicas)
    width, rows, hidden = sz.width, sz.rows, sz.hidden
    sets = [rows_of.transpose(0, 2, 1, 3) for rows_of in (global_rows, grad_global)]
    many = [rows_of.transpose(1, 2, 0, 3) for rows_of in (local_rows, grad_local)]
    wide = ((rows, width), bf16)
    triple_rows = ((rows, 3 * width), bf16)
    hidden_rows = ((rows, hidden), bf16)
    lse = ((sz.lse_rows, LANES), f32)
    flags = ((rows, LANES), f32)
    wide_f32 = ((rows, width), f32)
    turned = ((width, rows), bf16)
    small = ((sz.small_rows, LANES), f32)
    share = ((2, sz.extra, LANES), bf16)
    stage = ((sections, sz.extra, LANES), bf16)
    windows = [((length, length), f32) for _, length in sz.windows]
    totals = [sz.packed(full) for full in (sz.attend_full + sz.expand_full, sz.expand_full, sz.attend_full)]
    packs = [((sections, total, LANES), bf16) for total in totals]
    parts = [((2 * total, LANES), bf16) for total in totals]

    def placed(kinds, memory):
        return [kind + (memory,) for kind in kinds]

    (
        s0, s1, n0, n1, qkv, lses, context, active, slope, masked, grad, out_keep, out_send, keep, send
    ) = call(
        lambda *refs: front_kernel(sz, *refs),
        "front",
        placed([wide] * 4 + [triple_rows, lse, wide, hidden_rows, hidden_rows], ANY)
        + placed([flags, wide], VMEM)
        + placed([share] * 2 + [parts[0]] * 2, ANY),
        [ANY] * 4 + [VMEM, SMEM, VMEM, VMEM, VMEM, ANY, VMEM, ANY, VMEM, VMEM, VMEM, ANY, VMEM, ANY, VMEM],
        [(weight.shape, bf16) for weight in (triple_weight, output_weight, up_weight, down_weight)]
        + [wide] * 8 + [triple_rows] * 2 + [lse] * 2 + [wide] * 2 + [hidden_rows] * 4 + [wide_f32]
        + windows + [turned] * 2 + [wide] * 2 + [stage, packs[0], small, triple_rows, wide, wide]
        + [(sets[0].shape[1:], bf16), ((sz.locals,) + many[0].shape[1:], bf16)] * 2
        + [DMA((12,)), DMA((11,))],
        (
            sets[0], many[0], sets[1], many[1], patch_rank, ratio_bin, mask_token, attend_gain, attend_shift, triple_weight, pair_bias,
            output_weight, output_bias, expand_gain, expand_shift, up_weight, up_bias, down_weight, down_bias,
        ),
        8 << 30,
    )
    core = swap(out_send, other_core)
    later_steps = reduce_steps(sz, keep, send)
    later = next(later_steps)
    grad, keep, send = call(
        lambda *refs: expand_kernel(sz, *refs),
        "expand_back",
        placed([wide], VMEM) + placed([parts[1]] * 2, ANY),
        [VMEM] * 6 + [ANY] * 4,
        [wide_f32, turned, turned, packs[1], small, (up_weight.shape[1:], bf16), (down_weight.shape[1:], bf16), DMA((3,))],
        (s1, n1, grad, active, slope, expand_gain, up_weight, down_weight, later[:16], core),
        4 << 30,
    )
    out_rows = (out_keep, core, swap(jnp.stack([out_keep[1], core[1]]), other_x))
    later = next(later_steps)
    expand_steps = reduce_steps(sz, keep, send)
    expand = next(expand_steps)
    in_keep, in_send, keep, send = call(
        lambda *refs: attend_kernel(sz, *refs),
        "attend_back",
        placed([share] * 2 + [parts[2]] * 2, ANY),
        [VMEM] * 7 + [ANY] * 2 + [VMEM] + [ANY] * 3,
        [wide_f32, turned, turned, packs[2], small, triple_rows, wide] + windows
        + [stage, (triple_weight.shape[1:], bf16), (output_weight.shape[1:], bf16), DMA((4,))],
        (s0, n0, grad, qkv, lses, context, attend_gain, triple_weight, output_weight, masked, later[:16],
         out_rows[2], expand[:16]),
        4 << 30,
    )
    attend = finished(reduce_steps(sz, keep, send), keep)
    core = swap(in_send, other_core)
    in_rows = (in_keep, core, swap(jnp.stack([in_keep[1], core[1]]), other_x))
    later = finished(later_steps, later)
    expand = finished(expand_steps, expand)
    cut = sz.cut
    outs = [(sz.all_globals, cut, sz.global_len), local_rows.shape[1:3] + (sz.images, cut)] * 2 + [
        (1, cut), (2, cut), (2, cut), (2, cut, 3 * width), (2, 2 * cut), (2, cut, width), (2, cut), (2, cut), (2, cut),
        (2, cut, hidden), (2, sz.hidden_cut), (2, sz.hidden_cut, width), (2, cut),
    ]
    final = call(
        lambda *refs: finish_kernel(sz, *refs),
        "finish",
        [(shape, f32, VMEM) for shape in outs],
        [ANY] * 9,
        [((total, LANES), bf16) for total in totals]
        + [((2, 4, sz.extra, LANES), bf16), small, flags, DMA((2,))],
        (later, expand, attend, *out_rows, *in_rows),
        1 << 28,
    )
    shape = global_rows.shape[:2] + (cut, sz.global_len)
    return (
        final[0].reshape(shape).transpose(0, 1, 3, 2),
        final[1].transpose(2, 0, 1, 3),
        final[2].reshape(shape).transpose(0, 1, 3, 2),
        final[3].transpose(2, 0, 1, 3),
        *final[4:],
    )


def solution(mesh):
    rows, copied = P("dp", None, None, None), P()
    in_specs = (rows, rows, P("dp", None, None), P("dp")) + (copied,) * 13 + (rows, rows)
    wide, flat, deep = P("dp", None, None, "section"), P(None, "section"), P(None, "section", None)
    out_specs = (
        wide, wide, wide, wide, flat, flat, flat, deep, flat, deep, flat, flat, flat, deep, flat, deep, flat,
    )
    return jax.shard_map(per_device, mesh=mesh, in_specs=in_specs, out_specs=out_specs, check_vma=False)
```

```python
import math

import jax
import jax.numpy as jnp
from jax import lax
from jax.experimental import pallas as pl
from jax.experimental.pallas import tpu as pltpu
from jax.sharding import PartitionSpec as P

HEADS = 6
EPS = 1e-06
LANES = 128
VMEM_MIB = {"front": 26, "finish": 20}
CHOICES = (0, 0, 1, 0)
PLAN = (
    "A later_core later_attend A B expand",
    "core C B A C",
    "attend D D A B C",
    "output R A B D C",
    "B A C D B",
    "A D R C B",
    "D C R A D",
    "C B D A B",
    "C D R",
)
X_AXIS = -1

f32 = jnp.float32
bf16 = jnp.bfloat16


def up_to(value, step):
    return (value + step - 1) // step * step


class Sizes:
    def __init__(self, global_rows, local_rows, up_weight, sections, replicas):
        images, crops, self.global_len, self.width = global_rows.shape
        _, local_crops, self.local_len, _ = local_rows.shape
        self.hidden = up_weight.shape[2]
        self.sections = sections
        self.replicas = replicas
        self.images = images
        self.all_globals = images * crops
        self.all_locals = images * local_crops
        self.locals = self.all_locals // sections
        self.used = self.global_len + self.locals * self.local_len
        self.rows = up_to(self.used, LANES)
        self.head = self.width // HEADS
        self.cut = self.width // sections
        self.hidden_cut = self.hidden // sections
        self.tiles = self.width // LANES
        self.first_end = up_to(self.global_len, 16)
        self.second_start = self.global_len // 16 * 16
        self.windows = (
            (0, self.first_end),
            (self.second_start, self.rows - self.second_start),
        )
        self.attend_full = 4 * self.tiles * self.cut
        self.expand_full = self.hidden // LANES * self.cut + self.tiles * self.hidden_cut
        self.small_rows = up_to(max(6 * self.tiles, 3 * self.tiles + self.hidden // LANES), 16)
        self.extra = self.cut * self.rows // LANES
        bits = replicas.bit_length() - 1
        low = list(range(min(bits, 2)))
        last_first = low[1:] + [X_AXIS] + low[:1]
        first_last = [X_AXIS] + low
        middle = low[:1] + [X_AXIS] + low[1:]
        choices = ((first_last, last_first), (middle, last_first), (first_last, middle))
        self.orders = {name: choices[choice] for name, choice in zip("ABCD", CHOICES)}
        self.rest = list(range(len(low), bits))
        self.shards = 1 << len(low)
        self.unit = 16 * self.shards

    def packed(self, full):
        return up_to(full + self.small_rows, self.unit)

    def place(self, orders, core, across, offset):
        order = orders[core]
        return sum(
            (across if axis == X_AXIS else offset >> axis & 1) << (len(order) - 1 - at) for at, axis in enumerate(order)
        )

    def offset(self, orders, core, place):
        order = [axis for axis in orders[core] if axis != X_AXIS]
        return sum((place >> (len(order) - 1 - at) & 1) << axis for at, axis in enumerate(order))


def dot(a, b):
    return jnp.dot(a, b, preferred_element_type=f32)


def dot_last(a, b):
    return lax.dot_general(a, b, (((1,), (1,)), ((), ())), preferred_element_type=f32)


def dot_first(a, b):
    return lax.dot_general(a, b, (((0,), (0,)), ((), ())), preferred_element_type=f32)


def normalize(hidden):
    average = jnp.mean(hidden, axis=-1, keepdims=True)
    centred = hidden - average
    inverse = lax.rsqrt(jnp.mean(centred * centred, axis=-1, keepdims=True) + EPS)
    return centred * inverse, inverse


def row_blocks(sz):
    return [slice(i, i + LANES) for i in range(0, sz.rows, LANES)]


def head_mask(sz, rows, which):
    lane = lax.broadcasted_iota(jnp.int32, (rows, 2 * sz.head), 1)
    return lane < sz.head if which == 0 else lane >= sz.head


def window_bias(sz, which):
    start, length = sz.windows[which]

    def group(row):
        if which == 0:
            return jnp.where(row < sz.global_len, 0, 1)
        kind = jnp.where(row + start < sz.global_len, 0, 1)
        for crop in range(1, sz.locals + 1):
            kind = kind + jnp.where(row + start >= sz.global_len + crop * sz.local_len, 1, 0)
        return kind

    left = group(lax.broadcasted_iota(jnp.int32, (length, length), 0))
    right = group(lax.broadcasted_iota(jnp.int32, (length, length), 1))
    return jnp.where(left == right, 0.0, -1e30).astype(f32)


def own_rows(sz, which):
    start, length = sz.windows[which]
    row = lax.broadcasted_iota(jnp.int32, (length, 1), 0) + start
    return row < sz.global_len if which == 0 else row >= sz.global_len


def store_window(sz, which, ref, columns, value):
    start, length = sz.windows[which]
    if which == 0 or sz.first_end == start:
        ref[start : start + length, columns] = value.astype(bf16)
        return
    shared = sz.first_end - start
    row = lax.broadcasted_iota(jnp.int32, (shared, value.shape[1]), 0) + start
    before = ref[start : sz.first_end, columns].astype(f32)
    ref[start : sz.first_end, columns] = jnp.where(
        row < sz.global_len, before, value[:shared]
    ).astype(bf16)
    ref[sz.first_end : start + length, columns] = value[shared:].astype(bf16)


def norm_rows(sz, h_ref, gain, shift, normed_ref):
    for rows in row_blocks(sz):
        scaled, _ = normalize(h_ref[rows, :].astype(f32))
        normed_ref[rows, :] = (scaled * gain + shift).astype(bf16)


def stacked_heads(sz, value):
    zero = jnp.zeros_like(value)
    return jnp.concatenate([jnp.where(head_mask(sz, value.shape[0], which), value, zero) for which in range(2)], axis=0)


def attend_forward(sz, h_ref, weights, out_ref, normed_ref, qkv_ref, lse_ref, ctx_ref, bias_refs):
    gain, shift, triple_ref, pair_bias, output_ref, output_bias = weights
    width = sz.width
    norm_rows(sz, h_ref, gain, shift, normed_ref)
    scale = 1.0 / math.sqrt(sz.head)
    for part in range(3):
        columns = slice(part * width, (part + 1) * width)
        project = dot(normed_ref[...], triple_ref[:, columns])
        if part == 0:
            project = (project + pair_bias[:, :width]) * scale
        if part == 2:
            project = project + pair_bias[:, width:]
        qkv_ref[:, columns] = project.astype(bf16)
    for which, (start, length) in enumerate(sz.windows):
        rows = slice(start, start + length)
        bias = bias_refs[which]
        lane = lax.broadcasted_iota(jnp.int32, (length, LANES), 1)
        first = head_mask(sz, length, 0)
        kept = jnp.zeros((length, LANES), f32)
        for pair in range(HEADS // 2):
            at = 2 * sz.head * pair
            queries, keys, values = (
                qkv_ref[rows, part * width + at : part * width + at + 2 * sz.head] for part in range(3)
            )
            scores = dot_last(stacked_heads(sz, queries), keys)
            probs = []
            for which_head in range(2):
                own = scores[which_head * length : (which_head + 1) * length] + bias[...]
                top = jnp.max(own, axis=-1, keepdims=True)
                raised = jnp.exp(own - top)
                total = jnp.sum(raised, axis=-1, keepdims=True)
                kept = jnp.where(lane == 2 * pair + which_head, top + jnp.log(total), kept)
                probs.append((raised * (1.0 / total)).astype(bf16))
            context = dot(jnp.concatenate(probs, axis=0), values)
            store_window(
                sz, which, ctx_ref, slice(at, at + 2 * sz.head), jnp.where(first, context[:length], context[length:])
            )
        lse_ref[8 * which : 8 * which + 8, :length] = kept.T[:8]
    moved = dot(ctx_ref[...], output_ref[...]) + output_bias
    out_ref[...] = (h_ref[...].astype(f32) + moved).astype(bf16)


def expand_hidden(sz, h_ref, weights, normed_ref, active_ref, slope_ref):
    gain, shift, up_ref, up_bias = weights
    norm_rows(sz, h_ref, gain, shift, normed_ref)
    for at in range(0, sz.hidden, sz.hidden_cut):
        columns = slice(at, at + sz.hidden_cut)
        before = dot(normed_ref[...], up_ref[:, columns]) + up_bias[:, columns]
        share = 0.5 + 0.5 * lax.erf(before * math.sqrt(0.5))
        active_ref[:, columns] = (before * share).astype(bf16)
        density = jnp.exp(before * before * -0.5) * (1.0 / math.sqrt(2.0 * math.pi))
        slope_ref[:, columns] = (share + before * density).astype(bf16)


def expand_output(h_ref, active_ref, down_ref, down_bias):
    return h_ref[...].astype(f32) + dot(active_ref[...], down_ref[...]) + down_bias


def turned_blocks(sz, value, me, turned_ref, blocks_ref):
    turned_ref[...] = value.T
    for j in range(sz.sections):
        source = pl.multiple_of((me ^ j) * sz.cut, sz.cut)
        blocks_ref[j * sz.cut : (j + 1) * sz.cut, :] = turned_ref[pl.ds(source, sz.cut), :]


def put_vector(small, at, vector):
    for tile in range(vector.shape[1] // LANES):
        small[at + tile : at + tile + 1, :] = vector[:, tile * LANES : (tile + 1) * LANES]
    return at + vector.shape[1] // LANES


def put_tiles(pack, j, at, value):
    r = value.shape[0]
    for tile in range(value.shape[1] // LANES):
        pack[j, pl.ds(at + tile * r, r), :] = value[:, tile * LANES : (tile + 1) * LANES].astype(bf16)


def norm_backward(sz, h_ref, grad_ref, grad_normed_ref, gain, dh_ref):
    gain_sum = jnp.zeros((1, sz.width), f32)
    shift_sum = jnp.zeros((1, sz.width), f32)
    for rows in row_blocks(sz):
        scaled, inverse = normalize(h_ref[rows, :].astype(f32))
        grad_normed = grad_normed_ref[rows, :]
        grad_scaled = grad_normed * gain
        first = jnp.mean(grad_scaled, axis=-1, keepdims=True)
        second = jnp.mean(grad_scaled * scaled, axis=-1, keepdims=True)
        grad_in = inverse * (grad_scaled - first - scaled * second)
        dh_ref[rows, :] = (grad_ref[rows, :].astype(f32) + grad_in).astype(dh_ref.dtype)
        gain_sum += jnp.sum(grad_normed * scaled, axis=0, keepdims=True)
        shift_sum += jnp.sum(grad_normed, axis=0, keepdims=True)
    return gain_sum, shift_sum


def expand_backward(sz, me, h_ref, normed, grad_ref, act_ref, slope_ref, gain, up, down, dh_ref, scratch, pack, small):
    total, turned, blocks = scratch
    base = 0
    part = sz.hidden_cut
    up_rows = sz.hidden // LANES * sz.cut
    turned_blocks(sz, normed[...], me, turned, blocks)
    after = 2 * sz.tiles
    for j in range(sz.sections):
        owner = me ^ j
        columns = pl.ds(pl.multiple_of(owner * part, LANES), part)
        put_tiles(pack, j, base + up_rows, dot_first(act_ref[:, columns], grad_ref[...]))
        grad_active = dot_last(grad_ref[...], down[columns, :])
        grad_before = (grad_active * slope_ref[:, columns].astype(f32)).astype(bf16)
        up_sum = jnp.sum(grad_before.astype(f32), axis=0, keepdims=True)
        for tile in range(part // LANES):
            small[pl.ds(after + owner * (part // LANES) + tile, 1), :] = up_sum[:, tile * LANES : (tile + 1) * LANES]
        up_grad = dot(blocks[...], grad_before)
        at = base + pl.multiple_of(owner * (part // LANES * sz.cut), 16)
        for other in range(sz.sections):
            put_tiles(pack, other, at, up_grad[other * sz.cut : (other + 1) * sz.cut, :])
        more = dot_last(grad_before, up[:, columns])
        if j == 0:
            total[...] = more
        else:
            total[...] += more
    gain_sum, shift_sum = norm_backward(sz, h_ref, grad_ref, total, gain, dh_ref)
    put_vector(small, 0, gain_sum)
    put_vector(small, sz.tiles, shift_sum)
    put_vector(
        small, after + sz.hidden // LANES, jnp.sum(grad_ref[...].astype(f32), axis=0, keepdims=True)
    )


def attend_core_backward(sz, grad_ref, output, qkv_ref, lse_ref, proj, dctx, bias_refs):
    width = sz.width
    dctx[...] = dot_last(grad_ref[...], output[...]).astype(bf16)
    scale = 1.0 / math.sqrt(sz.head)
    for which, (start, length) in enumerate(sz.windows):
        rows = slice(start, start + length)
        bias = bias_refs[which]
        own = own_rows(sz, which)
        for pair in range(HEADS // 2):
            at = 2 * sz.head * pair
            columns = [slice(part * width + at, part * width + at + 2 * sz.head) for part in range(3)]
            queries, keys, values = (qkv_ref[rows, c] for c in columns)
            grad_ctx = jnp.where(own, dctx[rows, columns[0]], jnp.zeros((length, 2 * sz.head), bf16))
            keys = stacked_heads(sz, keys)
            scores = dot_last(keys, queries)
            grad_probs = dot_last(stacked_heads(sz, values), grad_ctx)
            probs, grad_scores = [], []
            for which_head in range(2):
                part = slice(which_head * length, (which_head + 1) * length)
                row = 8 * which + 2 * pair + which_head
                prob = jnp.exp(scores[part] + bias[...] - lse_ref[row : row + 1, :length])
                grad_prob = grad_probs[part]
                delta = jnp.sum(prob * grad_prob, axis=0, keepdims=True)
                grad_scores.append((prob * (grad_prob - delta)).astype(bf16))
                probs.append(prob.astype(bf16))
            grad_scores = jnp.concatenate(grad_scores, axis=0)
            first = head_mask(sz, length, 0)
            grad_keys = dot(grad_scores, queries)
            grad_values = dot(jnp.concatenate(probs, axis=0), grad_ctx)
            store_window(sz, which, proj, columns[0], dot_first(grad_scores, keys) * scale)
            store_window(sz, which, proj, columns[1], jnp.where(first, grad_keys[:length], grad_keys[length:]))
            store_window(sz, which, proj, columns[2], jnp.where(first, grad_values[:length], grad_values[length:]))


def attend_backward(sz, me, h_ref, normed, grad_ref, ctx_ref, proj, gain, triple, dh_ref, scratch, pack, small):
    total, turned, blocks = scratch
    width = sz.width
    grad = grad_ref[...]
    out_rows = 3 * sz.tiles * sz.cut
    turned_blocks(sz, ctx_ref[...], me, turned, blocks)
    output_grad = dot(blocks[...], grad)
    for j in range(sz.sections):
        put_tiles(pack, j, out_rows, output_grad[j * sz.cut : (j + 1) * sz.cut, :])
    turned_blocks(sz, normed[...], me, turned, blocks)
    after = 2 * sz.tiles
    for part in range(3):
        columns = slice(part * width, (part + 1) * width)
        grad_part = proj[:, columns]
        triple_grad = dot(blocks[...], grad_part)
        for j in range(sz.sections):
            put_tiles(pack, j, part * sz.tiles * sz.cut, triple_grad[j * sz.cut : (j + 1) * sz.cut, :])
        if part != 1:
            after = put_vector(small, after, jnp.sum(grad_part.astype(f32), axis=0, keepdims=True))
    total[...] = dot_last(proj[...], triple[...])
    gain_sum, shift_sum = norm_backward(sz, h_ref, grad_ref, total, gain, dh_ref)
    put_vector(small, 0, gain_sum)
    put_vector(small, sz.tiles, shift_sum)
    return put_vector(small, after, jnp.sum(grad.astype(f32), axis=0, keepdims=True))


def put_rows(sz, value, me, turned, blocks, keep, send):
    turned_blocks(sz, value, me, turned, blocks)
    for j in range(sz.sections):
        for tile in range(sz.rows // LANES):
            (keep, send)[j % 2][j // 2, tile * sz.cut : (tile + 1) * sz.cut, :] = blocks[
                j * sz.cut : (j + 1) * sz.cut, tile * LANES : (tile + 1) * LANES
            ]


def ship(sz, orders, me, replica, pack, rows, keep, send):
    size = rows // sz.shards
    for shard in range(sz.shards):
        offset = replica & sz.shards - 1 ^ shard
        for core in range(2):
            for across in range(2):
                options = [sz.place(orders, c, across, offset) for c in range(2)]
                place = jnp.where(me & 1 ^ core == 0, options[0], options[1])
                target = (keep, send)[core]
                target[pl.ds(pl.multiple_of(place * size, 16), size), :] = pack[
                    2 * across + core, shard * size : (shard + 1) * size, :
                ]


def put_small(pack, start, rows, small):
    held = small.shape[0]
    for j in range(pack.shape[0]):
        pack[j, start : start + held, :] = small[...].astype(bf16)
        if start + held < rows:
            pack[j, start + held : rows, :] = jnp.zeros((rows - start - held, LANES), bf16)


class Moves:
    def __init__(self, pairs, sems):
        self.copies = [pltpu.make_async_copy(source, target, sems.at[i]) for i, (source, target) in enumerate(pairs)]

    def start(self, *which):
        for i in which:
            self.copies[i].start()

    def wait(self, *which):
        for i in which:
            self.copies[i].wait()


def row_of(ref, layer):
    return ref[layer : layer + 1, :].astype(f32)


def pick_row(block, which):
    value = block[:, 0, :].astype(f32)
    for other in range(1, block.shape[1]):
        value = jnp.where(which == other, block[:, other, :].astype(f32), value)
    return value


def gather_rows(sz, of_global, of_local, crop, image, wide):
    wide[: sz.global_len, :] = pick_row(of_global, crop)
    for at in range(sz.locals):
        start = sz.global_len + at * sz.local_len
        wide[start : start + sz.local_len, :] = pick_row(of_local.at[at], image)
    wide[sz.used :, :] = jnp.zeros((sz.rows - sz.used, sz.width), f32)


def front_kernel(sz, *refs):
    rows_in, smalls_in, ratio_ref, weights_in, refs = refs[:4], refs[4:14], refs[14], refs[15:19], refs[19:]
    (
        s0, s1, s2, s3, n0, n1, n2, qkv0, qkv1, lse0, lse1, ctx0, ctx1, act0, act1, slope0, masked_ref, grad,
        triple0, triple1, output0, output1, up0, down0, down1, gain_a, gain_e, down_b, keep, send,
    ) = refs[:30]
    (
        up1, rank_ref, token_ref, shift_a, pair, output_b, shift_e, up_b, own_global, own_local, own_global_back,
        own_local_back, n3, slope1, wide, bias0, bias1, turned, blocks, pack, small, first_grad, load_sems,
    ) = refs[30:]
    own = (own_global, own_local, own_global_back, own_local_back)
    smalls = (rank_ref, token_ref, gain_a, shift_a, pair, output_b, gain_e, shift_e, up_b, down_b)
    weights = ((triple0, output0, up0, down0), (triple1, output1, up1, down1))
    me, replica = lax.axis_index("section"), lax.axis_index("dp")
    per_image = sz.sections // sz.images
    image, crop = me // per_image, me % per_image
    several = pl.ds(crop * sz.locals, sz.locals)
    places = [image, several, image, several]
    pairs = [(source.at[place], target) for source, place, target in zip(rows_in, places, own)]
    pairs += list(zip(smalls_in, smalls))
    pairs += [(weights_in[k].at[layer], weights[layer][k]) for layer in range(2) for k in range(4)]
    loads = Moves(pairs, load_sems)
    loads.start(*range(16))
    bias0[...] = window_bias(sz, 0)
    bias1[...] = window_bias(sz, 1)
    biases = (bias0, bias1)
    patches = sz.global_len - 1
    loads.wait(*range(14))
    loads.start(*range(16, 22))
    limit = lax.div((ratio_ref[image] + 1) * patches, jnp.int32(10))
    both = rank_ref[image]
    entry = lax.broadcasted_iota(jnp.int32, both.shape, 0)
    ranks = jnp.sum(jnp.where(entry == crop, both, 0), axis=0, keepdims=True)
    shape = (sz.rows, patches)
    row = lax.broadcasted_iota(jnp.int32, shape, 0)
    column = lax.broadcasted_iota(jnp.int32, shape, 1)
    chosen = jnp.where((row == column + 1) & (ranks < limit), 1.0, 0.0)
    chosen = jnp.max(chosen, axis=-1, keepdims=True)
    masked_ref[...] = jnp.broadcast_to(chosen, masked_ref.shape)
    gather_rows(sz, own[0], own[1], crop, image, wide)
    s0[...] = jnp.where(chosen > 0.5, token_ref[...].astype(f32), wide[...]).astype(bf16)
    gather_rows(sz, own[2], own[3], crop, image, wide)
    first_grad[...] = wide[...].astype(bf16)

    def attend_weights(layer):
        triple, output, _, _ = weights[layer]
        return (
            row_of(gain_a, layer), row_of(shift_a, layer), triple, row_of(pair, layer), output, row_of(output_b, layer),
        )

    def expand_weights(layer):
        return row_of(gain_e, layer), row_of(shift_e, layer), weights[layer][2], row_of(up_b, layer)

    loads.wait(14, 15)
    attend_forward(sz, s0, attend_weights(0), s1, n0, qkv0, lse0, ctx0, biases)
    loads.wait(16, 17)
    expand_hidden(sz, s1, expand_weights(0), n1, act0, slope0)
    s2[...] = expand_output(s1, act0, down0, row_of(down_b, 0)).astype(bf16)
    loads.wait(18, 19)
    attend_forward(sz, s2, attend_weights(1), s3, n2, qkv1, lse1, ctx1, biases)
    loads.wait(20, 21)
    expand_hidden(sz, s3, expand_weights(1), n3, act1, slope1)
    small[...] = jnp.zeros_like(small)
    expand_backward(
        sz, me, s3, n3, first_grad, act1, slope1, row_of(gain_e, 1), up1, down1, grad, (wide, turned, blocks), pack, small
    )
    rows = sz.packed(sz.expand_full)
    put_small(pack, sz.expand_full, rows, small)
    ship(sz, sz.orders["A"], me, replica, pack, rows, keep, send)


def output_kernel(sz, h_ref, act_ref, down, down_b, out_keep, out_send, turned, blocks):
    me = lax.axis_index("section")
    last = expand_output(h_ref, act_ref, down, row_of(down_b, 1)).astype(bf16)
    put_rows(sz, last, me, turned, blocks, out_keep, out_send)


def expand_kernel(sz, h, normed, grad, act, slope, up, down, gain, dh_ref, keep, send, total, turned, blocks, pack, small):
    me, replica = lax.axis_index("section"), lax.axis_index("dp")
    small[...] = jnp.zeros_like(small)
    expand_backward(
        sz, me, h, normed, grad, act, slope, row_of(gain, 0), up, down, dh_ref, (total, turned, blocks), pack, small
    )
    rows = sz.packed(sz.expand_full)
    put_small(pack, sz.expand_full, rows, small)
    ship(sz, sz.orders["C"], me, replica, pack, rows, keep, send)


def attend_core_kernel(sz, grad, output, qkv, lse, proj, dctx, bias0, bias1):
    bias0[...] = window_bias(sz, 0)
    bias1[...] = window_bias(sz, 1)
    attend_core_backward(sz, grad, output, qkv, lse, proj, dctx, (bias0, bias1))


def attend_kernel(sz, layer, *refs):
    h, normed, grad, ctx, proj, triple, gain, flags = refs[:8]
    if layer == 0:
        in_keep, in_send, keep, send, total, turned, blocks, pack, small = refs[8:]
        target = total
    else:
        target, keep, send, total, turned, blocks, pack, small = refs[8:]
    me, replica = lax.axis_index("section"), lax.axis_index("dp")
    small[...] = jnp.zeros_like(small)
    rows = sz.packed(sz.attend_full)
    after = attend_backward(
        sz, me, h, normed, grad, ctx, proj, row_of(gain, layer), triple, target, (total, turned, blocks), pack, small
    )
    if layer == 0:
        masked = flags[:, :1] > 0.5
        put_vector(small, after, jnp.sum(jnp.where(masked, total[...], 0.0), axis=0, keepdims=True))
        put_rows(sz, jnp.where(masked, 0.0, total[...]).astype(bf16), me, turned, blocks, in_keep, in_send)
    put_small(pack, sz.attend_full, rows, small)
    ship(sz, sz.orders["DB"[layer]], me, replica, pack, rows, keep, send)


def finish_kernel(sz, *refs):
    parts, (out_own, out_core, in_own, in_core, across) = refs[:4], refs[4:9]
    row_parts = (
        (out_own.at[0], out_core.at[0], across.at[0], across.at[1]),
        (in_own.at[0], in_core.at[0], across.at[2], across.at[3]),
    )
    (
        out_global, out_local, in_global, in_local, token, gain_a, shift_a, triple, pair, output, output_b,
        gain_e, shift_e, up, up_b, down, down_b,
    ) = refs[9:26]
    scratch = refs[26:30]
    vectors, wide = refs[30:]
    me, replica = lax.axis_index("section"), lax.axis_index("dp")
    for source, target, orders in zip(parts, scratch, (sz.orders[name] for name in "ABCD")):
        shard = target.shape[0] // sz.shards
        for place in range(sz.shards):
            options = [sz.offset(orders, core, place) for core in range(2)]
            offset = jnp.where(me & 1 == 0, options[0], options[1])
            at = pl.multiple_of((replica & sz.shards - 1 ^ offset) * shard, 16)
            target[pl.ds(at, shard), :] = source[place * shard : (place + 1) * shard, :]
    per_image = sz.sections // sz.images
    for which, (to_global, to_local) in enumerate(((out_global, out_local), (in_global, in_local))):
        for k in range(4):
            section = me ^ k
            image, crop = section // per_image, section % per_image
            turned = jnp.concatenate(
                [
                    row_parts[which][k][tile * sz.cut : (tile + 1) * sz.cut, :].astype(f32)
                    for tile in range(sz.rows // LANES)
                ],
                axis=1,
            )
            to_global[section] = turned[:, : sz.global_len]
            turned = jnp.concatenate([turned, jnp.zeros((LANES - sz.cut, sz.rows), f32)], axis=0)
            wide[...] = turned.T
            for at in range(sz.locals):
                start = sz.global_len + at * sz.local_len
                to_local[crop * sz.locals + at, :, pl.ds(image, 1), :] = wide[
                    start : start + sz.local_len, : sz.cut
                ].reshape(sz.local_len, 1, sz.cut)
    width, tiles, cut = sz.width, sz.tiles, sz.cut
    row = lax.broadcasted_iota(jnp.int32, (width, cut), 0)
    column = lax.broadcasted_iota(jnp.int32, (width, cut), 1)
    pick = jnp.where(row == column + me * cut, 1.0, 0.0).astype(bf16)
    row = lax.broadcasted_iota(jnp.int32, (2 * width, 2 * cut), 0)
    column = lax.broadcasted_iota(jnp.int32, (2 * width, 2 * cut), 1)
    pick_pair = jnp.where(row == column + me * 2 * cut, 1.0, 0.0).astype(bf16)
    hidden_tiles = sz.hidden // LANES
    for layer in range(2):
        one = slice(layer, layer + 1)
        expand, attend = (scratch[:2], scratch[2:])[1 - layer]

        def tile_row(source, base, tile):
            return source[base + tile * cut : base + (tile + 1) * cut, :].astype(f32)

        for tile in range(3 * tiles):
            triple[layer, :, tile * LANES : (tile + 1) * LANES] = tile_row(attend, 0, tile)
        for tile in range(tiles):
            output[layer, :, tile * LANES : (tile + 1) * LANES] = tile_row(attend, 3 * tiles * cut, tile)
        for tile in range(hidden_tiles):
            up[layer, :, tile * LANES : (tile + 1) * LANES] = tile_row(expand, 0, tile)
        for tile in range(tiles):
            base = hidden_tiles * cut + tile * sz.hidden_cut
            down[layer, :, tile * LANES : (tile + 1) * LANES] = expand[base : base + sz.hidden_cut, :].astype(f32)

        def vector(at, tiles_in):
            return jnp.concatenate([vectors[at + t : at + t + 1, :] for t in range(tiles_in)], axis=1)

        def picked(at):
            return dot(vector(at, tiles).astype(bf16), pick)

        vectors[...] = attend[sz.attend_full : sz.attend_full + sz.small_rows, :].astype(f32)
        gain_a[one, :] = picked(0)
        shift_a[one, :] = picked(tiles)
        pair[one, :] = dot(vector(2 * tiles, 2 * tiles).astype(bf16), pick_pair)
        output_b[one, :] = picked(4 * tiles)
        if layer == 0:
            token[...] = picked(5 * tiles)
        vectors[...] = expand[sz.expand_full : sz.expand_full + sz.small_rows, :].astype(f32)
        gain_e[one, :] = picked(0)
        shift_e[one, :] = picked(tiles)
        up_tiles = sz.hidden_cut // LANES
        for tile in range(up_tiles):
            up_b[one, tile * LANES : (tile + 1) * LANES] = vectors[
                pl.ds(2 * tiles + me * up_tiles + tile, 1), :
            ]
        down_b[one, :] = picked(2 * tiles + hidden_tiles)


VMEM = pl.BlockSpec(memory_space=pltpu.VMEM)
ANY = pl.BlockSpec(memory_space=pl.ANY)
HBM = pl.BlockSpec(memory_space=pltpu.HBM)
SMEM = pl.BlockSpec(memory_space=pltpu.SMEM)
DMA = pltpu.SemaphoreType.DMA


def call(body, name, outs, in_specs, scratch, args, flops):
    args = [
        pltpu.with_memory_space_constraint(arg, pltpu.HBM) if spec is HBM else arg for arg, spec in zip(args, in_specs)
    ]
    return pl.pallas_call(
        body,
        name=name,
        out_shape=tuple(jax.ShapeDtypeStruct(shape, kind) for shape, kind, _ in outs),
        in_specs=in_specs,
        out_specs=tuple(memory for _, _, memory in outs),
        scratch_shapes=[pltpu.VMEM(*item) if isinstance(item, tuple) else item for item in scratch],
        compiler_params=pltpu.CompilerParams(vmem_limit_bytes=VMEM_MIB.get(name, 14) << 20),
        cost_estimate=pl.CostEstimate(flops=flops, bytes_accessed=1 << 20, transcendentals=0),
    )(*args)


def add(first, *others):
    total = first.astype(f32)
    for other in others:
        total = total + other.astype(f32)
    return lax.reduce_precision(total, 8, 7).astype(bf16)


def swap(value, partner_of):
    sections, replicas = lax.axis_size("section"), lax.axis_size("dp")
    route = []
    for section in range(sections):
        for replica in range(replicas):
            to_section, to_replica = partner_of(section, replica)
            route.append((section * replicas + replica, to_section * replicas + to_replica))
    return lax.ppermute(value, ("section", "dp"), route)


def other_core(section, replica):
    return section ^ 1, replica


def other_x(section, replica):
    return section ^ 2, replica


def along(orders, step):
    def partner_of(section, replica):
        axis = orders[section & 1][step]
        return (section ^ 2, replica) if axis == X_AXIS else (section, replica ^ (1 << axis))

    return partner_of


class Sequence:
    def __init__(self):
        self.last = None

    def after(self, value):
        return value if self.last is None else lax.optimization_barrier((value, self.last))[0]

    def mark(self, value):
        self.last = value
        return value


def reduce_steps(sz, orders, order, keep, send):
    core = swap(send, other_core)
    yield
    core = order.after(core)
    half = keep.shape[0] // 2
    moved = swap(order.mark(add(keep[half:], core[half:])), along(orders, 0))
    yield
    moved = order.after(moved)
    mine = add(keep[:half], core[:half], moved)
    for step in range(1, len(orders[0])):
        half = mine.shape[0] // 2
        moved = swap(order.mark(mine[half:]), along(orders, step))
        yield
        mine = add(mine[:half], order.after(moved))
    for axis in sz.rest:
        moved = swap(order.mark(mine), along(([axis], [axis]), 0))
        yield
        mine = add(mine, order.after(moved))
    back = [[axis for axis in order_of if axis != X_AXIS] for order_of in orders]
    for step in reversed(range(len(back[0]))):
        moved = swap(order.mark(mine), along(back, step))
        yield
        mine = jnp.concatenate([mine, order.after(moved)], axis=0)
    yield mine


def row_steps(order, out_rows, in_rows):
    cores = [swap(send, other_core) for _, send in (out_rows, in_rows)]
    yield
    cores[0] = order.after(cores[0])
    across = swap(order.mark(jnp.stack([out_rows[0][1], cores[0][1], in_rows[0][1], cores[1][1]])), other_x)
    yield
    yield out_rows[0], cores[0], in_rows[0], cores[1], order.after(across)


def per_device(
    global_rows, local_rows, patch_rank, ratio_bin, mask_token, attend_gain, attend_shift, triple_weight,
    pair_bias, output_weight, output_bias, expand_gain, expand_shift, up_weight, up_bias, down_weight,
    down_bias, grad_global, grad_local,
):
    sections, replicas = lax.axis_size("section"), lax.axis_size("dp")
    sz = Sizes(global_rows, local_rows, up_weight, sections, replicas)
    width, rows, hidden = sz.width, sz.rows, sz.hidden
    sets = [rows_of.transpose(0, 2, 1, 3) for rows_of in (global_rows, grad_global)]
    many = [rows_of.transpose(1, 2, 0, 3) for rows_of in (local_rows, grad_local)]
    weights = (triple_weight, output_weight, up_weight, down_weight)
    smalls = (
        patch_rank, mask_token, attend_gain, attend_shift, pair_bias, output_bias, expand_gain, expand_shift, up_bias,
        down_bias,
    )
    wide = ((rows, width), bf16)
    triple_rows = ((rows, 3 * width), bf16)
    hidden_rows = ((rows, hidden), bf16)
    lse = ((16, up_to(max(length for _, length in sz.windows), LANES)), f32)
    flags = ((rows, LANES), f32)
    wide_f32 = ((rows, width), f32)
    turned = ((width, rows), bf16)
    small = ((sz.small_rows, LANES), f32)
    share = ((2, sz.extra, LANES), bf16)
    stage = ((sections, sz.extra, LANES), bf16)
    windows = [((length, length), f32) for _, length in sz.windows]
    totals = [sz.packed(full) for full in (sz.expand_full, sz.attend_full)]
    packs = [((sections, total, LANES), bf16) for total in totals]
    parts = [((2 * total, LANES), bf16) for total in totals]
    vectors = ((2, width), bf16)
    blocks = [(weight.shape[1:], bf16) for weight in weights]
    shared = [wide_f32, turned, turned]

    def run_kernel(body, name, outs, scratch, args):
        return call(
            lambda *refs: body(sz, *refs), name, [out + (VMEM,) for out in outs], [VMEM] * len(args), scratch, args, 4 << 30
        )

    (
        s0, s1, s2, s3, n0, n1, n2, qkv0, qkv1, lse0, lse1, ctx0, ctx1, act0, act1, slope0, masked, grad,
        triple0, triple1, output0, output1, up0, down0, down1, gain_a, gain_e, down_b, keep, send,
    ) = call(
        lambda *refs: front_kernel(sz, *refs),
        "front",
        [
            out + (VMEM,)
            for out in [wide] * 7 + [triple_rows] * 2 + [lse] * 2 + [wide] * 2 + [hidden_rows] * 3 + [flags, wide]
            + [blocks[0]] * 2 + [blocks[1]] * 2 + [blocks[2]] + [blocks[3]] * 2 + [vectors] * 3 + [parts[0]] * 2
        ],
        [HBM] * 14 + [SMEM] + [HBM] * 4,
        [blocks[2]]
        + [(one.shape, one.dtype) for one in (patch_rank, mask_token, attend_shift, pair_bias, output_bias)]
        + [(one.shape, one.dtype) for one in (expand_shift, up_bias)]
        + [(sets[0].shape[1:], bf16), ((sz.locals,) + many[0].shape[1:], bf16)] * 2
        + [wide, hidden_rows, wide_f32] + windows + [turned] * 2 + [packs[0], small, wide, DMA((22,))],
        (sets[0], many[0], sets[1], many[1], *smalls, ratio_bin, *weights),
        8 << 30,
    )
    order = Sequence()
    chains, results = {}, {}
    chains["A"] = reduce_steps(sz, sz.orders["A"], order, keep, send)
    core_scratch = [wide] + windows
    flow = {"grad": grad}

    def core_kernel(name, output, qkv, lse_of):
        proj, = run_kernel(
            attend_core_kernel, name, [triple_rows], core_scratch, (order.after(flow["grad"]), output, qkv, lse_of)
        )
        flow["proj"] = order.mark(proj)

    def later_core():
        core_kernel("later_core", output1, qkv1, lse1)

    def later_attend():
        dh, keep, send = run_kernel(
            lambda sz, *refs: attend_kernel(sz, 1, *refs), "later_attend", [wide] + [parts[1]] * 2,
            shared + [packs[1], small],
            (s2, n2, flow["grad"], ctx1, order.after(flow["proj"]), triple1, gain_a, masked),
        )
        flow["grad"] = order.mark(dh)
        chains["B"] = reduce_steps(sz, sz.orders["B"], order, keep, send)

    def expand():
        dh, keep, send = run_kernel(
            expand_kernel, "expand_back", [wide] + [parts[0]] * 2, shared + [packs[0], small],
            (s1, n1, order.after(flow["grad"]), act0, slope0, up0, down0, gain_e),
        )
        flow["grad"] = order.mark(dh)
        chains["C"] = reduce_steps(sz, sz.orders["C"], order, keep, send)

    def core():
        core_kernel("attend_core", output0, qkv0, lse0)

    def attend():
        in_keep, in_send, keep, send = run_kernel(
            lambda sz, *refs: attend_kernel(sz, 0, *refs), "attend_back", [share] * 2 + [parts[1]] * 2,
            shared + [packs[1], small],
            (s0, n0, flow["grad"], ctx0, order.after(flow["proj"]), triple0, gain_a, masked),
        )
        flow["in"] = (order.mark(in_keep), in_send)
        chains["D"] = reduce_steps(sz, sz.orders["D"], order, keep, send)

    def output_rows():
        out_rows = run_kernel(
            output_kernel, "output_rows", [share] * 2, [turned, turned], (s3, order.after(act1), down1, down_b)
        )
        order.mark(out_rows[0])
        chains["R"] = row_steps(order, out_rows, flow["in"])

    kernels = {
        "later_core": later_core, "later_attend": later_attend, "expand": expand, "core": core, "attend": attend,
        "output": output_rows,
    }
    for plan in PLAN:
        for step in plan.split():
            if step in kernels:
                kernels[step]()
            else:
                results[step] = next(chains[step], results.get(step))
    for _ in sz.rest:
        for step in "ABCD":
            results[step] = next(chains[step], results.get(step))
    cut = sz.cut
    outs = [(sz.all_globals, cut, sz.global_len), local_rows.shape[1:3] + (sz.images, cut)] * 2 + [
        (1, cut), (2, cut), (2, cut), (2, cut, 3 * width), (2, 2 * cut), (2, cut, width), (2, cut), (2, cut), (2, cut),
        (2, cut, hidden), (2, sz.hidden_cut), (2, sz.hidden_cut, width), (2, cut),
    ]
    final = call(
        lambda *refs: finish_kernel(sz, *refs),
        "finish",
        [(shape, f32, VMEM) for shape in outs],
        [VMEM] * 9,
        [((total, LANES), bf16) for total in totals * 2] + [small, flags],
        (*(results[step] for step in "ABCD"), *results["R"]),
        1 << 28,
    )
    shape = global_rows.shape[:2] + (cut, sz.global_len)
    return (
        final[0].reshape(shape).transpose(0, 1, 3, 2),
        final[1].transpose(2, 0, 1, 3),
        final[2].reshape(shape).transpose(0, 1, 3, 2),
        final[3].transpose(2, 0, 1, 3),
        *final[4:],
    )


def solution(mesh):
    rows, copied = P("dp", None, None, None), P()
    in_specs = (rows, rows, P("dp", None, None), P("dp")) + (copied,) * 13 + (rows, rows)
    wide, flat, deep = P("dp", None, None, "section"), P(None, "section"), P(None, "section", None)
    out_specs = (
        wide, wide, wide, wide, flat, flat, flat, deep, flat, deep, flat, flat, flat, deep, flat, deep, flat,
    )
    return jax.shard_map(per_device, mesh=mesh, in_specs=in_specs, out_specs=out_specs, check_vma=False)
```

```python
import math

import jax
import jax.numpy as jnp
from jax import lax
from jax.experimental import pallas as pl
from jax.experimental.pallas import tpu as pltpu
from jax.sharding import PartitionSpec as P

HEADS = 6
EPS = 1e-06
LANES = 128
VMEM_MIB = {"front": 26, "finish": 20}
CHOICES = (0, 0, 1, 0)
PLAN = (
    "A later_core later_attend A expand core",
    "C B A C B attend",
    "D D A B C output R",
    "A B D C B A C D B",
    "A D C R B D C R A",
    "D C B D A B R early C D",
)
X_AXIS = -1

f32 = jnp.float32
bf16 = jnp.bfloat16


def up_to(value, step):
    return (value + step - 1) // step * step


class Sizes:
    def __init__(self, global_rows, local_rows, up_weight, sections, replicas):
        images, crops, self.global_len, self.width = global_rows.shape
        _, local_crops, self.local_len, _ = local_rows.shape
        self.hidden = up_weight.shape[2]
        self.sections = sections
        self.replicas = replicas
        self.images = images
        self.all_globals = images * crops
        self.all_locals = images * local_crops
        self.locals = self.all_locals // sections
        self.used = self.global_len + self.locals * self.local_len
        self.rows = up_to(self.used, LANES)
        self.head = self.width // HEADS
        self.cut = self.width // sections
        self.hidden_cut = self.hidden // sections
        self.tiles = self.width // LANES
        self.first_end = up_to(self.global_len, 16)
        self.second_start = self.global_len // 16 * 16
        self.windows = (
            (0, self.first_end),
            (self.second_start, self.rows - self.second_start),
        )
        self.attend_full = 4 * self.tiles * self.cut
        self.expand_full = self.hidden // LANES * self.cut + self.tiles * self.hidden_cut
        self.small_rows = up_to(max(6 * self.tiles, 3 * self.tiles + self.hidden // LANES), 16)
        self.extra = self.cut * self.rows // LANES
        bits = replicas.bit_length() - 1
        low = list(range(min(bits, 2)))
        last_first = low[1:] + [X_AXIS] + low[:1]
        first_last = [X_AXIS] + low
        middle = low[:1] + [X_AXIS] + low[1:]
        choices = (
            (first_last, last_first), (middle, last_first), (first_last, middle), ([X_AXIS] + low[1:], low[1:] + [X_AXIS])
        )
        self.exchanges = {name: Exchange(choices[choice], bits) for name, choice in zip("ABCD", CHOICES)}
        self.unit = 16 << len(low)

    def packed(self, full):
        return up_to(full + self.small_rows, self.unit)


class Exchange:
    def __init__(self, orders, bits):
        self.orders = orders
        self.axes = sorted(axis for axis in orders[0] if axis != X_AXIS)
        self.rest = [axis for axis in range(bits) if axis not in self.axes]
        self.shards = 1 << len(self.axes)

    def shard_of(self, replica):
        return sum((replica >> axis & 1) << i for i, axis in enumerate(self.axes))

    def place(self, core, across, offset):
        order = self.orders[core]
        return sum(
            (across if axis == X_AXIS else offset >> self.axes.index(axis) & 1) << (len(order) - 1 - at)
            for at, axis in enumerate(order)
        )

    def offset(self, core, place):
        order = [axis for axis in self.orders[core] if axis != X_AXIS]
        return sum((place >> (len(order) - 1 - at) & 1) << self.axes.index(axis) for at, axis in enumerate(order))


def dot(a, b):
    return jnp.dot(a, b, preferred_element_type=f32)


def dot_last(a, b):
    return lax.dot_general(a, b, (((1,), (1,)), ((), ())), preferred_element_type=f32)


def dot_first(a, b):
    return lax.dot_general(a, b, (((0,), (0,)), ((), ())), preferred_element_type=f32)


def normalize(hidden):
    average = jnp.mean(hidden, axis=-1, keepdims=True)
    centred = hidden - average
    inverse = lax.rsqrt(jnp.mean(centred * centred, axis=-1, keepdims=True) + EPS)
    return centred * inverse, inverse


def row_blocks(sz):
    return [slice(i, i + LANES) for i in range(0, sz.rows, LANES)]


def head_mask(sz, rows, which):
    lane = lax.broadcasted_iota(jnp.int32, (rows, 2 * sz.head), 1)
    return lane < sz.head if which == 0 else lane >= sz.head


def window_bias(sz, which):
    start, length = sz.windows[which]

    def group(row):
        if which == 0:
            return jnp.where(row < sz.global_len, 0, 1)
        kind = jnp.where(row + start < sz.global_len, 0, 1)
        for crop in range(1, sz.locals + 1):
            kind = kind + jnp.where(row + start >= sz.global_len + crop * sz.local_len, 1, 0)
        return kind

    left = group(lax.broadcasted_iota(jnp.int32, (length, length), 0))
    right = group(lax.broadcasted_iota(jnp.int32, (length, length), 1))
    return jnp.where(left == right, 0.0, -1e30).astype(f32)


def own_rows(sz, which):
    start, length = sz.windows[which]
    row = lax.broadcasted_iota(jnp.int32, (length, 1), 0) + start
    return row < sz.global_len if which == 0 else row >= sz.global_len


def store_window(sz, which, ref, columns, value):
    start, length = sz.windows[which]
    if which == 0 or sz.first_end == start:
        ref[start : start + length, columns] = value.astype(bf16)
        return
    shared = sz.first_end - start
    row = lax.broadcasted_iota(jnp.int32, (shared, value.shape[1]), 0) + start
    before = ref[start : sz.first_end, columns].astype(f32)
    ref[start : sz.first_end, columns] = jnp.where(
        row < sz.global_len, before, value[:shared]
    ).astype(bf16)
    ref[sz.first_end : start + length, columns] = value[shared:].astype(bf16)


def norm_rows(sz, h_ref, gain, shift, normed_ref):
    for rows in row_blocks(sz):
        scaled, _ = normalize(h_ref[rows, :].astype(f32))
        normed_ref[rows, :] = (scaled * gain + shift).astype(bf16)


def stacked_heads(sz, value):
    zero = jnp.zeros_like(value)
    return jnp.concatenate([jnp.where(head_mask(sz, value.shape[0], which), value, zero) for which in range(2)], axis=0)


def attend_forward(sz, h_ref, weights, out_ref, normed_ref, qkv_ref, lse_ref, ctx_ref, bias_refs):
    gain, shift, triple_ref, pair_bias, output_ref, output_bias = weights
    width = sz.width
    norm_rows(sz, h_ref, gain, shift, normed_ref)
    scale = 1.0 / math.sqrt(sz.head)
    for part in range(3):
        columns = slice(part * width, (part + 1) * width)
        project = dot(normed_ref[...], triple_ref[:, columns])
        if part == 0:
            project = (project + pair_bias[:, :width]) * scale
        if part == 2:
            project = project + pair_bias[:, width:]
        qkv_ref[:, columns] = project.astype(bf16)
    for which, (start, length) in enumerate(sz.windows):
        rows = slice(start, start + length)
        bias = bias_refs[which]
        lane = lax.broadcasted_iota(jnp.int32, (length, LANES), 1)
        first = head_mask(sz, length, 0)
        kept = jnp.zeros((length, LANES), f32)
        for pair in range(HEADS // 2):
            at = 2 * sz.head * pair
            queries, keys, values = (
                qkv_ref[rows, part * width + at : part * width + at + 2 * sz.head] for part in range(3)
            )
            scores = dot_last(stacked_heads(sz, queries), keys)
            probs = []
            for which_head in range(2):
                own = scores[which_head * length : (which_head + 1) * length] + bias[...]
                top = jnp.max(own, axis=-1, keepdims=True)
                raised = jnp.exp(own - top)
                total = jnp.sum(raised, axis=-1, keepdims=True)
                kept = jnp.where(lane == 2 * pair + which_head, top + jnp.log(total), kept)
                probs.append((raised * (1.0 / total)).astype(bf16))
            context = dot(jnp.concatenate(probs, axis=0), values)
            store_window(
                sz, which, ctx_ref, slice(at, at + 2 * sz.head), jnp.where(first, context[:length], context[length:])
            )
        lse_ref[8 * which : 8 * which + 8, :length] = kept.T[:8]
    moved = dot(ctx_ref[...], output_ref[...]) + output_bias
    out_ref[...] = (h_ref[...].astype(f32) + moved).astype(bf16)


def expand_hidden(sz, h_ref, weights, normed_ref, active_ref, slope_ref):
    gain, shift, up_ref, up_bias = weights
    norm_rows(sz, h_ref, gain, shift, normed_ref)
    for at in range(0, sz.hidden, sz.hidden_cut):
        columns = slice(at, at + sz.hidden_cut)
        before = dot(normed_ref[...], up_ref[:, columns]) + up_bias[:, columns]
        share = 0.5 + 0.5 * lax.erf(before * math.sqrt(0.5))
        active_ref[:, columns] = (before * share).astype(bf16)
        density = jnp.exp(before * before * -0.5) * (1.0 / math.sqrt(2.0 * math.pi))
        slope_ref[:, columns] = (share + before * density).astype(bf16)


def expand_output(h_ref, active_ref, down_ref, down_bias):
    return h_ref[...].astype(f32) + dot(active_ref[...], down_ref[...]) + down_bias


def turned_blocks(sz, value, me, turned_ref, blocks_ref):
    turned_ref[...] = value.T
    for j in range(sz.sections):
        source = pl.multiple_of((me ^ j) * sz.cut, sz.cut)
        blocks_ref[j * sz.cut : (j + 1) * sz.cut, :] = turned_ref[pl.ds(source, sz.cut), :]


def put_vector(small, at, vector):
    for tile in range(vector.shape[1] // LANES):
        small[at + tile : at + tile + 1, :] = vector[:, tile * LANES : (tile + 1) * LANES]
    return at + vector.shape[1] // LANES


def put_tiles(pack, j, at, value):
    r = value.shape[0]
    for tile in range(value.shape[1] // LANES):
        pack[j, pl.ds(at + tile * r, r), :] = value[:, tile * LANES : (tile + 1) * LANES].astype(bf16)


def norm_backward(sz, h_ref, grad_ref, grad_normed_ref, gain, dh_ref):
    gain_sum = jnp.zeros((1, sz.width), f32)
    shift_sum = jnp.zeros((1, sz.width), f32)
    for rows in row_blocks(sz):
        scaled, inverse = normalize(h_ref[rows, :].astype(f32))
        grad_normed = grad_normed_ref[rows, :]
        grad_scaled = grad_normed * gain
        first = jnp.mean(grad_scaled, axis=-1, keepdims=True)
        second = jnp.mean(grad_scaled * scaled, axis=-1, keepdims=True)
        grad_in = inverse * (grad_scaled - first - scaled * second)
        dh_ref[rows, :] = (grad_ref[rows, :].astype(f32) + grad_in).astype(dh_ref.dtype)
        gain_sum += jnp.sum(grad_normed * scaled, axis=0, keepdims=True)
        shift_sum += jnp.sum(grad_normed, axis=0, keepdims=True)
    return gain_sum, shift_sum


def expand_backward(sz, me, h_ref, normed, grad_ref, act_ref, slope_ref, gain, up, down, dh_ref, scratch, pack, small):
    total, turned, blocks = scratch
    base = 0
    part = sz.hidden_cut
    up_rows = sz.hidden // LANES * sz.cut
    turned_blocks(sz, normed[...], me, turned, blocks)
    after = 2 * sz.tiles
    for j in range(sz.sections):
        owner = me ^ j
        columns = pl.ds(pl.multiple_of(owner * part, LANES), part)
        put_tiles(pack, j, base + up_rows, dot_first(act_ref[:, columns], grad_ref[...]))
        grad_active = dot_last(grad_ref[...], down[columns, :])
        grad_before = (grad_active * slope_ref[:, columns].astype(f32)).astype(bf16)
        up_sum = jnp.sum(grad_before.astype(f32), axis=0, keepdims=True)
        for tile in range(part // LANES):
            small[pl.ds(after + owner * (part // LANES) + tile, 1), :] = up_sum[:, tile * LANES : (tile + 1) * LANES]
        up_grad = dot(blocks[...], grad_before)
        at = base + pl.multiple_of(owner * (part // LANES * sz.cut), 16)
        for other in range(sz.sections):
            put_tiles(pack, other, at, up_grad[other * sz.cut : (other + 1) * sz.cut, :])
        more = dot_last(grad_before, up[:, columns])
        if j == 0:
            total[...] = more
        else:
            total[...] += more
    gain_sum, shift_sum = norm_backward(sz, h_ref, grad_ref, total, gain, dh_ref)
    put_vector(small, 0, gain_sum)
    put_vector(small, sz.tiles, shift_sum)
    put_vector(
        small, after + sz.hidden // LANES, jnp.sum(grad_ref[...].astype(f32), axis=0, keepdims=True)
    )


def attend_core_backward(sz, grad_ref, output, qkv_ref, lse_ref, proj, dctx, bias_refs):
    width = sz.width
    dctx[...] = dot_last(grad_ref[...], output[...]).astype(bf16)
    scale = 1.0 / math.sqrt(sz.head)
    for which, (start, length) in enumerate(sz.windows):
        rows = slice(start, start + length)
        bias = bias_refs[which]
        own = own_rows(sz, which)
        for pair in range(HEADS // 2):
            at = 2 * sz.head * pair
            columns = [slice(part * width + at, part * width + at + 2 * sz.head) for part in range(3)]
            queries, keys, values = (qkv_ref[rows, c] for c in columns)
            grad_ctx = jnp.where(own, dctx[rows, columns[0]], jnp.zeros((length, 2 * sz.head), bf16))
            keys = stacked_heads(sz, keys)
            scores = dot_last(keys, queries)
            grad_probs = dot_last(stacked_heads(sz, values), grad_ctx)
            probs, grad_scores = [], []
            for which_head in range(2):
                part = slice(which_head * length, (which_head + 1) * length)
                row = 8 * which + 2 * pair + which_head
                prob = jnp.exp(scores[part] + bias[...] - lse_ref[row : row + 1, :length])
                grad_prob = grad_probs[part]
                delta = jnp.sum(prob * grad_prob, axis=0, keepdims=True)
                grad_scores.append((prob * (grad_prob - delta)).astype(bf16))
                probs.append(prob.astype(bf16))
            grad_scores = jnp.concatenate(grad_scores, axis=0)
            first = head_mask(sz, length, 0)
            grad_keys = dot(grad_scores, queries)
            grad_values = dot(jnp.concatenate(probs, axis=0), grad_ctx)
            store_window(sz, which, proj, columns[0], dot_first(grad_scores, keys) * scale)
            store_window(sz, which, proj, columns[1], jnp.where(first, grad_keys[:length], grad_keys[length:]))
            store_window(sz, which, proj, columns[2], jnp.where(first, grad_values[:length], grad_values[length:]))


def attend_backward(sz, me, h_ref, normed, grad_ref, ctx_ref, proj, gain, triple, dh_ref, scratch, pack, small):
    total, turned, blocks = scratch
    width = sz.width
    grad = grad_ref[...]
    out_rows = 3 * sz.tiles * sz.cut
    turned_blocks(sz, ctx_ref[...], me, turned, blocks)
    output_grad = dot(blocks[...], grad)
    for j in range(sz.sections):
        put_tiles(pack, j, out_rows, output_grad[j * sz.cut : (j + 1) * sz.cut, :])
    turned_blocks(sz, normed[...], me, turned, blocks)
    after = 2 * sz.tiles
    for part in range(3):
        columns = slice(part * width, (part + 1) * width)
        grad_part = proj[:, columns]
        triple_grad = dot(blocks[...], grad_part)
        for j in range(sz.sections):
            put_tiles(pack, j, part * sz.tiles * sz.cut, triple_grad[j * sz.cut : (j + 1) * sz.cut, :])
        if part != 1:
            after = put_vector(small, after, jnp.sum(grad_part.astype(f32), axis=0, keepdims=True))
    total[...] = dot_last(proj[...], triple[...])
    gain_sum, shift_sum = norm_backward(sz, h_ref, grad_ref, total, gain, dh_ref)
    put_vector(small, 0, gain_sum)
    put_vector(small, sz.tiles, shift_sum)
    return put_vector(small, after, jnp.sum(grad.astype(f32), axis=0, keepdims=True))


def put_rows(sz, value, me, turned, blocks, keep, send):
    turned_blocks(sz, value, me, turned, blocks)
    for j in range(sz.sections):
        for tile in range(sz.rows // LANES):
            (keep, send)[j % 2][j // 2, tile * sz.cut : (tile + 1) * sz.cut, :] = blocks[
                j * sz.cut : (j + 1) * sz.cut, tile * LANES : (tile + 1) * LANES
            ]


def ship(exchange, me, replica, pack, rows, keep, send):
    size = rows // exchange.shards
    for shard in range(exchange.shards):
        offset = exchange.shard_of(replica) ^ shard
        for core in range(2):
            for across in range(2):
                options = [exchange.place(c, across, offset) for c in range(2)]
                place = jnp.where(me & 1 ^ core == 0, options[0], options[1])
                target = (keep, send)[core]
                target[pl.ds(pl.multiple_of(place * size, 16), size), :] = pack[
                    2 * across + core, shard * size : (shard + 1) * size, :
                ]


def put_small(pack, start, rows, small):
    held = small.shape[0]
    for j in range(pack.shape[0]):
        pack[j, start : start + held, :] = small[...].astype(bf16)
        if start + held < rows:
            pack[j, start + held : rows, :] = jnp.zeros((rows - start - held, LANES), bf16)


class Moves:
    def __init__(self, pairs, sems):
        self.copies = [pltpu.make_async_copy(source, target, sems.at[i]) for i, (source, target) in enumerate(pairs)]

    def start(self, *which):
        for i in which:
            self.copies[i].start()

    def wait(self, *which):
        for i in which:
            self.copies[i].wait()


def row_of(ref, layer):
    return ref[layer : layer + 1, :].astype(f32)


def pick_row(block, which):
    value = block[:, 0, :].astype(f32)
    for other in range(1, block.shape[1]):
        value = jnp.where(which == other, block[:, other, :].astype(f32), value)
    return value


def gather_rows(sz, of_global, of_local, crop, image, wide):
    wide[: sz.global_len, :] = pick_row(of_global, crop)
    for at in range(sz.locals):
        start = sz.global_len + at * sz.local_len
        wide[start : start + sz.local_len, :] = pick_row(of_local.at[at], image)
    wide[sz.used :, :] = jnp.zeros((sz.rows - sz.used, sz.width), f32)


def front_kernel(sz, *refs):
    rows_in, smalls_in, ratio_ref, weights_in, refs = refs[:4], refs[4:14], refs[14], refs[15:19], refs[19:]
    (
        s0, s1, s2, s3, n0, n1, n2, qkv0, qkv1, lse0, lse1, ctx0, ctx1, act0, act1, slope0, masked_ref, grad,
        triple0, triple1, output0, output1, up0, down0, down1, gain_a, gain_e, down_b, keep, send,
    ) = refs[:30]
    (
        up1, rank_ref, token_ref, shift_a, pair, output_b, shift_e, up_b, own_global, own_local, own_global_back,
        own_local_back, n3, slope1, wide, bias0, bias1, turned, blocks, pack, small, first_grad, load_sems,
    ) = refs[30:]
    own = (own_global, own_local, own_global_back, own_local_back)
    smalls = (rank_ref, token_ref, gain_a, shift_a, pair, output_b, gain_e, shift_e, up_b, down_b)
    weights = ((triple0, output0, up0, down0), (triple1, output1, up1, down1))
    me, replica = lax.axis_index("section"), lax.axis_index("dp")
    per_image = sz.sections // sz.images
    image, crop = me // per_image, me % per_image
    several = pl.ds(crop * sz.locals, sz.locals)
    places = [image, several, image, several]
    pairs = [(source.at[place], target) for source, place, target in zip(rows_in, places, own)]
    pairs += list(zip(smalls_in, smalls))
    pairs += [(weights_in[k].at[layer], weights[layer][k]) for layer in range(2) for k in range(4)]
    loads = Moves(pairs, load_sems)
    loads.start(0, 1, *range(4, 16))
    bias0[...] = window_bias(sz, 0)
    bias1[...] = window_bias(sz, 1)
    biases = (bias0, bias1)
    patches = sz.global_len - 1
    loads.wait(0, 1, *range(4, 14))
    loads.start(2, 3, *range(16, 22))
    limit = lax.div((ratio_ref[image] + 1) * patches, jnp.int32(10))
    both = rank_ref[image]
    entry = lax.broadcasted_iota(jnp.int32, both.shape, 0)
    ranks = jnp.sum(jnp.where(entry == crop, both, 0), axis=0, keepdims=True)
    shape = (sz.rows, patches)
    row = lax.broadcasted_iota(jnp.int32, shape, 0)
    column = lax.broadcasted_iota(jnp.int32, shape, 1)
    chosen = jnp.where((row == column + 1) & (ranks < limit), 1.0, 0.0)
    chosen = jnp.max(chosen, axis=-1, keepdims=True)
    masked_ref[...] = jnp.broadcast_to(chosen, masked_ref.shape)
    gather_rows(sz, own[0], own[1], crop, image, wide)
    s0[...] = jnp.where(chosen > 0.5, token_ref[...].astype(f32), wide[...]).astype(bf16)

    def attend_weights(layer):
        triple, output, _, _ = weights[layer]
        return (
            row_of(gain_a, layer), row_of(shift_a, layer), triple, row_of(pair, layer), output, row_of(output_b, layer),
        )

    def expand_weights(layer):
        return row_of(gain_e, layer), row_of(shift_e, layer), weights[layer][2], row_of(up_b, layer)

    loads.wait(14, 15)
    attend_forward(sz, s0, attend_weights(0), s1, n0, qkv0, lse0, ctx0, biases)
    loads.wait(16, 17)
    expand_hidden(sz, s1, expand_weights(0), n1, act0, slope0)
    s2[...] = expand_output(s1, act0, down0, row_of(down_b, 0)).astype(bf16)
    loads.wait(18, 19)
    attend_forward(sz, s2, attend_weights(1), s3, n2, qkv1, lse1, ctx1, biases)
    loads.wait(20, 21)
    expand_hidden(sz, s3, expand_weights(1), n3, act1, slope1)
    loads.wait(2, 3)
    gather_rows(sz, own[2], own[3], crop, image, wide)
    first_grad[...] = wide[...].astype(bf16)
    small[...] = jnp.zeros_like(small)
    expand_backward(
        sz, me, s3, n3, first_grad, act1, slope1, row_of(gain_e, 1), up1, down1, grad, (wide, turned, blocks), pack, small
    )
    rows = sz.packed(sz.expand_full)
    put_small(pack, sz.expand_full, rows, small)
    ship(sz.exchanges["A"], me, replica, pack, rows, keep, send)


def output_kernel(sz, h_ref, act_ref, down, down_b, out_keep, out_send, turned, blocks):
    me = lax.axis_index("section")
    last = expand_output(h_ref, act_ref, down, row_of(down_b, 1)).astype(bf16)
    put_rows(sz, last, me, turned, blocks, out_keep, out_send)


def expand_kernel(sz, h, normed, grad, act, slope, up, down, gain, dh_ref, keep, send, total, turned, blocks, pack, small):
    me, replica = lax.axis_index("section"), lax.axis_index("dp")
    small[...] = jnp.zeros_like(small)
    expand_backward(
        sz, me, h, normed, grad, act, slope, row_of(gain, 0), up, down, dh_ref, (total, turned, blocks), pack, small
    )
    rows = sz.packed(sz.expand_full)
    put_small(pack, sz.expand_full, rows, small)
    ship(sz.exchanges["C"], me, replica, pack, rows, keep, send)


def attend_core_kernel(sz, grad, output, qkv, lse, proj, dctx, bias0, bias1):
    bias0[...] = window_bias(sz, 0)
    bias1[...] = window_bias(sz, 1)
    attend_core_backward(sz, grad, output, qkv, lse, proj, dctx, (bias0, bias1))


def attend_kernel(sz, layer, *refs):
    h, normed, grad, ctx, proj, triple, gain, flags = refs[:8]
    if layer == 0:
        in_keep, in_send, keep, send, total, turned, blocks, pack, small = refs[8:]
        target = total
    else:
        target, keep, send, total, turned, blocks, pack, small = refs[8:]
    me, replica = lax.axis_index("section"), lax.axis_index("dp")
    small[...] = jnp.zeros_like(small)
    rows = sz.packed(sz.attend_full)
    after = attend_backward(
        sz, me, h, normed, grad, ctx, proj, row_of(gain, layer), triple, target, (total, turned, blocks), pack, small
    )
    if layer == 0:
        masked = flags[:, :1] > 0.5
        put_vector(small, after, jnp.sum(jnp.where(masked, total[...], 0.0), axis=0, keepdims=True))
        put_rows(sz, jnp.where(masked, 0.0, total[...]).astype(bf16), me, turned, blocks, in_keep, in_send)
    put_small(pack, sz.attend_full, rows, small)
    ship(sz.exchanges["DB"[layer]], me, replica, pack, rows, keep, send)


def unpack(exchange, me, replica, source, target):
    shard = target.shape[0] // exchange.shards
    for place in range(exchange.shards):
        options = [exchange.offset(core, place) for core in range(2)]
        offset = jnp.where(me & 1 == 0, options[0], options[1])
        at = pl.multiple_of((exchange.shard_of(replica) ^ offset) * shard, 16)
        target[pl.ds(at, shard), :] = source[place * shard : (place + 1) * shard, :]


def widen_tiles(source, base, target):
    r, columns = target.shape
    for tile in range(columns // LANES):
        target[:, tile * LANES : (tile + 1) * LANES] = source[base + tile * r : base + (tile + 1) * r, :].astype(f32)


def widen(sz, attend, expand, targets, moves):
    triple, output, up, down = targets
    hidden_rows = sz.hidden // LANES * sz.cut
    for index, (source, base, target) in enumerate(
        ((expand, 0, up), (expand, hidden_rows, down), (attend, 0, triple), (attend, 3 * sz.tiles * sz.cut, output))
    ):
        widen_tiles(source, base, target)
        moves[(2, 3, 0, 1)[index]].start()


def early_kernel(sz, *refs):
    (expand_in, attend_in), (out_own, out_core, in_own, in_core, across) = refs[:2], refs[2:7]
    (out_global, out_local, in_global, in_local), outs, vectors = refs[7:11], refs[11:15], refs[15]
    expand, attend, targets, wide, sems = refs[16], refs[17], refs[18:22], refs[22], refs[23]
    me, replica = lax.axis_index("section"), lax.axis_index("dp")
    moves = [pltpu.make_async_copy(target, out.at[1], sems.at[i]) for i, (target, out) in enumerate(zip(targets, outs))]
    unpack(sz.exchanges["A"], me, replica, expand_in, expand)
    unpack(sz.exchanges["B"], me, replica, attend_in, attend)
    widen(sz, attend, expand, targets, moves)
    vectors[: sz.small_rows, :] = attend[sz.attend_full : sz.attend_full + sz.small_rows, :].astype(f32)
    vectors[sz.small_rows :, :] = expand[sz.expand_full : sz.expand_full + sz.small_rows, :].astype(f32)
    row_parts = (
        (out_own.at[0], out_core.at[0], across.at[0], across.at[1]),
        (in_own.at[0], in_core.at[0], across.at[2], across.at[3]),
    )
    per_image = sz.sections // sz.images
    for which, (to_global, to_local) in enumerate(((out_global, out_local), (in_global, in_local))):
        for k in range(4):
            section = me ^ k
            image, crop = section // per_image, section % per_image
            turned = jnp.concatenate(
                [
                    row_parts[which][k][tile * sz.cut : (tile + 1) * sz.cut, :].astype(f32)
                    for tile in range(sz.rows // LANES)
                ],
                axis=1,
            )
            to_global[section] = turned[:, : sz.global_len]
            turned = jnp.concatenate([turned, jnp.zeros((LANES - sz.cut, sz.rows), f32)], axis=0)
            wide[...] = turned.T
            for at in range(sz.locals):
                start = sz.global_len + at * sz.local_len
                to_local[crop * sz.locals + at, :, pl.ds(image, 1), :] = wide[
                    start : start + sz.local_len, : sz.cut
                ].reshape(sz.local_len, 1, sz.cut)
    for move in moves:
        move.wait()


def finish_kernel(sz, *refs):
    expand_in, attend_in, later_vectors = refs[:3]
    (token, gain_a, shift_a, pair, output_b, gain_e, shift_e, up_b, down_b), outs = refs[7:16], refs[16:20]
    expand, attend, targets, vectors, sems = refs[20], refs[21], refs[22:26], refs[26], refs[27]
    me, replica = lax.axis_index("section"), lax.axis_index("dp")
    moves = [pltpu.make_async_copy(target, out.at[0], sems.at[i]) for i, (target, out) in enumerate(zip(targets, outs))]
    unpack(sz.exchanges["C"], me, replica, expand_in, expand)
    unpack(sz.exchanges["D"], me, replica, attend_in, attend)
    widen(sz, attend, expand, targets, moves)
    width, tiles, cut = sz.width, sz.tiles, sz.cut
    row = lax.broadcasted_iota(jnp.int32, (width, cut), 0)
    column = lax.broadcasted_iota(jnp.int32, (width, cut), 1)
    pick = jnp.where(row == column + me * cut, 1.0, 0.0).astype(bf16)
    row = lax.broadcasted_iota(jnp.int32, (2 * width, 2 * cut), 0)
    column = lax.broadcasted_iota(jnp.int32, (2 * width, 2 * cut), 1)
    pick_pair = jnp.where(row == column + me * 2 * cut, 1.0, 0.0).astype(bf16)
    hidden_tiles, up_tiles = sz.hidden // LANES, sz.hidden_cut // LANES
    vectors[: sz.small_rows, :] = attend[sz.attend_full : sz.attend_full + sz.small_rows, :].astype(f32)
    vectors[sz.small_rows :, :] = expand[sz.expand_full : sz.expand_full + sz.small_rows, :].astype(f32)
    for layer, held in enumerate((vectors, later_vectors)):
        one = slice(layer, layer + 1)

        def vector(at, tiles_in):
            return jnp.concatenate([held[at + t : at + t + 1, :] for t in range(tiles_in)], axis=1)

        def picked(at):
            return dot(vector(at, tiles).astype(bf16), pick)

        gain_a[one, :] = picked(0)
        shift_a[one, :] = picked(tiles)
        pair[one, :] = dot(vector(2 * tiles, 2 * tiles).astype(bf16), pick_pair)
        output_b[one, :] = picked(4 * tiles)
        if layer == 0:
            token[...] = picked(5 * tiles)
        base = sz.small_rows
        gain_e[one, :] = picked(base)
        shift_e[one, :] = picked(base + tiles)
        for tile in range(up_tiles):
            up_b[one, tile * LANES : (tile + 1) * LANES] = held[pl.ds(base + 2 * tiles + me * up_tiles + tile, 1), :]
        down_b[one, :] = picked(base + 2 * tiles + hidden_tiles)
    for move in moves:
        move.wait()


VMEM = pl.BlockSpec(memory_space=pltpu.VMEM)
ANY = pl.BlockSpec(memory_space=pl.ANY)
HBM = pl.BlockSpec(memory_space=pltpu.HBM)
SMEM = pl.BlockSpec(memory_space=pltpu.SMEM)
DMA = pltpu.SemaphoreType.DMA


def call(body, name, outs, in_specs, scratch, args, flops, aliases=()):
    args = [
        pltpu.with_memory_space_constraint(arg, pltpu.HBM) if spec is HBM else arg for arg, spec in zip(args, in_specs)
    ]
    return pl.pallas_call(
        body,
        name=name,
        out_shape=tuple(jax.ShapeDtypeStruct(shape, kind) for shape, kind, _ in outs),
        in_specs=in_specs,
        out_specs=tuple(memory for _, _, memory in outs),
        scratch_shapes=[pltpu.VMEM(*item) if isinstance(item, tuple) else item for item in scratch],
        input_output_aliases=dict(aliases),
        compiler_params=pltpu.CompilerParams(vmem_limit_bytes=VMEM_MIB.get(name, 14) << 20),
        cost_estimate=pl.CostEstimate(flops=flops, bytes_accessed=1 << 20, transcendentals=0),
    )(*args)


def add(first, *others):
    total = first.astype(f32)
    for other in others:
        total = total + other.astype(f32)
    return lax.reduce_precision(total, 8, 7).astype(bf16)


def swap(value, partner_of):
    sections, replicas = lax.axis_size("section"), lax.axis_size("dp")
    route = []
    for section in range(sections):
        for replica in range(replicas):
            to_section, to_replica = partner_of(section, replica)
            route.append((section * replicas + replica, to_section * replicas + to_replica))
    return lax.ppermute(value, ("section", "dp"), route)


def other_core(section, replica):
    return section ^ 1, replica


def other_x(section, replica):
    return section ^ 2, replica


def along(orders, step):
    def partner_of(section, replica):
        axis = orders[section & 1][step]
        return (section ^ 2, replica) if axis == X_AXIS else (section, replica ^ (1 << axis))

    return partner_of


class Sequence:
    def __init__(self):
        self.last = None

    def after(self, value):
        return value if self.last is None else lax.optimization_barrier((value, self.last))[0]

    def mark(self, value):
        self.last = value
        return value


def reduce_steps(exchange, order, keep, send):
    orders = exchange.orders
    core = swap(send, other_core)
    yield
    core = order.after(core)
    half = keep.shape[0] // 2
    moved = swap(order.mark(add(keep[half:], core[half:])), along(orders, 0))
    yield
    moved = order.after(moved)
    mine = add(keep[:half], core[:half], moved)
    for step in range(1, len(orders[0])):
        half = mine.shape[0] // 2
        moved = swap(order.mark(mine[half:]), along(orders, step))
        yield
        mine = add(mine[:half], order.after(moved))
    for axis in exchange.rest:
        moved = swap(order.mark(mine), along(([axis], [axis]), 0))
        yield
        mine = add(mine, order.after(moved))
    back = [[axis for axis in order_of if axis != X_AXIS] for order_of in orders]
    for step in reversed(range(len(back[0]))):
        moved = swap(order.mark(mine), along(back, step))
        yield
        mine = jnp.concatenate([mine, order.after(moved)], axis=0)
    yield mine


def row_steps(order, out_rows, in_rows):
    cores = [swap(send, other_core) for _, send in (out_rows, in_rows)]
    yield
    cores[0] = order.after(cores[0])
    across = swap(order.mark(jnp.stack([out_rows[0][1], cores[0][1], in_rows[0][1], cores[1][1]])), other_x)
    yield
    yield out_rows[0], cores[0], in_rows[0], cores[1], order.after(across)


def per_device(
    global_rows, local_rows, patch_rank, ratio_bin, mask_token, attend_gain, attend_shift, triple_weight,
    pair_bias, output_weight, output_bias, expand_gain, expand_shift, up_weight, up_bias, down_weight,
    down_bias, grad_global, grad_local,
):
    sections, replicas = lax.axis_size("section"), lax.axis_size("dp")
    sz = Sizes(global_rows, local_rows, up_weight, sections, replicas)
    width, rows, hidden = sz.width, sz.rows, sz.hidden
    sets = [rows_of.transpose(0, 2, 1, 3) for rows_of in (global_rows, grad_global)]
    many = [rows_of.transpose(1, 2, 0, 3) for rows_of in (local_rows, grad_local)]
    weights = (triple_weight, output_weight, up_weight, down_weight)
    smalls = (
        patch_rank, mask_token, attend_gain, attend_shift, pair_bias, output_bias, expand_gain, expand_shift, up_bias,
        down_bias,
    )
    wide = ((rows, width), bf16)
    triple_rows = ((rows, 3 * width), bf16)
    hidden_rows = ((rows, hidden), bf16)
    lse = ((16, up_to(max(length for _, length in sz.windows), LANES)), f32)
    flags = ((rows, LANES), f32)
    wide_f32 = ((rows, width), f32)
    turned = ((width, rows), bf16)
    small = ((sz.small_rows, LANES), f32)
    share = ((2, sz.extra, LANES), bf16)
    stage = ((sections, sz.extra, LANES), bf16)
    windows = [((length, length), f32) for _, length in sz.windows]
    totals = [sz.packed(full) for full in (sz.expand_full, sz.attend_full)]
    packs = [((sections, total, LANES), bf16) for total in totals]
    parts = [((2 * total, LANES), bf16) for total in totals]
    vectors = ((2, width), bf16)
    blocks = [(weight.shape[1:], bf16) for weight in weights]
    shared = [wide_f32, turned, turned]

    def run_kernel(body, name, outs, scratch, args):
        return call(
            lambda *refs: body(sz, *refs), name, [out + (VMEM,) for out in outs], [VMEM] * len(args), scratch, args, 4 << 30
        )

    (
        s0, s1, s2, s3, n0, n1, n2, qkv0, qkv1, lse0, lse1, ctx0, ctx1, act0, act1, slope0, masked, grad,
        triple0, triple1, output0, output1, up0, down0, down1, gain_a, gain_e, down_b, keep, send,
    ) = call(
        lambda *refs: front_kernel(sz, *refs),
        "front",
        [
            out + (VMEM,)
            for out in [wide] * 7 + [triple_rows] * 2 + [lse] * 2 + [wide] * 2 + [hidden_rows] * 3 + [flags, wide]
            + [blocks[0]] * 2 + [blocks[1]] * 2 + [blocks[2]] + [blocks[3]] * 2 + [vectors] * 3 + [parts[0]] * 2
        ],
        [HBM] * 14 + [SMEM] + [HBM] * 4,
        [blocks[2]]
        + [(one.shape, one.dtype) for one in (patch_rank, mask_token, attend_shift, pair_bias, output_bias)]
        + [(one.shape, one.dtype) for one in (expand_shift, up_bias)]
        + [(sets[0].shape[1:], bf16), ((sz.locals,) + many[0].shape[1:], bf16)] * 2
        + [wide, hidden_rows, wide_f32] + windows + [turned] * 2 + [packs[0], small, wide, DMA((22,))],
        (sets[0], many[0], sets[1], many[1], *smalls, ratio_bin, *weights),
        8 << 30,
    )
    order = Sequence()
    chains, results = {}, {}
    chains["A"] = reduce_steps(sz.exchanges["A"], order, keep, send)
    core_scratch = [wide] + windows
    flow = {"grad": grad}

    def core_kernel(name, output, qkv, lse_of):
        proj, = run_kernel(
            attend_core_kernel, name, [triple_rows], core_scratch, (order.after(flow["grad"]), output, qkv, lse_of)
        )
        flow["proj"] = order.mark(proj)

    def later_core():
        core_kernel("later_core", output1, qkv1, lse1)

    def later_attend():
        dh, keep, send = run_kernel(
            lambda sz, *refs: attend_kernel(sz, 1, *refs), "later_attend", [wide] + [parts[1]] * 2,
            shared + [packs[1], small],
            (s2, n2, flow["grad"], ctx1, order.after(flow["proj"]), triple1, gain_a, masked),
        )
        flow["grad"] = order.mark(dh)
        chains["B"] = reduce_steps(sz.exchanges["B"], order, keep, send)

    def expand():
        dh, keep, send = run_kernel(
            expand_kernel, "expand_back", [wide] + [parts[0]] * 2, shared + [packs[0], small],
            (s1, n1, order.after(flow["grad"]), act0, slope0, up0, down0, gain_e),
        )
        flow["grad"] = order.mark(dh)
        chains["C"] = reduce_steps(sz.exchanges["C"], order, keep, send)

    def core():
        core_kernel("attend_core", output0, qkv0, lse0)

    def attend():
        in_keep, in_send, keep, send = run_kernel(
            lambda sz, *refs: attend_kernel(sz, 0, *refs), "attend_back", [share] * 2 + [parts[1]] * 2,
            shared + [packs[1], small],
            (s0, n0, flow["grad"], ctx0, order.after(flow["proj"]), triple0, gain_a, masked),
        )
        flow["in"] = (order.mark(in_keep), in_send)
        chains["D"] = reduce_steps(sz.exchanges["D"], order, keep, send)

    def output_rows():
        out_rows = run_kernel(
            output_kernel, "output_rows", [share] * 2, [turned, turned], (s3, order.after(act1), down1, down_b)
        )
        order.mark(out_rows[0])
        chains["R"] = row_steps(order, out_rows, flow["in"])

    cut = sz.cut
    weight_outs = [(2, cut, 3 * width), (2, cut, width), (2, cut, hidden), (2, sz.hidden_cut, width)]
    row_outs = [(sz.all_globals, cut, sz.global_len), local_rows.shape[1:3] + (sz.images, cut)] * 2
    both_small = ((2 * sz.small_rows, LANES), f32)
    finish_scratch = [((total, LANES), bf16) for total in totals] + [(shape[1:], f32) for shape in weight_outs]

    def early():
        expand_of, attend_of = (order.after(results[step]) for step in "AB")
        flow["early"] = call(
            lambda *refs: early_kernel(sz, *refs), "early",
            [(shape, f32, VMEM) for shape in row_outs] + [(shape, f32, ANY) for shape in weight_outs] + [both_small + (VMEM,)],
            [VMEM] * 7, finish_scratch + [flags, DMA((4,))], (expand_of, attend_of, *results["R"]), 1 << 28,
        )
        order.mark(flow["early"][-1])

    kernels = {
        "later_core": later_core, "later_attend": later_attend, "expand": expand, "core": core, "attend": attend,
        "output": output_rows, "early": early,
    }
    for plan in PLAN:
        for step in plan.split():
            if step == "early":
                for _ in range(3, len(sz.exchanges["A"].rest) + len(sz.exchanges["A"].axes)):
                    for name in "ABCD":
                        results[name] = next(chains[name], results.get(name))
            if step in kernels:
                kernels[step]()
            else:
                results[step] = next(chains[step], results.get(step))
    *row_values, triple, output, up, down, late_vectors = flow["early"]
    vector_outs = [(1, cut), (2, cut), (2, cut), (2, 2 * cut)] + [(2, cut)] * 3 + [(2, sz.hidden_cut), (2, cut)]
    final = call(
        lambda *refs: finish_kernel(sz, *refs), "finish",
        [(shape, f32, VMEM) for shape in vector_outs] + [(shape, f32, ANY) for shape in weight_outs],
        [VMEM] * 3 + [ANY] * 4, finish_scratch + [both_small, DMA((4,))],
        (order.after(results["C"]), results["D"], late_vectors, triple, output, up, down), 1 << 28,
        [(3 + i, len(vector_outs) + i) for i in range(4)],
    )
    token, gain_a, shift_a, pair, output_b, gain_e, shift_e, up_b, down_b, triple, output, up, down = final
    shape = global_rows.shape[:2] + (cut, sz.global_len)
    return (
        row_values[0].reshape(shape).transpose(0, 1, 3, 2), row_values[1].transpose(2, 0, 1, 3),
        row_values[2].reshape(shape).transpose(0, 1, 3, 2), row_values[3].transpose(2, 0, 1, 3),
        token, gain_a, shift_a, triple, pair, output, output_b, gain_e, shift_e, up, up_b, down, down_b,
    )


def solution(mesh):
    rows, copied = P("dp", None, None, None), P()
    in_specs = (rows, rows, P("dp", None, None), P("dp")) + (copied,) * 13 + (rows, rows)
    wide, flat, deep = P("dp", None, None, "section"), P(None, "section"), P(None, "section", None)
    out_specs = (
        wide, wide, wide, wide, flat, flat, flat, deep, flat, deep, flat, flat, flat, deep, flat, deep, flat,
    )
    return jax.shard_map(per_device, mesh=mesh, in_specs=in_specs, out_specs=out_specs, check_vma=False)
```

```python
import math

import jax
import jax.numpy as jnp
from jax import lax
from jax.experimental import pallas as pl
from jax.experimental.pallas import tpu as pltpu
from jax.sharding import PartitionSpec as P

HEADS = 6
EPS = 1e-06
LANES = 128
VMEM_MIB = {"front": 26, "finish": 20}
CHOICES = (0, 0, 1, 0)
PLAN = (
    "A later_core later_attend A expand core",
    "C B A C B attend",
    "D C D A B output R",
    "A B D C B A C D B",
    "A D C R B D C R D A",
    "C B D A B R early C D",
)
X_AXIS = -1

f32 = jnp.float32
bf16 = jnp.bfloat16


def up_to(value, step):
    return (value + step - 1) // step * step


class Sizes:
    def __init__(self, global_rows, local_rows, up_weight, sections, replicas):
        images, crops, self.global_len, self.width = global_rows.shape
        _, local_crops, self.local_len, _ = local_rows.shape
        self.hidden = up_weight.shape[2]
        self.sections = sections
        self.replicas = replicas
        self.images = images
        self.all_globals = images * crops
        self.all_locals = images * local_crops
        self.locals = self.all_locals // sections
        self.used = self.global_len + self.locals * self.local_len
        self.rows = up_to(self.used, LANES)
        self.head = self.width // HEADS
        self.cut = self.width // sections
        self.hidden_cut = self.hidden // sections
        self.tiles = self.width // LANES
        self.first_end = up_to(self.global_len, 16)
        self.second_start = self.global_len // 16 * 16
        self.windows = (
            (0, self.first_end),
            (self.second_start, self.rows - self.second_start),
        )
        self.attend_full = 4 * self.tiles * self.cut
        self.expand_full = self.hidden // LANES * self.cut + self.tiles * self.hidden_cut
        self.small_rows = up_to(max(6 * self.tiles, 3 * self.tiles + self.hidden // LANES), 16)
        self.extra = self.cut * self.rows // LANES
        bits = replicas.bit_length() - 1
        low = list(range(min(bits, 2)))
        last_first = low[1:] + [X_AXIS] + low[:1]
        first_last = [X_AXIS] + low
        middle = low[:1] + [X_AXIS] + low[1:]
        choices = (
            (first_last, last_first), (middle, last_first), (first_last, middle), ([X_AXIS] + low[1:], low[1:] + [X_AXIS])
        )
        self.exchanges = {name: Exchange(choices[choice], bits) for name, choice in zip("ABCD", CHOICES)}
        self.unit = 16 << len(low)

    def packed(self, full):
        return up_to(full + self.small_rows, self.unit)


class Exchange:
    def __init__(self, orders, bits):
        self.orders = orders
        self.axes = sorted(axis for axis in orders[0] if axis != X_AXIS)
        self.rest = [axis for axis in range(bits) if axis not in self.axes]
        self.shards = 1 << len(self.axes)

    def shard_of(self, replica):
        return sum((replica >> axis & 1) << i for i, axis in enumerate(self.axes))

    def place(self, core, across, offset):
        order = self.orders[core]
        return sum(
            (across if axis == X_AXIS else offset >> self.axes.index(axis) & 1) << (len(order) - 1 - at)
            for at, axis in enumerate(order)
        )

    def offset(self, core, place):
        order = [axis for axis in self.orders[core] if axis != X_AXIS]
        return sum((place >> (len(order) - 1 - at) & 1) << self.axes.index(axis) for at, axis in enumerate(order))


def dot(a, b):
    return jnp.dot(a, b, preferred_element_type=f32)


def dot_last(a, b):
    return lax.dot_general(a, b, (((1,), (1,)), ((), ())), preferred_element_type=f32)


def dot_first(a, b):
    return lax.dot_general(a, b, (((0,), (0,)), ((), ())), preferred_element_type=f32)


def normalize(hidden):
    average = jnp.mean(hidden, axis=-1, keepdims=True)
    centred = hidden - average
    inverse = lax.rsqrt(jnp.mean(centred * centred, axis=-1, keepdims=True) + EPS)
    return centred * inverse, inverse


def row_blocks(sz):
    return [slice(i, i + LANES) for i in range(0, sz.rows, LANES)]


def head_mask(sz, rows, which):
    lane = lax.broadcasted_iota(jnp.int32, (rows, 2 * sz.head), 1)
    return lane < sz.head if which == 0 else lane >= sz.head


def window_bias(sz, which):
    start, length = sz.windows[which]

    def group(row):
        if which == 0:
            return jnp.where(row < sz.global_len, 0, 1)
        kind = jnp.where(row + start < sz.global_len, 0, 1)
        for crop in range(1, sz.locals + 1):
            kind = kind + jnp.where(row + start >= sz.global_len + crop * sz.local_len, 1, 0)
        return kind

    left = group(lax.broadcasted_iota(jnp.int32, (length, length), 0))
    right = group(lax.broadcasted_iota(jnp.int32, (length, length), 1))
    return jnp.where(left == right, 0.0, -1e30).astype(f32)


def own_rows(sz, which):
    start, length = sz.windows[which]
    row = lax.broadcasted_iota(jnp.int32, (length, 1), 0) + start
    return row < sz.global_len if which == 0 else row >= sz.global_len


def store_window(sz, which, ref, columns, value):
    start, length = sz.windows[which]
    if which == 0 or sz.first_end == start:
        ref[start : start + length, columns] = value.astype(bf16)
        return
    shared = sz.first_end - start
    row = lax.broadcasted_iota(jnp.int32, (shared, value.shape[1]), 0) + start
    before = ref[start : sz.first_end, columns].astype(f32)
    ref[start : sz.first_end, columns] = jnp.where(
        row < sz.global_len, before, value[:shared]
    ).astype(bf16)
    ref[sz.first_end : start + length, columns] = value[shared:].astype(bf16)


def norm_rows(sz, h_ref, gain, shift, normed_ref):
    for rows in row_blocks(sz):
        scaled, _ = normalize(h_ref[rows, :].astype(f32))
        normed_ref[rows, :] = (scaled * gain + shift).astype(bf16)


def stacked_heads(sz, value):
    zero = jnp.zeros_like(value)
    return jnp.concatenate([jnp.where(head_mask(sz, value.shape[0], which), value, zero) for which in range(2)], axis=0)


def attend_forward(sz, h_ref, weights, out_ref, normed_ref, qkv_ref, lse_ref, ctx_ref, bias_refs):
    gain, shift, triple_ref, pair_bias, output_ref, output_bias = weights
    width = sz.width
    norm_rows(sz, h_ref, gain, shift, normed_ref)
    scale = 1.0 / math.sqrt(sz.head)
    for part in range(3):
        columns = slice(part * width, (part + 1) * width)
        project = dot(normed_ref[...], triple_ref[:, columns])
        if part == 0:
            project = (project + pair_bias[:, :width]) * scale
        if part == 2:
            project = project + pair_bias[:, width:]
        qkv_ref[:, columns] = project.astype(bf16)
    for which, (start, length) in enumerate(sz.windows):
        rows = slice(start, start + length)
        bias = bias_refs[which]
        lane = lax.broadcasted_iota(jnp.int32, (length, LANES), 1)
        first = head_mask(sz, length, 0)
        kept = jnp.zeros((length, LANES), f32)
        for pair in range(HEADS // 2):
            at = 2 * sz.head * pair
            queries, keys, values = (
                qkv_ref[rows, part * width + at : part * width + at + 2 * sz.head] for part in range(3)
            )
            scores = dot_last(stacked_heads(sz, queries), keys)
            probs = []
            for which_head in range(2):
                own = scores[which_head * length : (which_head + 1) * length] + bias[...]
                top = jnp.max(own, axis=-1, keepdims=True)
                raised = jnp.exp(own - top)
                total = jnp.sum(raised, axis=-1, keepdims=True)
                kept = jnp.where(lane == 2 * pair + which_head, top + jnp.log(total), kept)
                probs.append((raised * (1.0 / total)).astype(bf16))
            context = dot(jnp.concatenate(probs, axis=0), values)
            store_window(
                sz, which, ctx_ref, slice(at, at + 2 * sz.head), jnp.where(first, context[:length], context[length:])
            )
        lse_ref[8 * which : 8 * which + 8, :length] = kept.T[:8]
    moved = dot(ctx_ref[...], output_ref[...]) + output_bias
    out_ref[...] = (h_ref[...].astype(f32) + moved).astype(bf16)


def expand_hidden(sz, h_ref, weights, normed_ref, active_ref, slope_ref):
    gain, shift, up_ref, up_bias = weights
    norm_rows(sz, h_ref, gain, shift, normed_ref)
    for at in range(0, sz.hidden, sz.hidden_cut):
        columns = slice(at, at + sz.hidden_cut)
        before = dot(normed_ref[...], up_ref[:, columns]) + up_bias[:, columns]
        share = 0.5 + 0.5 * lax.erf(before * math.sqrt(0.5))
        active_ref[:, columns] = (before * share).astype(bf16)
        density = jnp.exp(before * before * -0.5) * (1.0 / math.sqrt(2.0 * math.pi))
        slope_ref[:, columns] = (share + before * density).astype(bf16)


def expand_output(h_ref, active_ref, down_ref, down_bias):
    return h_ref[...].astype(f32) + dot(active_ref[...], down_ref[...]) + down_bias


def turned_blocks(sz, value, me, turned_ref, blocks_ref):
    turned_ref[...] = value.T
    for j in range(sz.sections):
        source = pl.multiple_of((me ^ j) * sz.cut, sz.cut)
        blocks_ref[j * sz.cut : (j + 1) * sz.cut, :] = turned_ref[pl.ds(source, sz.cut), :]


def put_vector(small, at, vector):
    for tile in range(vector.shape[1] // LANES):
        small[at + tile : at + tile + 1, :] = vector[:, tile * LANES : (tile + 1) * LANES]
    return at + vector.shape[1] // LANES


def put_tiles(pack, j, at, value):
    r = value.shape[0]
    for tile in range(value.shape[1] // LANES):
        pack[j, pl.ds(at + tile * r, r), :] = value[:, tile * LANES : (tile + 1) * LANES].astype(bf16)


def norm_backward(sz, h_ref, grad_ref, grad_normed_ref, gain, dh_ref):
    gain_sum = jnp.zeros((1, sz.width), f32)
    shift_sum = jnp.zeros((1, sz.width), f32)
    for rows in row_blocks(sz):
        scaled, inverse = normalize(h_ref[rows, :].astype(f32))
        grad_normed = grad_normed_ref[rows, :]
        grad_scaled = grad_normed * gain
        first = jnp.mean(grad_scaled, axis=-1, keepdims=True)
        second = jnp.mean(grad_scaled * scaled, axis=-1, keepdims=True)
        grad_in = inverse * (grad_scaled - first - scaled * second)
        dh_ref[rows, :] = (grad_ref[rows, :].astype(f32) + grad_in).astype(dh_ref.dtype)
        gain_sum += jnp.sum(grad_normed * scaled, axis=0, keepdims=True)
        shift_sum += jnp.sum(grad_normed, axis=0, keepdims=True)
    return gain_sum, shift_sum


def expand_backward(sz, me, h_ref, normed, grad_ref, act_ref, slope_ref, gain, up, down, dh_ref, scratch, pack, small):
    total, turned, blocks = scratch
    base = 0
    part = sz.hidden_cut
    up_rows = sz.hidden // LANES * sz.cut
    turned_blocks(sz, normed[...], me, turned, blocks)
    after = 2 * sz.tiles
    for j in range(sz.sections):
        owner = me ^ j
        columns = pl.ds(pl.multiple_of(owner * part, LANES), part)
        put_tiles(pack, j, base + up_rows, dot_first(act_ref[:, columns], grad_ref[...]))
        grad_active = dot_last(grad_ref[...], down[columns, :])
        grad_before = (grad_active * slope_ref[:, columns].astype(f32)).astype(bf16)
        up_sum = jnp.sum(grad_before.astype(f32), axis=0, keepdims=True)
        for tile in range(part // LANES):
            small[pl.ds(after + owner * (part // LANES) + tile, 1), :] = up_sum[:, tile * LANES : (tile + 1) * LANES]
        up_grad = dot(blocks[...], grad_before)
        at = base + pl.multiple_of(owner * (part // LANES * sz.cut), 16)
        for other in range(sz.sections):
            put_tiles(pack, other, at, up_grad[other * sz.cut : (other + 1) * sz.cut, :])
        more = dot_last(grad_before, up[:, columns])
        if j == 0:
            total[...] = more
        else:
            total[...] += more
    gain_sum, shift_sum = norm_backward(sz, h_ref, grad_ref, total, gain, dh_ref)
    put_vector(small, 0, gain_sum)
    put_vector(small, sz.tiles, shift_sum)
    put_vector(
        small, after + sz.hidden // LANES, jnp.sum(grad_ref[...].astype(f32), axis=0, keepdims=True)
    )


def attend_core_backward(sz, grad_ref, output, qkv_ref, lse_ref, proj, dctx, bias_refs):
    width = sz.width
    dctx[...] = dot_last(grad_ref[...], output[...]).astype(bf16)
    scale = 1.0 / math.sqrt(sz.head)
    for which, (start, length) in enumerate(sz.windows):
        rows = slice(start, start + length)
        bias = bias_refs[which]
        own = own_rows(sz, which)
        for pair in range(HEADS // 2):
            at = 2 * sz.head * pair
            columns = [slice(part * width + at, part * width + at + 2 * sz.head) for part in range(3)]
            queries, keys, values = (qkv_ref[rows, c] for c in columns)
            grad_ctx = jnp.where(own, dctx[rows, columns[0]], jnp.zeros((length, 2 * sz.head), bf16))
            keys = stacked_heads(sz, keys)
            scores = dot_last(keys, queries)
            grad_probs = dot_last(stacked_heads(sz, values), grad_ctx)
            probs, grad_scores = [], []
            for which_head in range(2):
                part = slice(which_head * length, (which_head + 1) * length)
                row = 8 * which + 2 * pair + which_head
                prob = jnp.exp(scores[part] + bias[...] - lse_ref[row : row + 1, :length])
                grad_prob = grad_probs[part]
                delta = jnp.sum(prob * grad_prob, axis=0, keepdims=True)
                grad_scores.append((prob * (grad_prob - delta)).astype(bf16))
                probs.append(prob.astype(bf16))
            grad_scores = jnp.concatenate(grad_scores, axis=0)
            first = head_mask(sz, length, 0)
            grad_keys = dot(grad_scores, queries)
            grad_values = dot(jnp.concatenate(probs, axis=0), grad_ctx)
            store_window(sz, which, proj, columns[0], dot_first(grad_scores, keys) * scale)
            store_window(sz, which, proj, columns[1], jnp.where(first, grad_keys[:length], grad_keys[length:]))
            store_window(sz, which, proj, columns[2], jnp.where(first, grad_values[:length], grad_values[length:]))


def attend_backward(sz, me, h_ref, normed, grad_ref, ctx_ref, proj, gain, triple, dh_ref, scratch, pack, small):
    total, turned, blocks = scratch
    width = sz.width
    grad = grad_ref[...]
    out_rows = 3 * sz.tiles * sz.cut
    turned_blocks(sz, ctx_ref[...], me, turned, blocks)
    output_grad = dot(blocks[...], grad)
    for j in range(sz.sections):
        put_tiles(pack, j, out_rows, output_grad[j * sz.cut : (j + 1) * sz.cut, :])
    turned_blocks(sz, normed[...], me, turned, blocks)
    after = 2 * sz.tiles
    for part in range(3):
        columns = slice(part * width, (part + 1) * width)
        grad_part = proj[:, columns]
        triple_grad = dot(blocks[...], grad_part)
        for j in range(sz.sections):
            put_tiles(pack, j, part * sz.tiles * sz.cut, triple_grad[j * sz.cut : (j + 1) * sz.cut, :])
        if part != 1:
            after = put_vector(small, after, jnp.sum(grad_part.astype(f32), axis=0, keepdims=True))
    total[...] = dot_last(proj[...], triple[...])
    gain_sum, shift_sum = norm_backward(sz, h_ref, grad_ref, total, gain, dh_ref)
    put_vector(small, 0, gain_sum)
    put_vector(small, sz.tiles, shift_sum)
    return put_vector(small, after, jnp.sum(grad.astype(f32), axis=0, keepdims=True))


def put_rows(sz, value, me, turned, blocks, keep, send):
    turned_blocks(sz, value, me, turned, blocks)
    for j in range(sz.sections):
        for tile in range(sz.rows // LANES):
            (keep, send)[j % 2][j // 2, tile * sz.cut : (tile + 1) * sz.cut, :] = blocks[
                j * sz.cut : (j + 1) * sz.cut, tile * LANES : (tile + 1) * LANES
            ]


def ship(exchange, me, replica, pack, rows, keep, send):
    size = rows // exchange.shards
    for shard in range(exchange.shards):
        offset = exchange.shard_of(replica) ^ shard
        for core in range(2):
            for across in range(2):
                options = [exchange.place(c, across, offset) for c in range(2)]
                place = jnp.where(me & 1 ^ core == 0, options[0], options[1])
                target = (keep, send)[core]
                target[pl.ds(pl.multiple_of(place * size, 16), size), :] = pack[
                    2 * across + core, shard * size : (shard + 1) * size, :
                ]


def put_small(pack, start, rows, small):
    held = small.shape[0]
    for j in range(pack.shape[0]):
        pack[j, start : start + held, :] = small[...].astype(bf16)
        if start + held < rows:
            pack[j, start + held : rows, :] = jnp.zeros((rows - start - held, LANES), bf16)


class Moves:
    def __init__(self, pairs, sems):
        self.copies = [pltpu.make_async_copy(source, target, sems.at[i]) for i, (source, target) in enumerate(pairs)]

    def start(self, *which):
        for i in which:
            self.copies[i].start()

    def wait(self, *which):
        for i in which:
            self.copies[i].wait()


def row_of(ref, layer):
    return ref[layer : layer + 1, :].astype(f32)


def pick_row(block, which):
    value = block[:, 0, :].astype(f32)
    for other in range(1, block.shape[1]):
        value = jnp.where(which == other, block[:, other, :].astype(f32), value)
    return value


def gather_rows(sz, of_global, of_local, crop, image, wide):
    wide[: sz.global_len, :] = pick_row(of_global, crop)
    for at in range(sz.locals):
        start = sz.global_len + at * sz.local_len
        wide[start : start + sz.local_len, :] = pick_row(of_local.at[at], image)
    wide[sz.used :, :] = jnp.zeros((sz.rows - sz.used, sz.width), f32)


def front_kernel(sz, *refs):
    rows_in, smalls_in, ratio_ref, weights_in, refs = refs[:4], refs[4:14], refs[14], refs[15:19], refs[19:]
    (
        s0, s1, s2, s3, n0, n1, n2, qkv0, qkv1, lse0, lse1, ctx0, ctx1, act0, act1, slope0, masked_ref, grad,
        triple0, triple1, output0, output1, up0, down0, down1, gain_a, gain_e, down_b, keep, send,
    ) = refs[:30]
    (
        up1, rank_ref, token_ref, shift_a, pair, output_b, shift_e, up_b, own_global, own_local, own_global_back,
        own_local_back, n3, slope1, wide, bias0, bias1, turned, blocks, pack, small, first_grad, load_sems,
    ) = refs[30:]
    own = (own_global, own_local, own_global_back, own_local_back)
    smalls = (rank_ref, token_ref, gain_a, shift_a, pair, output_b, gain_e, shift_e, up_b, down_b)
    weights = ((triple0, output0, up0, down0), (triple1, output1, up1, down1))
    me, replica = lax.axis_index("section"), lax.axis_index("dp")
    per_image = sz.sections // sz.images
    image, crop = me // per_image, me % per_image
    several = pl.ds(crop * sz.locals, sz.locals)
    places = [image, several, image, several]
    pairs = [(source.at[place], target) for source, place, target in zip(rows_in, places, own)]
    pairs += list(zip(smalls_in, smalls))
    pairs += [(weights_in[k].at[layer], weights[layer][k]) for layer in range(2) for k in range(4)]
    loads = Moves(pairs, load_sems)
    loads.start(0, 1, *range(4, 16))
    bias0[...] = window_bias(sz, 0)
    bias1[...] = window_bias(sz, 1)
    biases = (bias0, bias1)
    patches = sz.global_len - 1
    loads.wait(0, 1, *range(4, 14))
    loads.start(2, 3, *range(16, 22))
    limit = lax.div((ratio_ref[image] + 1) * patches, jnp.int32(10))
    both = rank_ref[image]
    entry = lax.broadcasted_iota(jnp.int32, both.shape, 0)
    ranks = jnp.sum(jnp.where(entry == crop, both, 0), axis=0, keepdims=True)
    shape = (sz.rows, patches)
    row = lax.broadcasted_iota(jnp.int32, shape, 0)
    column = lax.broadcasted_iota(jnp.int32, shape, 1)
    chosen = jnp.where((row == column + 1) & (ranks < limit), 1.0, 0.0)
    chosen = jnp.max(chosen, axis=-1, keepdims=True)
    masked_ref[...] = jnp.broadcast_to(chosen, masked_ref.shape)
    gather_rows(sz, own[0], own[1], crop, image, wide)
    s0[...] = jnp.where(chosen > 0.5, token_ref[...].astype(f32), wide[...]).astype(bf16)

    def attend_weights(layer):
        triple, output, _, _ = weights[layer]
        return (
            row_of(gain_a, layer), row_of(shift_a, layer), triple, row_of(pair, layer), output, row_of(output_b, layer),
        )

    def expand_weights(layer):
        return row_of(gain_e, layer), row_of(shift_e, layer), weights[layer][2], row_of(up_b, layer)

    loads.wait(14, 15)
    attend_forward(sz, s0, attend_weights(0), s1, n0, qkv0, lse0, ctx0, biases)
    loads.wait(16, 17)
    expand_hidden(sz, s1, expand_weights(0), n1, act0, slope0)
    s2[...] = expand_output(s1, act0, down0, row_of(down_b, 0)).astype(bf16)
    loads.wait(18, 19)
    attend_forward(sz, s2, attend_weights(1), s3, n2, qkv1, lse1, ctx1, biases)
    loads.wait(20, 21)
    expand_hidden(sz, s3, expand_weights(1), n3, act1, slope1)
    loads.wait(2, 3)
    gather_rows(sz, own[2], own[3], crop, image, wide)
    first_grad[...] = wide[...].astype(bf16)
    small[...] = jnp.zeros_like(small)
    expand_backward(
        sz, me, s3, n3, first_grad, act1, slope1, row_of(gain_e, 1), up1, down1, grad, (wide, turned, blocks), pack, small
    )
    rows = sz.packed(sz.expand_full)
    put_small(pack, sz.expand_full, rows, small)
    ship(sz.exchanges["A"], me, replica, pack, rows, keep, send)


def output_kernel(sz, h_ref, act_ref, down, down_b, out_keep, out_send, turned, blocks):
    me = lax.axis_index("section")
    last = expand_output(h_ref, act_ref, down, row_of(down_b, 1)).astype(bf16)
    put_rows(sz, last, me, turned, blocks, out_keep, out_send)


def expand_kernel(sz, h, normed, grad, act, slope, up, down, gain, dh_ref, keep, send, total, turned, blocks, pack, small):
    me, replica = lax.axis_index("section"), lax.axis_index("dp")
    small[...] = jnp.zeros_like(small)
    expand_backward(
        sz, me, h, normed, grad, act, slope, row_of(gain, 0), up, down, dh_ref, (total, turned, blocks), pack, small
    )
    rows = sz.packed(sz.expand_full)
    put_small(pack, sz.expand_full, rows, small)
    ship(sz.exchanges["C"], me, replica, pack, rows, keep, send)


def attend_core_kernel(sz, grad, output, qkv, lse, proj, dctx, bias0, bias1):
    bias0[...] = window_bias(sz, 0)
    bias1[...] = window_bias(sz, 1)
    attend_core_backward(sz, grad, output, qkv, lse, proj, dctx, (bias0, bias1))


def attend_kernel(sz, layer, *refs):
    h, normed, grad, ctx, proj, triple, gain, flags = refs[:8]
    if layer == 0:
        in_keep, in_send, keep, send, total, turned, blocks, pack, small = refs[8:]
        target = total
    else:
        target, keep, send, total, turned, blocks, pack, small = refs[8:]
    me, replica = lax.axis_index("section"), lax.axis_index("dp")
    small[...] = jnp.zeros_like(small)
    rows = sz.packed(sz.attend_full)
    after = attend_backward(
        sz, me, h, normed, grad, ctx, proj, row_of(gain, layer), triple, target, (total, turned, blocks), pack, small
    )
    if layer == 0:
        masked = flags[:, :1] > 0.5
        put_vector(small, after, jnp.sum(jnp.where(masked, total[...], 0.0), axis=0, keepdims=True))
        put_rows(sz, jnp.where(masked, 0.0, total[...]).astype(bf16), me, turned, blocks, in_keep, in_send)
    put_small(pack, sz.attend_full, rows, small)
    ship(sz.exchanges["DB"[layer]], me, replica, pack, rows, keep, send)


def unpack(exchange, me, replica, source, target):
    shard = target.shape[0] // exchange.shards
    for place in range(exchange.shards):
        options = [exchange.offset(core, place) for core in range(2)]
        offset = jnp.where(me & 1 == 0, options[0], options[1])
        at = pl.multiple_of((exchange.shard_of(replica) ^ offset) * shard, 16)
        target[pl.ds(at, shard), :] = source[place * shard : (place + 1) * shard, :]


def widen_tiles(source, base, target):
    r, columns = target.shape
    for tile in range(columns // LANES):
        target[:, tile * LANES : (tile + 1) * LANES] = source[base + tile * r : base + (tile + 1) * r, :].astype(f32)


def widen(sz, attend, expand, targets, moves):
    triple, output, up, down = targets
    hidden_rows = sz.hidden // LANES * sz.cut
    for index, (source, base, target) in enumerate(
        ((expand, 0, up), (expand, hidden_rows, down), (attend, 0, triple), (attend, 3 * sz.tiles * sz.cut, output))
    ):
        widen_tiles(source, base, target)
        moves[(2, 3, 0, 1)[index]].start()


def early_kernel(sz, *refs):
    (expand_in, attend_in), (out_own, out_core, in_own, in_core, across) = refs[:2], refs[2:7]
    (out_global, out_local, in_global, in_local), outs, vectors = refs[7:11], refs[11:15], refs[15]
    expand, attend, targets, wide, sems = refs[16], refs[17], refs[18:22], refs[22], refs[23]
    me, replica = lax.axis_index("section"), lax.axis_index("dp")
    moves = [pltpu.make_async_copy(target, out.at[1], sems.at[i]) for i, (target, out) in enumerate(zip(targets, outs))]
    unpack(sz.exchanges["A"], me, replica, expand_in, expand)
    unpack(sz.exchanges["B"], me, replica, attend_in, attend)
    widen(sz, attend, expand, targets, moves)
    vectors[: sz.small_rows, :] = attend[sz.attend_full : sz.attend_full + sz.small_rows, :].astype(f32)
    vectors[sz.small_rows :, :] = expand[sz.expand_full : sz.expand_full + sz.small_rows, :].astype(f32)
    row_parts = (
        (out_own.at[0], out_core.at[0], across.at[0], across.at[1]),
        (in_own.at[0], in_core.at[0], across.at[2], across.at[3]),
    )
    per_image = sz.sections // sz.images
    for which, (to_global, to_local) in enumerate(((out_global, out_local), (in_global, in_local))):
        for k in range(4):
            section = me ^ k
            image, crop = section // per_image, section % per_image
            turned = jnp.concatenate(
                [
                    row_parts[which][k][tile * sz.cut : (tile + 1) * sz.cut, :].astype(f32)
                    for tile in range(sz.rows // LANES)
                ],
                axis=1,
            )
            to_global[section] = turned[:, : sz.global_len]
            turned = jnp.concatenate([turned, jnp.zeros((LANES - sz.cut, sz.rows), f32)], axis=0)
            wide[...] = turned.T
            for at in range(sz.locals):
                start = sz.global_len + at * sz.local_len
                to_local[crop * sz.locals + at, :, pl.ds(image, 1), :] = wide[
                    start : start + sz.local_len, : sz.cut
                ].reshape(sz.local_len, 1, sz.cut)
    for move in moves:
        move.wait()


def finish_kernel(sz, *refs):
    expand_in, attend_in, later_vectors = refs[:3]
    (token, gain_a, shift_a, pair, output_b, gain_e, shift_e, up_b, down_b), outs = refs[7:16], refs[16:20]
    expand, attend, targets, vectors, sems = refs[20], refs[21], refs[22:26], refs[26], refs[27]
    me, replica = lax.axis_index("section"), lax.axis_index("dp")
    moves = [pltpu.make_async_copy(target, out.at[0], sems.at[i]) for i, (target, out) in enumerate(zip(targets, outs))]
    unpack(sz.exchanges["C"], me, replica, expand_in, expand)
    unpack(sz.exchanges["D"], me, replica, attend_in, attend)
    widen(sz, attend, expand, targets, moves)
    width, tiles, cut = sz.width, sz.tiles, sz.cut
    row = lax.broadcasted_iota(jnp.int32, (width, cut), 0)
    column = lax.broadcasted_iota(jnp.int32, (width, cut), 1)
    pick = jnp.where(row == column + me * cut, 1.0, 0.0).astype(bf16)
    row = lax.broadcasted_iota(jnp.int32, (2 * width, 2 * cut), 0)
    column = lax.broadcasted_iota(jnp.int32, (2 * width, 2 * cut), 1)
    pick_pair = jnp.where(row == column + me * 2 * cut, 1.0, 0.0).astype(bf16)
    hidden_tiles, up_tiles = sz.hidden // LANES, sz.hidden_cut // LANES
    vectors[: sz.small_rows, :] = attend[sz.attend_full : sz.attend_full + sz.small_rows, :].astype(f32)
    vectors[sz.small_rows :, :] = expand[sz.expand_full : sz.expand_full + sz.small_rows, :].astype(f32)
    for layer, held in enumerate((vectors, later_vectors)):
        one = slice(layer, layer + 1)

        def vector(at, tiles_in):
            return jnp.concatenate([held[at + t : at + t + 1, :] for t in range(tiles_in)], axis=1)

        def picked(at):
            return dot(vector(at, tiles).astype(bf16), pick)

        gain_a[one, :] = picked(0)
        shift_a[one, :] = picked(tiles)
        pair[one, :] = dot(vector(2 * tiles, 2 * tiles).astype(bf16), pick_pair)
        output_b[one, :] = picked(4 * tiles)
        if layer == 0:
            token[...] = picked(5 * tiles)
        base = sz.small_rows
        gain_e[one, :] = picked(base)
        shift_e[one, :] = picked(base + tiles)
        for tile in range(up_tiles):
            up_b[one, tile * LANES : (tile + 1) * LANES] = held[pl.ds(base + 2 * tiles + me * up_tiles + tile, 1), :]
        down_b[one, :] = picked(base + 2 * tiles + hidden_tiles)
    for move in moves:
        move.wait()


VMEM = pl.BlockSpec(memory_space=pltpu.VMEM)
ANY = pl.BlockSpec(memory_space=pl.ANY)
HBM = pl.BlockSpec(memory_space=pltpu.HBM)
SMEM = pl.BlockSpec(memory_space=pltpu.SMEM)
DMA = pltpu.SemaphoreType.DMA


def call(body, name, outs, in_specs, scratch, args, flops, aliases=()):
    args = [
        pltpu.with_memory_space_constraint(arg, pltpu.HBM) if spec is HBM else arg for arg, spec in zip(args, in_specs)
    ]
    return pl.pallas_call(
        body,
        name=name,
        out_shape=tuple(jax.ShapeDtypeStruct(shape, kind) for shape, kind, _ in outs),
        in_specs=in_specs,
        out_specs=tuple(memory for _, _, memory in outs),
        scratch_shapes=[pltpu.VMEM(*item) if isinstance(item, tuple) else item for item in scratch],
        input_output_aliases=dict(aliases),
        compiler_params=pltpu.CompilerParams(vmem_limit_bytes=VMEM_MIB.get(name, 14) << 20),
        cost_estimate=pl.CostEstimate(flops=flops, bytes_accessed=1 << 20, transcendentals=0),
    )(*args)


def add(first, *others):
    total = first.astype(f32)
    for other in others:
        total = total + other.astype(f32)
    return lax.reduce_precision(total, 8, 7).astype(bf16)


def swap(value, partner_of):
    sections, replicas = lax.axis_size("section"), lax.axis_size("dp")
    route = []
    for section in range(sections):
        for replica in range(replicas):
            to_section, to_replica = partner_of(section, replica)
            route.append((section * replicas + replica, to_section * replicas + to_replica))
    return lax.ppermute(value, ("section", "dp"), route)


def other_core(section, replica):
    return section ^ 1, replica


def other_x(section, replica):
    return section ^ 2, replica


def along(orders, step):
    def partner_of(section, replica):
        axis = orders[section & 1][step]
        return (section ^ 2, replica) if axis == X_AXIS else (section, replica ^ (1 << axis))

    return partner_of


class Sequence:
    def __init__(self):
        self.last = None

    def after(self, value):
        return value if self.last is None else lax.optimization_barrier((value, self.last))[0]

    def mark(self, value):
        self.last = value
        return value


def reduce_steps(exchange, order, keep, send):
    orders = exchange.orders
    core = swap(send, other_core)
    yield
    core = order.after(core)
    half = keep.shape[0] // 2
    moved = swap(order.mark(add(keep[half:], core[half:])), along(orders, 0))
    yield
    moved = order.after(moved)
    mine = add(keep[:half], core[:half], moved)
    for step in range(1, len(orders[0])):
        half = mine.shape[0] // 2
        moved = swap(order.mark(mine[half:]), along(orders, step))
        yield
        mine = add(mine[:half], order.after(moved))
    for axis in exchange.rest:
        moved = swap(order.mark(mine), along(([axis], [axis]), 0))
        yield
        mine = add(mine, order.after(moved))
    back = [[axis for axis in order_of if axis != X_AXIS] for order_of in orders]
    for step in reversed(range(len(back[0]))):
        moved = swap(order.mark(mine), along(back, step))
        yield
        mine = jnp.concatenate([mine, order.after(moved)], axis=0)
    yield mine


def row_steps(order, out_rows, in_rows):
    cores = [swap(send, other_core) for _, send in (out_rows, in_rows)]
    yield
    cores[0] = order.after(cores[0])
    across = swap(order.mark(jnp.stack([out_rows[0][1], cores[0][1], in_rows[0][1], cores[1][1]])), other_x)
    yield
    yield out_rows[0], cores[0], in_rows[0], cores[1], order.after(across)


def per_device(
    global_rows, local_rows, patch_rank, ratio_bin, mask_token, attend_gain, attend_shift, triple_weight,
    pair_bias, output_weight, output_bias, expand_gain, expand_shift, up_weight, up_bias, down_weight,
    down_bias, grad_global, grad_local,
):
    sections, replicas = lax.axis_size("section"), lax.axis_size("dp")
    sz = Sizes(global_rows, local_rows, up_weight, sections, replicas)
    width, rows, hidden = sz.width, sz.rows, sz.hidden
    sets = [rows_of.transpose(0, 2, 1, 3) for rows_of in (global_rows, grad_global)]
    many = [rows_of.transpose(1, 2, 0, 3) for rows_of in (local_rows, grad_local)]
    weights = (triple_weight, output_weight, up_weight, down_weight)
    smalls = (
        patch_rank, mask_token, attend_gain, attend_shift, pair_bias, output_bias, expand_gain, expand_shift, up_bias,
        down_bias,
    )
    wide = ((rows, width), bf16)
    triple_rows = ((rows, 3 * width), bf16)
    hidden_rows = ((rows, hidden), bf16)
    lse = ((16, up_to(max(length for _, length in sz.windows), LANES)), f32)
    flags = ((rows, LANES), f32)
    wide_f32 = ((rows, width), f32)
    turned = ((width, rows), bf16)
    small = ((sz.small_rows, LANES), f32)
    share = ((2, sz.extra, LANES), bf16)
    stage = ((sections, sz.extra, LANES), bf16)
    windows = [((length, length), f32) for _, length in sz.windows]
    totals = [sz.packed(full) for full in (sz.expand_full, sz.attend_full)]
    packs = [((sections, total, LANES), bf16) for total in totals]
    parts = [((2 * total, LANES), bf16) for total in totals]
    vectors = ((2, width), bf16)
    blocks = [(weight.shape[1:], bf16) for weight in weights]
    shared = [wide_f32, turned, turned]

    def run_kernel(body, name, outs, scratch, args):
        return call(
            lambda *refs: body(sz, *refs), name, [out + (VMEM,) for out in outs], [VMEM] * len(args), scratch, args, 4 << 30
        )

    (
        s0, s1, s2, s3, n0, n1, n2, qkv0, qkv1, lse0, lse1, ctx0, ctx1, act0, act1, slope0, masked, grad,
        triple0, triple1, output0, output1, up0, down0, down1, gain_a, gain_e, down_b, keep, send,
    ) = call(
        lambda *refs: front_kernel(sz, *refs),
        "front",
        [
            out + (VMEM,)
            for out in [wide] * 7 + [triple_rows] * 2 + [lse] * 2 + [wide] * 2 + [hidden_rows] * 3 + [flags, wide]
            + [blocks[0]] * 2 + [blocks[1]] * 2 + [blocks[2]] + [blocks[3]] * 2 + [vectors] * 3 + [parts[0]] * 2
        ],
        [HBM] * 14 + [SMEM] + [HBM] * 4,
        [blocks[2]]
        + [(one.shape, one.dtype) for one in (patch_rank, mask_token, attend_shift, pair_bias, output_bias)]
        + [(one.shape, one.dtype) for one in (expand_shift, up_bias)]
        + [(sets[0].shape[1:], bf16), ((sz.locals,) + many[0].shape[1:], bf16)] * 2
        + [wide, hidden_rows, wide_f32] + windows + [turned] * 2 + [packs[0], small, wide, DMA((22,))],
        (sets[0], many[0], sets[1], many[1], *smalls, ratio_bin, *weights),
        8 << 30,
    )
    order = Sequence()
    chains, results = {}, {}
    chains["A"] = reduce_steps(sz.exchanges["A"], order, keep, send)
    core_scratch = [wide] + windows
    flow = {"grad": grad}

    def core_kernel(name, output, qkv, lse_of):
        proj, = run_kernel(
            attend_core_kernel, name, [triple_rows], core_scratch, (order.after(flow["grad"]), output, qkv, lse_of)
        )
        flow["proj"] = order.mark(proj)

    def later_core():
        core_kernel("later_core", output1, qkv1, lse1)

    def later_attend():
        dh, keep, send = run_kernel(
            lambda sz, *refs: attend_kernel(sz, 1, *refs), "later_attend", [wide] + [parts[1]] * 2,
            shared + [packs[1], small],
            (s2, n2, flow["grad"], ctx1, order.after(flow["proj"]), triple1, gain_a, masked),
        )
        flow["grad"] = order.mark(dh)
        chains["B"] = reduce_steps(sz.exchanges["B"], order, keep, send)

    def expand():
        dh, keep, send = run_kernel(
            expand_kernel, "expand_back", [wide] + [parts[0]] * 2, shared + [packs[0], small],
            (s1, n1, order.after(flow["grad"]), act0, slope0, up0, down0, gain_e),
        )
        flow["grad"] = order.mark(dh)
        chains["C"] = reduce_steps(sz.exchanges["C"], order, keep, send)

    def core():
        core_kernel("attend_core", output0, qkv0, lse0)

    def attend():
        in_keep, in_send, keep, send = run_kernel(
            lambda sz, *refs: attend_kernel(sz, 0, *refs), "attend_back", [share] * 2 + [parts[1]] * 2,
            shared + [packs[1], small],
            (s0, n0, flow["grad"], ctx0, order.after(flow["proj"]), triple0, gain_a, masked),
        )
        flow["in"] = (order.mark(in_keep), in_send)
        chains["D"] = reduce_steps(sz.exchanges["D"], order, keep, send)

    def output_rows():
        out_rows = run_kernel(
            output_kernel, "output_rows", [share] * 2, [turned, turned], (s3, order.after(act1), down1, down_b)
        )
        order.mark(out_rows[0])
        chains["R"] = row_steps(order, out_rows, flow["in"])

    cut = sz.cut
    weight_outs = [(2, cut, 3 * width), (2, cut, width), (2, cut, hidden), (2, sz.hidden_cut, width)]
    row_outs = [(sz.all_globals, cut, sz.global_len), local_rows.shape[1:3] + (sz.images, cut)] * 2
    both_small = ((2 * sz.small_rows, LANES), f32)
    finish_scratch = [((total, LANES), bf16) for total in totals] + [(shape[1:], f32) for shape in weight_outs]

    def early():
        expand_of, attend_of = (order.after(results[step]) for step in "AB")
        flow["early"] = call(
            lambda *refs: early_kernel(sz, *refs), "early",
            [(shape, f32, VMEM) for shape in row_outs] + [(shape, f32, ANY) for shape in weight_outs] + [both_small + (VMEM,)],
            [VMEM] * 7, finish_scratch + [flags, DMA((4,))], (expand_of, attend_of, *results["R"]), 1 << 28,
        )
        order.mark(flow["early"][-1])

    kernels = {
        "later_core": later_core, "later_attend": later_attend, "expand": expand, "core": core, "attend": attend,
        "output": output_rows, "early": early,
    }
    for plan in PLAN:
        for step in plan.split():
            if step == "early":
                for _ in range(3, len(sz.exchanges["A"].rest) + len(sz.exchanges["A"].axes)):
                    for name in "ABCD":
                        results[name] = next(chains[name], results.get(name))
            if step in kernels:
                kernels[step]()
            else:
                results[step] = next(chains[step], results.get(step))
    *row_values, triple, output, up, down, late_vectors = flow["early"]
    vector_outs = [(1, cut), (2, cut), (2, cut), (2, 2 * cut)] + [(2, cut)] * 3 + [(2, sz.hidden_cut), (2, cut)]
    final = call(
        lambda *refs: finish_kernel(sz, *refs), "finish",
        [(shape, f32, VMEM) for shape in vector_outs] + [(shape, f32, ANY) for shape in weight_outs],
        [VMEM] * 3 + [ANY] * 4, finish_scratch + [both_small, DMA((4,))],
        (order.after(results["C"]), results["D"], late_vectors, triple, output, up, down), 1 << 28,
        [(3 + i, len(vector_outs) + i) for i in range(4)],
    )
    token, gain_a, shift_a, pair, output_b, gain_e, shift_e, up_b, down_b, triple, output, up, down = final
    shape = global_rows.shape[:2] + (cut, sz.global_len)
    return (
        row_values[0].reshape(shape).transpose(0, 1, 3, 2), row_values[1].transpose(2, 0, 1, 3),
        row_values[2].reshape(shape).transpose(0, 1, 3, 2), row_values[3].transpose(2, 0, 1, 3),
        token, gain_a, shift_a, triple, pair, output, output_b, gain_e, shift_e, up, up_b, down, down_b,
    )


def solution(mesh):
    rows, copied = P("dp", None, None, None), P()
    in_specs = (rows, rows, P("dp", None, None), P("dp")) + (copied,) * 13 + (rows, rows)
    wide, flat, deep = P("dp", None, None, "section"), P(None, "section"), P(None, "section", None)
    out_specs = (
        wide, wide, wide, wide, flat, flat, flat, deep, flat, deep, flat, flat, flat, deep, flat, deep, flat,
    )
    return jax.shard_map(per_device, mesh=mesh, in_specs=in_specs, out_specs=out_specs, check_vma=False)
```

```python
import math

import jax
import jax.numpy as jnp
from jax import lax
from jax.experimental import pallas as pl
from jax.experimental.pallas import tpu as pltpu
from jax.sharding import PartitionSpec as P

HEADS = 6
EPS = 1e-06
LANES = 128
VMEM_MIB = {"front": 26, "finish": 20}
CHOICES = (0, 0, 1, 0)
PLAN = (
    "A later_core later_attend A",
    "expand core C B",
    "A C B attend",
    "D C D A",
    "B output R A",
    "B D C B",
    "A C D B",
    "A D C R",
    "B D C R",
    "D A C B",
    "D A B R",
    "early C D",
)
X_AXIS = -1

f32 = jnp.float32
bf16 = jnp.bfloat16


def up_to(value, step):
    return (value + step - 1) // step * step


class Sizes:
    def __init__(self, global_rows, local_rows, up_weight, sections, replicas):
        images, crops, self.global_len, self.width = global_rows.shape
        _, local_crops, self.local_len, _ = local_rows.shape
        self.hidden = up_weight.shape[2]
        self.sections = sections
        self.replicas = replicas
        self.images = images
        self.all_globals = images * crops
        self.all_locals = images * local_crops
        self.locals = self.all_locals // sections
        self.used = self.global_len + self.locals * self.local_len
        self.rows = up_to(self.used, LANES)
        self.head = self.width // HEADS
        self.cut = self.width // sections
        self.hidden_cut = self.hidden // sections
        self.tiles = self.width // LANES
        self.first_end = up_to(self.global_len, 16)
        self.second_start = self.global_len // 16 * 16
        self.windows = (
            (0, self.first_end),
            (self.second_start, self.rows - self.second_start),
        )
        self.attend_full = 4 * self.tiles * self.cut
        self.expand_full = self.hidden // LANES * self.cut + self.tiles * self.hidden_cut
        self.small_rows = up_to(max(6 * self.tiles, 3 * self.tiles + self.hidden // LANES), 16)
        self.extra = self.cut * self.rows // LANES
        bits = replicas.bit_length() - 1
        low = list(range(min(bits, 2)))
        last_first = low[1:] + [X_AXIS] + low[:1]
        first_last = [X_AXIS] + low
        middle = low[:1] + [X_AXIS] + low[1:]
        choices = (
            (first_last, last_first), (middle, last_first), (first_last, middle), ([X_AXIS] + low[1:], low[1:] + [X_AXIS])
        )
        self.exchanges = {name: Exchange(choices[choice], bits) for name, choice in zip("ABCD", CHOICES)}
        self.unit = 16 << len(low)

    def packed(self, full):
        return up_to(full + self.small_rows, self.unit)


class Exchange:
    def __init__(self, orders, bits):
        self.orders = orders
        self.axes = sorted(axis for axis in orders[0] if axis != X_AXIS)
        self.rest = [axis for axis in range(bits) if axis not in self.axes]
        self.shards = 1 << len(self.axes)

    def shard_of(self, replica):
        return sum((replica >> axis & 1) << i for i, axis in enumerate(self.axes))

    def place(self, core, across, offset):
        order = self.orders[core]
        return sum(
            (across if axis == X_AXIS else offset >> self.axes.index(axis) & 1) << (len(order) - 1 - at)
            for at, axis in enumerate(order)
        )

    def offset(self, core, place):
        order = [axis for axis in self.orders[core] if axis != X_AXIS]
        return sum((place >> (len(order) - 1 - at) & 1) << self.axes.index(axis) for at, axis in enumerate(order))


def dot(a, b):
    return jnp.dot(a, b, preferred_element_type=f32)


def dot_last(a, b):
    return lax.dot_general(a, b, (((1,), (1,)), ((), ())), preferred_element_type=f32)


def dot_first(a, b):
    return lax.dot_general(a, b, (((0,), (0,)), ((), ())), preferred_element_type=f32)


def normalize(hidden):
    average = jnp.mean(hidden, axis=-1, keepdims=True)
    centred = hidden - average
    inverse = lax.rsqrt(jnp.mean(centred * centred, axis=-1, keepdims=True) + EPS)
    return centred * inverse, inverse


def row_blocks(sz):
    return [slice(i, i + LANES) for i in range(0, sz.rows, LANES)]


def head_mask(sz, rows, which):
    lane = lax.broadcasted_iota(jnp.int32, (rows, 2 * sz.head), 1)
    return lane < sz.head if which == 0 else lane >= sz.head


def window_bias(sz, which):
    start, length = sz.windows[which]

    def group(row):
        if which == 0:
            return jnp.where(row < sz.global_len, 0, 1)
        kind = jnp.where(row + start < sz.global_len, 0, 1)
        for crop in range(1, sz.locals + 1):
            kind = kind + jnp.where(row + start >= sz.global_len + crop * sz.local_len, 1, 0)
        return kind

    left = group(lax.broadcasted_iota(jnp.int32, (length, length), 0))
    right = group(lax.broadcasted_iota(jnp.int32, (length, length), 1))
    return jnp.where(left == right, 0.0, -1e30).astype(f32)


def own_rows(sz, which):
    start, length = sz.windows[which]
    row = lax.broadcasted_iota(jnp.int32, (length, 1), 0) + start
    return row < sz.global_len if which == 0 else row >= sz.global_len


def store_window(sz, which, ref, columns, value):
    start, length = sz.windows[which]
    if which == 0 or sz.first_end == start:
        ref[start : start + length, columns] = value.astype(bf16)
        return
    shared = sz.first_end - start
    row = lax.broadcasted_iota(jnp.int32, (shared, value.shape[1]), 0) + start
    before = ref[start : sz.first_end, columns].astype(f32)
    ref[start : sz.first_end, columns] = jnp.where(
        row < sz.global_len, before, value[:shared]
    ).astype(bf16)
    ref[sz.first_end : start + length, columns] = value[shared:].astype(bf16)


def norm_rows(sz, h_ref, gain, shift, normed_ref):
    for rows in row_blocks(sz):
        scaled, _ = normalize(h_ref[rows, :].astype(f32))
        normed_ref[rows, :] = (scaled * gain + shift).astype(bf16)


def stacked_heads(sz, value):
    zero = jnp.zeros_like(value)
    return jnp.concatenate([jnp.where(head_mask(sz, value.shape[0], which), value, zero) for which in range(2)], axis=0)


def attend_forward(sz, h_ref, weights, out_ref, normed_ref, qkv_ref, lse_ref, ctx_ref, bias_refs):
    gain, shift, triple_ref, pair_bias, output_ref, output_bias = weights
    width = sz.width
    norm_rows(sz, h_ref, gain, shift, normed_ref)
    scale = 1.0 / math.sqrt(sz.head)
    for part in range(3):
        columns = slice(part * width, (part + 1) * width)
        project = dot(normed_ref[...], triple_ref[:, columns])
        if part == 0:
            project = (project + pair_bias[:, :width]) * scale
        if part == 2:
            project = project + pair_bias[:, width:]
        qkv_ref[:, columns] = project.astype(bf16)
    for which, (start, length) in enumerate(sz.windows):
        rows = slice(start, start + length)
        bias = bias_refs[which]
        lane = lax.broadcasted_iota(jnp.int32, (length, LANES), 1)
        first = head_mask(sz, length, 0)
        kept = jnp.zeros((length, LANES), f32)
        for pair in range(HEADS // 2):
            at = 2 * sz.head * pair
            queries, keys, values = (
                qkv_ref[rows, part * width + at : part * width + at + 2 * sz.head] for part in range(3)
            )
            scores = dot_last(stacked_heads(sz, queries), keys)
            probs = []
            for which_head in range(2):
                own = scores[which_head * length : (which_head + 1) * length] + bias[...]
                top = jnp.max(own, axis=-1, keepdims=True)
                raised = jnp.exp(own - top)
                total = jnp.sum(raised, axis=-1, keepdims=True)
                kept = jnp.where(lane == 2 * pair + which_head, top + jnp.log(total), kept)
                probs.append((raised * (1.0 / total)).astype(bf16))
            context = dot(jnp.concatenate(probs, axis=0), values)
            store_window(
                sz, which, ctx_ref, slice(at, at + 2 * sz.head), jnp.where(first, context[:length], context[length:])
            )
        lse_ref[8 * which : 8 * which + 8, :length] = kept.T[:8]
    moved = dot(ctx_ref[...], output_ref[...]) + output_bias
    out_ref[...] = (h_ref[...].astype(f32) + moved).astype(bf16)


def expand_hidden(sz, h_ref, weights, normed_ref, active_ref, slope_ref):
    gain, shift, up_ref, up_bias = weights
    norm_rows(sz, h_ref, gain, shift, normed_ref)
    for at in range(0, sz.hidden, sz.hidden_cut):
        columns = slice(at, at + sz.hidden_cut)
        before = dot(normed_ref[...], up_ref[:, columns]) + up_bias[:, columns]
        share = 0.5 + 0.5 * lax.erf(before * math.sqrt(0.5))
        active_ref[:, columns] = (before * share).astype(bf16)
        density = jnp.exp(before * before * -0.5) * (1.0 / math.sqrt(2.0 * math.pi))
        slope_ref[:, columns] = (share + before * density).astype(bf16)


def expand_output(h_ref, active_ref, down_ref, down_bias):
    return h_ref[...].astype(f32) + dot(active_ref[...], down_ref[...]) + down_bias


def turned_blocks(sz, value, me, turned_ref, blocks_ref):
    turned_ref[...] = value.T
    for j in range(sz.sections):
        source = pl.multiple_of((me ^ j) * sz.cut, sz.cut)
        blocks_ref[j * sz.cut : (j + 1) * sz.cut, :] = turned_ref[pl.ds(source, sz.cut), :]


def put_vector(small, at, vector):
    for tile in range(vector.shape[1] // LANES):
        small[at + tile : at + tile + 1, :] = vector[:, tile * LANES : (tile + 1) * LANES]
    return at + vector.shape[1] // LANES


def put_tiles(pack, j, at, value):
    r = value.shape[0]
    for tile in range(value.shape[1] // LANES):
        pack[j, pl.ds(at + tile * r, r), :] = value[:, tile * LANES : (tile + 1) * LANES].astype(bf16)


def norm_backward(sz, h_ref, grad_ref, grad_normed_ref, gain, dh_ref):
    gain_sum = jnp.zeros((1, sz.width), f32)
    shift_sum = jnp.zeros((1, sz.width), f32)
    for rows in row_blocks(sz):
        scaled, inverse = normalize(h_ref[rows, :].astype(f32))
        grad_normed = grad_normed_ref[rows, :]
        grad_scaled = grad_normed * gain
        first = jnp.mean(grad_scaled, axis=-1, keepdims=True)
        second = jnp.mean(grad_scaled * scaled, axis=-1, keepdims=True)
        grad_in = inverse * (grad_scaled - first - scaled * second)
        dh_ref[rows, :] = (grad_ref[rows, :].astype(f32) + grad_in).astype(dh_ref.dtype)
        gain_sum += jnp.sum(grad_normed * scaled, axis=0, keepdims=True)
        shift_sum += jnp.sum(grad_normed, axis=0, keepdims=True)
    return gain_sum, shift_sum


def expand_backward(sz, me, h_ref, normed, grad_ref, act_ref, slope_ref, gain, up, down, dh_ref, scratch, pack, small):
    total, turned, blocks = scratch
    base = 0
    part = sz.hidden_cut
    up_rows = sz.hidden // LANES * sz.cut
    turned_blocks(sz, normed[...], me, turned, blocks)
    after = 2 * sz.tiles
    for j in range(sz.sections):
        owner = me ^ j
        columns = pl.ds(pl.multiple_of(owner * part, LANES), part)
        put_tiles(pack, j, base + up_rows, dot_first(act_ref[:, columns], grad_ref[...]))
        grad_active = dot_last(grad_ref[...], down[columns, :])
        grad_before = (grad_active * slope_ref[:, columns].astype(f32)).astype(bf16)
        up_sum = jnp.sum(grad_before.astype(f32), axis=0, keepdims=True)
        for tile in range(part // LANES):
            small[pl.ds(after + owner * (part // LANES) + tile, 1), :] = up_sum[:, tile * LANES : (tile + 1) * LANES]
        up_grad = dot(blocks[...], grad_before)
        at = base + pl.multiple_of(owner * (part // LANES * sz.cut), 16)
        for other in range(sz.sections):
            put_tiles(pack, other, at, up_grad[other * sz.cut : (other + 1) * sz.cut, :])
        more = dot_last(grad_before, up[:, columns])
        if j == 0:
            total[...] = more
        else:
            total[...] += more
    gain_sum, shift_sum = norm_backward(sz, h_ref, grad_ref, total, gain, dh_ref)
    put_vector(small, 0, gain_sum)
    put_vector(small, sz.tiles, shift_sum)
    put_vector(
        small, after + sz.hidden // LANES, jnp.sum(grad_ref[...].astype(f32), axis=0, keepdims=True)
    )


def attend_core_backward(sz, grad_ref, output, qkv_ref, lse_ref, proj, dctx, bias_refs):
    width = sz.width
    dctx[...] = dot_last(grad_ref[...], output[...]).astype(bf16)
    scale = 1.0 / math.sqrt(sz.head)
    for which, (start, length) in enumerate(sz.windows):
        rows = slice(start, start + length)
        bias = bias_refs[which]
        own = own_rows(sz, which)
        for pair in range(HEADS // 2):
            at = 2 * sz.head * pair
            columns = [slice(part * width + at, part * width + at + 2 * sz.head) for part in range(3)]
            queries, keys, values = (qkv_ref[rows, c] for c in columns)
            grad_ctx = jnp.where(own, dctx[rows, columns[0]], jnp.zeros((length, 2 * sz.head), bf16))
            keys = stacked_heads(sz, keys)
            scores = dot_last(keys, queries)
            grad_probs = dot_last(stacked_heads(sz, values), grad_ctx)
            probs, grad_scores = [], []
            for which_head in range(2):
                part = slice(which_head * length, (which_head + 1) * length)
                row = 8 * which + 2 * pair + which_head
                prob = jnp.exp(scores[part] + bias[...] - lse_ref[row : row + 1, :length])
                grad_prob = grad_probs[part]
                delta = jnp.sum(prob * grad_prob, axis=0, keepdims=True)
                grad_scores.append((prob * (grad_prob - delta)).astype(bf16))
                probs.append(prob.astype(bf16))
            grad_scores = jnp.concatenate(grad_scores, axis=0)
            first = head_mask(sz, length, 0)
            grad_keys = dot(grad_scores, queries)
            grad_values = dot(jnp.concatenate(probs, axis=0), grad_ctx)
            store_window(sz, which, proj, columns[0], dot_first(grad_scores, keys) * scale)
            store_window(sz, which, proj, columns[1], jnp.where(first, grad_keys[:length], grad_keys[length:]))
            store_window(sz, which, proj, columns[2], jnp.where(first, grad_values[:length], grad_values[length:]))


def attend_backward(sz, me, h_ref, normed, grad_ref, ctx_ref, proj, gain, triple, dh_ref, scratch, pack, small):
    total, turned, blocks = scratch
    width = sz.width
    grad = grad_ref[...]
    out_rows = 3 * sz.tiles * sz.cut
    turned_blocks(sz, ctx_ref[...], me, turned, blocks)
    output_grad = dot(blocks[...], grad)
    for j in range(sz.sections):
        put_tiles(pack, j, out_rows, output_grad[j * sz.cut : (j + 1) * sz.cut, :])
    turned_blocks(sz, normed[...], me, turned, blocks)
    after = 2 * sz.tiles
    for part in range(3):
        columns = slice(part * width, (part + 1) * width)
        grad_part = proj[:, columns]
        triple_grad = dot(blocks[...], grad_part)
        for j in range(sz.sections):
            put_tiles(pack, j, part * sz.tiles * sz.cut, triple_grad[j * sz.cut : (j + 1) * sz.cut, :])
        if part != 1:
            after = put_vector(small, after, jnp.sum(grad_part.astype(f32), axis=0, keepdims=True))
    total[...] = dot_last(proj[...], triple[...])
    gain_sum, shift_sum = norm_backward(sz, h_ref, grad_ref, total, gain, dh_ref)
    put_vector(small, 0, gain_sum)
    put_vector(small, sz.tiles, shift_sum)
    return put_vector(small, after, jnp.sum(grad.astype(f32), axis=0, keepdims=True))


def put_rows(sz, value, me, turned, blocks, keep, send):
    turned_blocks(sz, value, me, turned, blocks)
    for j in range(sz.sections):
        for tile in range(sz.rows // LANES):
            (keep, send)[j % 2][j // 2, tile * sz.cut : (tile + 1) * sz.cut, :] = blocks[
                j * sz.cut : (j + 1) * sz.cut, tile * LANES : (tile + 1) * LANES
            ]


def ship(exchange, me, replica, pack, rows, keep, send):
    size = rows // exchange.shards
    for shard in range(exchange.shards):
        offset = exchange.shard_of(replica) ^ shard
        for core in range(2):
            for across in range(2):
                options = [exchange.place(c, across, offset) for c in range(2)]
                place = jnp.where(me & 1 ^ core == 0, options[0], options[1])
                target = (keep, send)[core]
                target[pl.ds(pl.multiple_of(place * size, 16), size), :] = pack[
                    2 * across + core, shard * size : (shard + 1) * size, :
                ]


def put_small(pack, start, rows, small):
    held = small.shape[0]
    for j in range(pack.shape[0]):
        pack[j, start : start + held, :] = small[...].astype(bf16)
        if start + held < rows:
            pack[j, start + held : rows, :] = jnp.zeros((rows - start - held, LANES), bf16)


class Moves:
    def __init__(self, pairs, sems):
        self.copies = [pltpu.make_async_copy(source, target, sems.at[i]) for i, (source, target) in enumerate(pairs)]

    def start(self, *which):
        for i in which:
            self.copies[i].start()

    def wait(self, *which):
        for i in which:
            self.copies[i].wait()


def row_of(ref, layer):
    return ref[layer : layer + 1, :].astype(f32)


def pick_row(block, which):
    value = block[:, 0, :].astype(f32)
    for other in range(1, block.shape[1]):
        value = jnp.where(which == other, block[:, other, :].astype(f32), value)
    return value


def gather_rows(sz, of_global, of_local, crop, image, wide):
    wide[: sz.global_len, :] = pick_row(of_global, crop)
    for at in range(sz.locals):
        start = sz.global_len + at * sz.local_len
        wide[start : start + sz.local_len, :] = pick_row(of_local.at[at], image)
    wide[sz.used :, :] = jnp.zeros((sz.rows - sz.used, sz.width), f32)


def front_kernel(sz, *refs):
    rows_in, smalls_in, ratio_ref, weights_in, refs = refs[:4], refs[4:14], refs[14], refs[15:19], refs[19:]
    (
        s0, s1, s2, s3, n0, n1, n2, qkv0, qkv1, lse0, lse1, ctx0, ctx1, act0, act1, slope0, masked_ref, grad,
        triple0, triple1, output0, output1, up0, down0, down1, gain_a, gain_e, down_b, keep, send,
    ) = refs[:30]
    (
        up1, rank_ref, token_ref, shift_a, pair, output_b, shift_e, up_b, own_global, own_local, own_global_back,
        own_local_back, n3, slope1, wide, bias0, bias1, turned, blocks, pack, small, first_grad, load_sems,
    ) = refs[30:]
    own = (own_global, own_local, own_global_back, own_local_back)
    smalls = (rank_ref, token_ref, gain_a, shift_a, pair, output_b, gain_e, shift_e, up_b, down_b)
    weights = ((triple0, output0, up0, down0), (triple1, output1, up1, down1))
    me, replica = lax.axis_index("section"), lax.axis_index("dp")
    per_image = sz.sections // sz.images
    image, crop = me // per_image, me % per_image
    several = pl.ds(crop * sz.locals, sz.locals)
    places = [image, several, image, several]
    pairs = [(source.at[place], target) for source, place, target in zip(rows_in, places, own)]
    pairs += list(zip(smalls_in, smalls))
    pairs += [(weights_in[k].at[layer], weights[layer][k]) for layer in range(2) for k in range(4)]
    loads = Moves(pairs, load_sems)
    loads.start(0, 1, *range(4, 16))
    bias0[...] = window_bias(sz, 0)
    bias1[...] = window_bias(sz, 1)
    biases = (bias0, bias1)
    patches = sz.global_len - 1
    loads.wait(0, 1, *range(4, 14))
    loads.start(2, 3, *range(16, 22))
    limit = lax.div((ratio_ref[image] + 1) * patches, jnp.int32(10))
    both = rank_ref[image]
    entry = lax.broadcasted_iota(jnp.int32, both.shape, 0)
    ranks = jnp.sum(jnp.where(entry == crop, both, 0), axis=0, keepdims=True)
    shape = (sz.rows, patches)
    row = lax.broadcasted_iota(jnp.int32, shape, 0)
    column = lax.broadcasted_iota(jnp.int32, shape, 1)
    chosen = jnp.where((row == column + 1) & (ranks < limit), 1.0, 0.0)
    chosen = jnp.max(chosen, axis=-1, keepdims=True)
    masked_ref[...] = jnp.broadcast_to(chosen, masked_ref.shape)
    gather_rows(sz, own[0], own[1], crop, image, wide)
    s0[...] = jnp.where(chosen > 0.5, token_ref[...].astype(f32), wide[...]).astype(bf16)

    def attend_weights(layer):
        triple, output, _, _ = weights[layer]
        return (
            row_of(gain_a, layer), row_of(shift_a, layer), triple, row_of(pair, layer), output, row_of(output_b, layer),
        )

    def expand_weights(layer):
        return row_of(gain_e, layer), row_of(shift_e, layer), weights[layer][2], row_of(up_b, layer)

    loads.wait(14, 15)
    attend_forward(sz, s0, attend_weights(0), s1, n0, qkv0, lse0, ctx0, biases)
    loads.wait(16, 17)
    expand_hidden(sz, s1, expand_weights(0), n1, act0, slope0)
    s2[...] = expand_output(s1, act0, down0, row_of(down_b, 0)).astype(bf16)
    loads.wait(18, 19)
    attend_forward(sz, s2, attend_weights(1), s3, n2, qkv1, lse1, ctx1, biases)
    loads.wait(20, 21)
    expand_hidden(sz, s3, expand_weights(1), n3, act1, slope1)
    loads.wait(2, 3)
    gather_rows(sz, own[2], own[3], crop, image, wide)
    first_grad[...] = wide[...].astype(bf16)
    small[...] = jnp.zeros_like(small)
    expand_backward(
        sz, me, s3, n3, first_grad, act1, slope1, row_of(gain_e, 1), up1, down1, grad, (wide, turned, blocks), pack, small
    )
    rows = sz.packed(sz.expand_full)
    put_small(pack, sz.expand_full, rows, small)
    ship(sz.exchanges["A"], me, replica, pack, rows, keep, send)


def output_kernel(sz, h_ref, act_ref, down, down_b, out_keep, out_send, turned, blocks):
    me = lax.axis_index("section")
    last = expand_output(h_ref, act_ref, down, row_of(down_b, 1)).astype(bf16)
    put_rows(sz, last, me, turned, blocks, out_keep, out_send)


def expand_kernel(sz, h, normed, grad, act, slope, up, down, gain, dh_ref, keep, send, total, turned, blocks, pack, small):
    me, replica = lax.axis_index("section"), lax.axis_index("dp")
    small[...] = jnp.zeros_like(small)
    expand_backward(
        sz, me, h, normed, grad, act, slope, row_of(gain, 0), up, down, dh_ref, (total, turned, blocks), pack, small
    )
    rows = sz.packed(sz.expand_full)
    put_small(pack, sz.expand_full, rows, small)
    ship(sz.exchanges["C"], me, replica, pack, rows, keep, send)


def attend_core_kernel(sz, grad, output, qkv, lse, proj, dctx, bias0, bias1):
    bias0[...] = window_bias(sz, 0)
    bias1[...] = window_bias(sz, 1)
    attend_core_backward(sz, grad, output, qkv, lse, proj, dctx, (bias0, bias1))


def attend_kernel(sz, layer, *refs):
    h, normed, grad, ctx, proj, triple, gain, flags = refs[:8]
    if layer == 0:
        in_keep, in_send, keep, send, total, turned, blocks, pack, small = refs[8:]
        target = total
    else:
        target, keep, send, total, turned, blocks, pack, small = refs[8:]
    me, replica = lax.axis_index("section"), lax.axis_index("dp")
    small[...] = jnp.zeros_like(small)
    rows = sz.packed(sz.attend_full)
    after = attend_backward(
        sz, me, h, normed, grad, ctx, proj, row_of(gain, layer), triple, target, (total, turned, blocks), pack, small
    )
    if layer == 0:
        masked = flags[:, :1] > 0.5
        put_vector(small, after, jnp.sum(jnp.where(masked, total[...], 0.0), axis=0, keepdims=True))
        put_rows(sz, jnp.where(masked, 0.0, total[...]).astype(bf16), me, turned, blocks, in_keep, in_send)
    put_small(pack, sz.attend_full, rows, small)
    ship(sz.exchanges["DB"[layer]], me, replica, pack, rows, keep, send)


def unpack(exchange, me, replica, source, target):
    shard = target.shape[0] // exchange.shards
    for place in range(exchange.shards):
        options = [exchange.offset(core, place) for core in range(2)]
        offset = jnp.where(me & 1 == 0, options[0], options[1])
        at = pl.multiple_of((exchange.shard_of(replica) ^ offset) * shard, 16)
        target[pl.ds(at, shard), :] = source[place * shard : (place + 1) * shard, :]


def widen_tiles(source, base, target):
    r, columns = target.shape
    for tile in range(columns // LANES):
        target[:, tile * LANES : (tile + 1) * LANES] = source[base + tile * r : base + (tile + 1) * r, :].astype(f32)


def widen(sz, attend, expand, targets, moves):
    triple, output, up, down = targets
    hidden_rows = sz.hidden // LANES * sz.cut
    for index, (source, base, target) in enumerate(
        ((expand, 0, up), (expand, hidden_rows, down), (attend, 0, triple), (attend, 3 * sz.tiles * sz.cut, output))
    ):
        widen_tiles(source, base, target)
        moves[(2, 3, 0, 1)[index]].start()


def early_kernel(sz, *refs):
    (expand_in, attend_in), (out_own, out_core, in_own, in_core, across) = refs[:2], refs[2:7]
    (out_global, out_local, in_global, in_local), outs, vectors = refs[7:11], refs[11:15], refs[15]
    expand, attend, targets, wide, sems = refs[16], refs[17], refs[18:22], refs[22], refs[23]
    me, replica = lax.axis_index("section"), lax.axis_index("dp")
    moves = [pltpu.make_async_copy(target, out.at[1], sems.at[i]) for i, (target, out) in enumerate(zip(targets, outs))]
    unpack(sz.exchanges["A"], me, replica, expand_in, expand)
    unpack(sz.exchanges["B"], me, replica, attend_in, attend)
    widen(sz, attend, expand, targets, moves)
    vectors[: sz.small_rows, :] = attend[sz.attend_full : sz.attend_full + sz.small_rows, :].astype(f32)
    vectors[sz.small_rows :, :] = expand[sz.expand_full : sz.expand_full + sz.small_rows, :].astype(f32)
    row_parts = (
        (out_own.at[0], out_core.at[0], across.at[0], across.at[1]),
        (in_own.at[0], in_core.at[0], across.at[2], across.at[3]),
    )
    per_image = sz.sections // sz.images
    for which, (to_global, to_local) in enumerate(((out_global, out_local), (in_global, in_local))):
        for k in range(4):
            section = me ^ k
            image, crop = section // per_image, section % per_image
            turned = jnp.concatenate(
                [
                    row_parts[which][k][tile * sz.cut : (tile + 1) * sz.cut, :].astype(f32)
                    for tile in range(sz.rows // LANES)
                ],
                axis=1,
            )
            to_global[section] = turned[:, : sz.global_len]
            turned = jnp.concatenate([turned, jnp.zeros((LANES - sz.cut, sz.rows), f32)], axis=0)
            wide[...] = turned.T
            for at in range(sz.locals):
                start = sz.global_len + at * sz.local_len
                to_local[crop * sz.locals + at, :, pl.ds(image, 1), :] = wide[
                    start : start + sz.local_len, : sz.cut
                ].reshape(sz.local_len, 1, sz.cut)
    for move in moves:
        move.wait()


def finish_kernel(sz, *refs):
    expand_in, attend_in, later_vectors = refs[:3]
    (token, gain_a, shift_a, pair, output_b, gain_e, shift_e, up_b, down_b), outs = refs[7:16], refs[16:20]
    expand, attend, targets, vectors, sems = refs[20], refs[21], refs[22:26], refs[26], refs[27]
    me, replica = lax.axis_index("section"), lax.axis_index("dp")
    moves = [pltpu.make_async_copy(target, out.at[0], sems.at[i]) for i, (target, out) in enumerate(zip(targets, outs))]
    unpack(sz.exchanges["C"], me, replica, expand_in, expand)
    unpack(sz.exchanges["D"], me, replica, attend_in, attend)
    widen(sz, attend, expand, targets, moves)
    width, tiles, cut = sz.width, sz.tiles, sz.cut
    row = lax.broadcasted_iota(jnp.int32, (width, cut), 0)
    column = lax.broadcasted_iota(jnp.int32, (width, cut), 1)
    pick = jnp.where(row == column + me * cut, 1.0, 0.0).astype(bf16)
    row = lax.broadcasted_iota(jnp.int32, (2 * width, 2 * cut), 0)
    column = lax.broadcasted_iota(jnp.int32, (2 * width, 2 * cut), 1)
    pick_pair = jnp.where(row == column + me * 2 * cut, 1.0, 0.0).astype(bf16)
    hidden_tiles, up_tiles = sz.hidden // LANES, sz.hidden_cut // LANES
    vectors[: sz.small_rows, :] = attend[sz.attend_full : sz.attend_full + sz.small_rows, :].astype(f32)
    vectors[sz.small_rows :, :] = expand[sz.expand_full : sz.expand_full + sz.small_rows, :].astype(f32)
    for layer, held in enumerate((vectors, later_vectors)):
        one = slice(layer, layer + 1)

        def vector(at, tiles_in):
            return jnp.concatenate([held[at + t : at + t + 1, :] for t in range(tiles_in)], axis=1)

        def picked(at):
            return dot(vector(at, tiles).astype(bf16), pick)

        gain_a[one, :] = picked(0)
        shift_a[one, :] = picked(tiles)
        pair[one, :] = dot(vector(2 * tiles, 2 * tiles).astype(bf16), pick_pair)
        output_b[one, :] = picked(4 * tiles)
        if layer == 0:
            token[...] = picked(5 * tiles)
        base = sz.small_rows
        gain_e[one, :] = picked(base)
        shift_e[one, :] = picked(base + tiles)
        for tile in range(up_tiles):
            up_b[one, tile * LANES : (tile + 1) * LANES] = held[pl.ds(base + 2 * tiles + me * up_tiles + tile, 1), :]
        down_b[one, :] = picked(base + 2 * tiles + hidden_tiles)
    for move in moves:
        move.wait()


VMEM = pl.BlockSpec(memory_space=pltpu.VMEM)
ANY = pl.BlockSpec(memory_space=pl.ANY)
HBM = pl.BlockSpec(memory_space=pltpu.HBM)
SMEM = pl.BlockSpec(memory_space=pltpu.SMEM)
DMA = pltpu.SemaphoreType.DMA


def call(body, name, outs, in_specs, scratch, args, flops, aliases=()):
    args = [
        pltpu.with_memory_space_constraint(arg, pltpu.HBM) if spec is HBM else arg for arg, spec in zip(args, in_specs)
    ]
    return pl.pallas_call(
        body,
        name=name,
        out_shape=tuple(jax.ShapeDtypeStruct(shape, kind) for shape, kind, _ in outs),
        in_specs=in_specs,
        out_specs=tuple(memory for _, _, memory in outs),
        scratch_shapes=[pltpu.VMEM(*item) if isinstance(item, tuple) else item for item in scratch],
        input_output_aliases=dict(aliases),
        compiler_params=pltpu.CompilerParams(vmem_limit_bytes=VMEM_MIB.get(name, 14) << 20),
        cost_estimate=pl.CostEstimate(flops=flops, bytes_accessed=1 << 20, transcendentals=0),
    )(*args)


def add(first, *others):
    total = first.astype(f32)
    for other in others:
        total = total + other.astype(f32)
    return lax.reduce_precision(total, 8, 7).astype(bf16)


def swap(value, partner_of):
    sections, replicas = lax.axis_size("section"), lax.axis_size("dp")
    route = []
    for section in range(sections):
        for replica in range(replicas):
            to_section, to_replica = partner_of(section, replica)
            route.append((section * replicas + replica, to_section * replicas + to_replica))
    return lax.ppermute(value, ("section", "dp"), route)


def other_core(section, replica):
    return section ^ 1, replica


def other_x(section, replica):
    return section ^ 2, replica


def along(orders, step):
    def partner_of(section, replica):
        axis = orders[section & 1][step]
        return (section ^ 2, replica) if axis == X_AXIS else (section, replica ^ (1 << axis))

    return partner_of


class Sequence:
    def __init__(self):
        self.last = None

    def after(self, value):
        return value if self.last is None else lax.optimization_barrier((value, self.last))[0]

    def mark(self, value):
        self.last = value
        return value


def reduce_steps(exchange, order, keep, send):
    orders = exchange.orders
    core = swap(send, other_core)
    yield
    core = order.after(core)
    half = keep.shape[0] // 2
    moved = swap(order.mark(add(keep[half:], core[half:])), along(orders, 0))
    yield
    moved = order.after(moved)
    mine = add(keep[:half], core[:half], moved)
    for step in range(1, len(orders[0])):
        half = mine.shape[0] // 2
        moved = swap(order.mark(mine[half:]), along(orders, step))
        yield
        mine = add(mine[:half], order.after(moved))
    for axis in exchange.rest:
        moved = swap(order.mark(mine), along(([axis], [axis]), 0))
        yield
        mine = add(mine, order.after(moved))
    back = [[axis for axis in order_of if axis != X_AXIS] for order_of in orders]
    for step in reversed(range(len(back[0]))):
        moved = swap(order.mark(mine), along(back, step))
        yield
        mine = jnp.concatenate([mine, order.after(moved)], axis=0)
    yield mine


def row_steps(order, out_rows, in_rows):
    cores = [swap(send, other_core) for _, send in (out_rows, in_rows)]
    yield
    cores[0] = order.after(cores[0])
    across = swap(order.mark(jnp.stack([out_rows[0][1], cores[0][1], in_rows[0][1], cores[1][1]])), other_x)
    yield
    yield out_rows[0], cores[0], in_rows[0], cores[1], order.after(across)


def per_device(
    global_rows, local_rows, patch_rank, ratio_bin, mask_token, attend_gain, attend_shift, triple_weight,
    pair_bias, output_weight, output_bias, expand_gain, expand_shift, up_weight, up_bias, down_weight,
    down_bias, grad_global, grad_local,
):
    sections, replicas = lax.axis_size("section"), lax.axis_size("dp")
    sz = Sizes(global_rows, local_rows, up_weight, sections, replicas)
    width, rows, hidden = sz.width, sz.rows, sz.hidden
    sets = [rows_of.transpose(0, 2, 1, 3) for rows_of in (global_rows, grad_global)]
    many = [rows_of.transpose(1, 2, 0, 3) for rows_of in (local_rows, grad_local)]
    weights = (triple_weight, output_weight, up_weight, down_weight)
    smalls = (
        patch_rank, mask_token, attend_gain, attend_shift, pair_bias, output_bias, expand_gain, expand_shift, up_bias,
        down_bias,
    )
    wide = ((rows, width), bf16)
    triple_rows = ((rows, 3 * width), bf16)
    hidden_rows = ((rows, hidden), bf16)
    lse = ((16, up_to(max(length for _, length in sz.windows), LANES)), f32)
    flags = ((rows, LANES), f32)
    wide_f32 = ((rows, width), f32)
    turned = ((width, rows), bf16)
    small = ((sz.small_rows, LANES), f32)
    share = ((2, sz.extra, LANES), bf16)
    stage = ((sections, sz.extra, LANES), bf16)
    windows = [((length, length), f32) for _, length in sz.windows]
    totals = [sz.packed(full) for full in (sz.expand_full, sz.attend_full)]
    packs = [((sections, total, LANES), bf16) for total in totals]
    parts = [((2 * total, LANES), bf16) for total in totals]
    vectors = ((2, width), bf16)
    blocks = [(weight.shape[1:], bf16) for weight in weights]
    shared = [wide_f32, turned, turned]

    def run_kernel(body, name, outs, scratch, args):
        return call(
            lambda *refs: body(sz, *refs), name, [out + (VMEM,) for out in outs], [VMEM] * len(args), scratch, args, 4 << 30
        )

    (
        s0, s1, s2, s3, n0, n1, n2, qkv0, qkv1, lse0, lse1, ctx0, ctx1, act0, act1, slope0, masked, grad,
        triple0, triple1, output0, output1, up0, down0, down1, gain_a, gain_e, down_b, keep, send,
    ) = call(
        lambda *refs: front_kernel(sz, *refs),
        "front",
        [
            out + (VMEM,)
            for out in [wide] * 7 + [triple_rows] * 2 + [lse] * 2 + [wide] * 2 + [hidden_rows] * 3 + [flags, wide]
            + [blocks[0]] * 2 + [blocks[1]] * 2 + [blocks[2]] + [blocks[3]] * 2 + [vectors] * 3 + [parts[0]] * 2
        ],
        [HBM] * 14 + [SMEM] + [HBM] * 4,
        [blocks[2]]
        + [(one.shape, one.dtype) for one in (patch_rank, mask_token, attend_shift, pair_bias, output_bias)]
        + [(one.shape, one.dtype) for one in (expand_shift, up_bias)]
        + [(sets[0].shape[1:], bf16), ((sz.locals,) + many[0].shape[1:], bf16)] * 2
        + [wide, hidden_rows, wide_f32] + windows + [turned] * 2 + [packs[0], small, wide, DMA((22,))],
        (sets[0], many[0], sets[1], many[1], *smalls, ratio_bin, *weights),
        8 << 30,
    )
    order = Sequence()
    chains, results = {}, {}
    chains["A"] = reduce_steps(sz.exchanges["A"], order, keep, send)
    core_scratch = [wide] + windows
    flow = {"grad": grad}

    def core_kernel(name, output, qkv, lse_of):
        proj, = run_kernel(
            attend_core_kernel, name, [triple_rows], core_scratch, (order.after(flow["grad"]), output, qkv, lse_of)
        )
        flow["proj"] = order.mark(proj)

    def later_core():
        core_kernel("later_core", output1, qkv1, lse1)

    def later_attend():
        dh, keep, send = run_kernel(
            lambda sz, *refs: attend_kernel(sz, 1, *refs), "later_attend", [wide] + [parts[1]] * 2,
            shared + [packs[1], small],
            (s2, n2, flow["grad"], ctx1, order.after(flow["proj"]), triple1, gain_a, masked),
        )
        flow["grad"] = order.mark(dh)
        chains["B"] = reduce_steps(sz.exchanges["B"], order, keep, send)

    def expand():
        dh, keep, send = run_kernel(
            expand_kernel, "expand_back", [wide] + [parts[0]] * 2, shared + [packs[0], small],
            (s1, n1, order.after(flow["grad"]), act0, slope0, up0, down0, gain_e),
        )
        flow["grad"] = order.mark(dh)
        chains["C"] = reduce_steps(sz.exchanges["C"], order, keep, send)

    def core():
        core_kernel("attend_core", output0, qkv0, lse0)

    def attend():
        in_keep, in_send, keep, send = run_kernel(
            lambda sz, *refs: attend_kernel(sz, 0, *refs), "attend_back", [share] * 2 + [parts[1]] * 2,
            shared + [packs[1], small],
            (s0, n0, flow["grad"], ctx0, order.after(flow["proj"]), triple0, gain_a, masked),
        )
        flow["in"] = (order.mark(in_keep), in_send)
        chains["D"] = reduce_steps(sz.exchanges["D"], order, keep, send)

    def output_rows():
        out_rows = run_kernel(
            output_kernel, "output_rows", [share] * 2, [turned, turned], (s3, order.after(act1), down1, down_b)
        )
        order.mark(out_rows[0])
        chains["R"] = row_steps(order, out_rows, flow["in"])

    cut = sz.cut
    weight_outs = [(2, cut, 3 * width), (2, cut, width), (2, cut, hidden), (2, sz.hidden_cut, width)]
    row_outs = [(sz.all_globals, cut, sz.global_len), local_rows.shape[1:3] + (sz.images, cut)] * 2
    both_small = ((2 * sz.small_rows, LANES), f32)
    finish_scratch = [((total, LANES), bf16) for total in totals] + [(shape[1:], f32) for shape in weight_outs]

    def early():
        expand_of, attend_of = (order.after(results[step]) for step in "AB")
        flow["early"] = call(
            lambda *refs: early_kernel(sz, *refs), "early",
            [(shape, f32, VMEM) for shape in row_outs] + [(shape, f32, ANY) for shape in weight_outs] + [both_small + (VMEM,)],
            [VMEM] * 7, finish_scratch + [flags, DMA((4,))], (expand_of, attend_of, *results["R"]), 1 << 28,
        )
        order.mark(flow["early"][-1])

    kernels = {
        "later_core": later_core, "later_attend": later_attend, "expand": expand, "core": core, "attend": attend,
        "output": output_rows, "early": early,
    }
    for plan in PLAN:
        for step in plan.split():
            if step == "early":
                for _ in range(3, len(sz.exchanges["A"].rest) + len(sz.exchanges["A"].axes)):
                    for name in "ABCD":
                        results[name] = next(chains[name], results.get(name))
            if step in kernels:
                kernels[step]()
            else:
                results[step] = next(chains[step], results.get(step))
    *row_values, triple, output, up, down, late_vectors = flow["early"]
    vector_outs = [(1, cut), (2, cut), (2, cut), (2, 2 * cut)] + [(2, cut)] * 3 + [(2, sz.hidden_cut), (2, cut)]
    final = call(
        lambda *refs: finish_kernel(sz, *refs), "finish",
        [(shape, f32, VMEM) for shape in vector_outs] + [(shape, f32, ANY) for shape in weight_outs],
        [VMEM] * 3 + [ANY] * 4, finish_scratch + [both_small, DMA((4,))],
        (order.after(results["C"]), results["D"], late_vectors, triple, output, up, down), 1 << 28,
        [(3 + i, len(vector_outs) + i) for i in range(4)],
    )
    token, gain_a, shift_a, pair, output_b, gain_e, shift_e, up_b, down_b, triple, output, up, down = final
    shape = global_rows.shape[:2] + (cut, sz.global_len)
    return (
        row_values[0].reshape(shape).transpose(0, 1, 3, 2), row_values[1].transpose(2, 0, 1, 3),
        row_values[2].reshape(shape).transpose(0, 1, 3, 2), row_values[3].transpose(2, 0, 1, 3),
        token, gain_a, shift_a, triple, pair, output, output_b, gain_e, shift_e, up, up_b, down, down_b,
    )


def solution(mesh):
    rows, copied = P("dp", None, None, None), P()
    in_specs = (rows, rows, P("dp", None, None), P("dp")) + (copied,) * 13 + (rows, rows)
    wide, flat, deep = P("dp", None, None, "section"), P(None, "section"), P(None, "section", None)
    out_specs = (
        wide, wide, wide, wide, flat, flat, flat, deep, flat, deep, flat, flat, flat, deep, flat, deep, flat,
    )
    return jax.shard_map(per_device, mesh=mesh, in_specs=in_specs, out_specs=out_specs, check_vma=False)
```

```python
import math

import jax
import jax.numpy as jnp
from jax import lax
from jax.experimental import pallas as pl
from jax.experimental.pallas import tpu as pltpu
from jax.sharding import PartitionSpec as P

HEADS = 6
EPS = 1e-06
LANES = 128
VMEM_MIB = {"front": 26, "finish": 20}
CHOICES = (0, 0, 1, 0)
PLAN = (
    "A later_core later_attend A",
    "expand core C B",
    "A C B attend",
    "D C D A",
    "B output R A",
    "B D C B",
    "A C D B",
    "A D C R",
    "B D C R",
    "D A C B",
    "D A B R",
    "early C D",
)
X_AXIS = -1

f32 = jnp.float32
bf16 = jnp.bfloat16


def up_to(value, step):
    return (value + step - 1) // step * step


class Sizes:
    def __init__(self, global_rows, local_rows, up_weight, sections, replicas):
        images, crops, self.global_len, self.width = global_rows.shape
        _, local_crops, self.local_len, _ = local_rows.shape
        self.hidden = up_weight.shape[2]
        self.sections = sections
        self.replicas = replicas
        self.images = images
        self.all_globals = images * crops
        self.all_locals = images * local_crops
        self.locals = self.all_locals // sections
        self.used = self.global_len + self.locals * self.local_len
        self.rows = up_to(self.used, LANES)
        self.head = self.width // HEADS
        self.cut = self.width // sections
        self.hidden_cut = self.hidden // sections
        self.tiles = self.width // LANES
        self.first_end = up_to(self.global_len, 16)
        self.second_start = self.global_len // 16 * 16
        self.windows = (
            (0, self.first_end),
            (self.second_start, self.rows - self.second_start),
        )
        self.attend_full = 4 * self.tiles * self.cut
        self.expand_full = self.hidden // LANES * self.cut + self.tiles * self.hidden_cut
        self.small_rows = up_to(max(6 * self.tiles, 3 * self.tiles + self.hidden // LANES), 16)
        self.extra = self.cut * self.rows // LANES
        bits = replicas.bit_length() - 1
        low = list(range(min(bits, 2)))
        last_first = low[1:] + [X_AXIS] + low[:1]
        first_last = [X_AXIS] + low
        middle = low[:1] + [X_AXIS] + low[1:]
        choices = (
            (first_last, last_first), (middle, last_first), (first_last, middle), ([X_AXIS] + low[1:], low[1:] + [X_AXIS])
        )
        self.exchanges = {name: Exchange(choices[choice], bits) for name, choice in zip("ABCD", CHOICES)}
        self.unit = 16 << len(low)

    def packed(self, full):
        return up_to(full + self.small_rows, self.unit)


class Exchange:
    def __init__(self, orders, bits):
        self.orders = orders
        self.axes = sorted(axis for axis in orders[0] if axis != X_AXIS)
        self.rest = [axis for axis in range(bits) if axis not in self.axes]
        self.shards = 1 << len(self.axes)

    def shard_of(self, replica):
        return sum((replica >> axis & 1) << i for i, axis in enumerate(self.axes))

    def place(self, core, across, offset):
        order = self.orders[core]
        return sum(
            (across if axis == X_AXIS else offset >> self.axes.index(axis) & 1) << (len(order) - 1 - at)
            for at, axis in enumerate(order)
        )

    def offset(self, core, place):
        order = [axis for axis in self.orders[core] if axis != X_AXIS]
        return sum((place >> (len(order) - 1 - at) & 1) << self.axes.index(axis) for at, axis in enumerate(order))


def dot(a, b):
    return jnp.dot(a, b, preferred_element_type=f32)


def dot_last(a, b):
    return lax.dot_general(a, b, (((1,), (1,)), ((), ())), preferred_element_type=f32)


def dot_first(a, b):
    return lax.dot_general(a, b, (((0,), (0,)), ((), ())), preferred_element_type=f32)


def normalize(hidden):
    average = jnp.mean(hidden, axis=-1, keepdims=True)
    centred = hidden - average
    inverse = lax.rsqrt(jnp.mean(centred * centred, axis=-1, keepdims=True) + EPS)
    return centred * inverse, inverse


def row_blocks(sz):
    return [slice(i, i + LANES) for i in range(0, sz.rows, LANES)]


def head_mask(sz, rows, which):
    lane = lax.broadcasted_iota(jnp.int32, (rows, 2 * sz.head), 1)
    return lane < sz.head if which == 0 else lane >= sz.head


def window_bias(sz, which):
    start, length = sz.windows[which]

    def group(row):
        if which == 0:
            return jnp.where(row < sz.global_len, 0, 1)
        kind = jnp.where(row + start < sz.global_len, 0, 1)
        for crop in range(1, sz.locals + 1):
            kind = kind + jnp.where(row + start >= sz.global_len + crop * sz.local_len, 1, 0)
        return kind

    left = group(lax.broadcasted_iota(jnp.int32, (length, length), 0))
    right = group(lax.broadcasted_iota(jnp.int32, (length, length), 1))
    return jnp.where(left == right, 0.0, -1e30).astype(f32)


def own_rows(sz, which):
    start, length = sz.windows[which]
    row = lax.broadcasted_iota(jnp.int32, (length, 1), 0) + start
    return row < sz.global_len if which == 0 else row >= sz.global_len


def store_window(sz, which, ref, columns, value):
    start, length = sz.windows[which]
    if which == 0 or sz.first_end == start:
        ref[start : start + length, columns] = value.astype(bf16)
        return
    shared = sz.first_end - start
    row = lax.broadcasted_iota(jnp.int32, (shared, value.shape[1]), 0) + start
    before = ref[start : sz.first_end, columns].astype(f32)
    ref[start : sz.first_end, columns] = jnp.where(
        row < sz.global_len, before, value[:shared]
    ).astype(bf16)
    ref[sz.first_end : start + length, columns] = value[shared:].astype(bf16)


def norm_rows(sz, h_ref, gain, shift, normed_ref):
    for rows in row_blocks(sz):
        scaled, _ = normalize(h_ref[rows, :].astype(f32))
        normed_ref[rows, :] = (scaled * gain + shift).astype(bf16)


def stacked_heads(sz, value):
    zero = jnp.zeros_like(value)
    return jnp.concatenate([jnp.where(head_mask(sz, value.shape[0], which), value, zero) for which in range(2)], axis=0)


def attend_forward(sz, h_ref, weights, out_ref, normed_ref, qkv_ref, lse_ref, ctx_ref, bias_refs):
    gain, shift, triple_ref, pair_bias, output_ref, output_bias = weights
    width = sz.width
    norm_rows(sz, h_ref, gain, shift, normed_ref)
    scale = 1.0 / math.sqrt(sz.head)
    for part in range(3):
        columns = slice(part * width, (part + 1) * width)
        project = dot(normed_ref[...], triple_ref[:, columns])
        if part == 0:
            project = (project + pair_bias[:, :width]) * scale
        if part == 2:
            project = project + pair_bias[:, width:]
        qkv_ref[:, columns] = project.astype(bf16)
    for which, (start, length) in enumerate(sz.windows):
        rows = slice(start, start + length)
        bias = bias_refs[which]
        lane = lax.broadcasted_iota(jnp.int32, (length, LANES), 1)
        first = head_mask(sz, length, 0)
        kept = jnp.zeros((length, LANES), f32)
        for pair in range(HEADS // 2):
            at = 2 * sz.head * pair
            queries, keys, values = (
                qkv_ref[rows, part * width + at : part * width + at + 2 * sz.head] for part in range(3)
            )
            scores = dot_last(stacked_heads(sz, queries), keys)
            probs = []
            for which_head in range(2):
                own = scores[which_head * length : (which_head + 1) * length] + bias[...]
                top = jnp.max(own, axis=-1, keepdims=True)
                raised = jnp.exp(own - top)
                total = jnp.sum(raised, axis=-1, keepdims=True)
                kept = jnp.where(lane == 2 * pair + which_head, top + jnp.log(total), kept)
                probs.append((raised * (1.0 / total)).astype(bf16))
            context = dot(jnp.concatenate(probs, axis=0), values)
            store_window(
                sz, which, ctx_ref, slice(at, at + 2 * sz.head), jnp.where(first, context[:length], context[length:])
            )
        lse_ref[8 * which : 8 * which + 8, :length] = kept.T[:8]
    moved = dot(ctx_ref[...], output_ref[...]) + output_bias
    out_ref[...] = (h_ref[...].astype(f32) + moved).astype(bf16)


def expand_hidden(sz, h_ref, weights, normed_ref, active_ref, slope_ref):
    gain, shift, up_ref, up_bias = weights
    norm_rows(sz, h_ref, gain, shift, normed_ref)
    for at in range(0, sz.hidden, sz.hidden_cut):
        columns = slice(at, at + sz.hidden_cut)
        before = dot(normed_ref[...], up_ref[:, columns]) + up_bias[:, columns]
        share = 0.5 + 0.5 * lax.erf(before * math.sqrt(0.5))
        active_ref[:, columns] = (before * share).astype(bf16)
        density = jnp.exp(before * before * -0.5) * (1.0 / math.sqrt(2.0 * math.pi))
        slope_ref[:, columns] = (share + before * density).astype(bf16)


def expand_output(h_ref, active_ref, down_ref, down_bias):
    return h_ref[...].astype(f32) + dot(active_ref[...], down_ref[...]) + down_bias


def turned_blocks(sz, value, me, turned_ref, blocks_ref):
    turned_ref[...] = value.T
    for j in range(sz.sections):
        source = pl.multiple_of((me ^ j) * sz.cut, sz.cut)
        blocks_ref[j * sz.cut : (j + 1) * sz.cut, :] = turned_ref[pl.ds(source, sz.cut), :]


def put_vector(small, at, vector):
    for tile in range(vector.shape[1] // LANES):
        small[at + tile : at + tile + 1, :] = vector[:, tile * LANES : (tile + 1) * LANES]
    return at + vector.shape[1] // LANES


def put_tiles(pack, j, at, value):
    r = value.shape[0]
    for tile in range(value.shape[1] // LANES):
        pack[j, pl.ds(at + tile * r, r), :] = value[:, tile * LANES : (tile + 1) * LANES].astype(bf16)


def norm_backward(sz, h_ref, grad_ref, grad_normed_ref, gain, dh_ref):
    gain_sum = jnp.zeros((1, sz.width), f32)
    shift_sum = jnp.zeros((1, sz.width), f32)
    for rows in row_blocks(sz):
        scaled, inverse = normalize(h_ref[rows, :].astype(f32))
        grad_normed = grad_normed_ref[rows, :]
        grad_scaled = grad_normed * gain
        first = jnp.mean(grad_scaled, axis=-1, keepdims=True)
        second = jnp.mean(grad_scaled * scaled, axis=-1, keepdims=True)
        grad_in = inverse * (grad_scaled - first - scaled * second)
        dh_ref[rows, :] = (grad_ref[rows, :].astype(f32) + grad_in).astype(dh_ref.dtype)
        gain_sum += jnp.sum(grad_normed * scaled, axis=0, keepdims=True)
        shift_sum += jnp.sum(grad_normed, axis=0, keepdims=True)
    return gain_sum, shift_sum


def expand_backward(sz, me, h_ref, normed, grad_ref, act_ref, slope_ref, gain, up, down, dh_ref, scratch, pack, small):
    total, turned, blocks = scratch
    base = 0
    part = sz.hidden_cut
    up_rows = sz.hidden // LANES * sz.cut
    turned_blocks(sz, normed[...], me, turned, blocks)
    after = 2 * sz.tiles
    for j in range(sz.sections):
        owner = me ^ j
        columns = pl.ds(pl.multiple_of(owner * part, LANES), part)
        put_tiles(pack, j, base + up_rows, dot_first(act_ref[:, columns], grad_ref[...]))
        grad_active = dot_last(grad_ref[...], down[columns, :])
        grad_before = (grad_active * slope_ref[:, columns].astype(f32)).astype(bf16)
        up_sum = jnp.sum(grad_before.astype(f32), axis=0, keepdims=True)
        for tile in range(part // LANES):
            small[pl.ds(after + owner * (part // LANES) + tile, 1), :] = up_sum[:, tile * LANES : (tile + 1) * LANES]
        up_grad = dot(blocks[...], grad_before)
        at = base + pl.multiple_of(owner * (part // LANES * sz.cut), 16)
        for other in range(sz.sections):
            put_tiles(pack, other, at, up_grad[other * sz.cut : (other + 1) * sz.cut, :])
        more = dot_last(grad_before, up[:, columns])
        if j == 0:
            total[...] = more
        else:
            total[...] += more
    gain_sum, shift_sum = norm_backward(sz, h_ref, grad_ref, total, gain, dh_ref)
    put_vector(small, 0, gain_sum)
    put_vector(small, sz.tiles, shift_sum)
    put_vector(
        small, after + sz.hidden // LANES, jnp.sum(grad_ref[...].astype(f32), axis=0, keepdims=True)
    )


def attend_core_backward(sz, grad_ref, output, qkv_ref, lse_ref, proj, dctx, bias_refs):
    width = sz.width
    dctx[...] = dot_last(grad_ref[...], output[...]).astype(bf16)
    scale = 1.0 / math.sqrt(sz.head)
    for which, (start, length) in enumerate(sz.windows):
        rows = slice(start, start + length)
        bias = bias_refs[which]
        own = own_rows(sz, which)
        for pair in range(HEADS // 2):
            at = 2 * sz.head * pair
            columns = [slice(part * width + at, part * width + at + 2 * sz.head) for part in range(3)]
            queries, keys, values = (qkv_ref[rows, c] for c in columns)
            grad_ctx = jnp.where(own, dctx[rows, columns[0]], jnp.zeros((length, 2 * sz.head), bf16))
            keys = stacked_heads(sz, keys)
            scores = dot_last(keys, queries)
            grad_probs = dot_last(stacked_heads(sz, values), grad_ctx)
            probs, grad_scores = [], []
            for which_head in range(2):
                part = slice(which_head * length, (which_head + 1) * length)
                row = 8 * which + 2 * pair + which_head
                prob = jnp.exp(scores[part] + bias[...] - lse_ref[row : row + 1, :length])
                grad_prob = grad_probs[part]
                delta = jnp.sum(prob * grad_prob, axis=0, keepdims=True)
                grad_scores.append((prob * (grad_prob - delta)).astype(bf16))
                probs.append(prob.astype(bf16))
            grad_scores = jnp.concatenate(grad_scores, axis=0)
            first = head_mask(sz, length, 0)
            grad_keys = dot(grad_scores, queries)
            grad_values = dot(jnp.concatenate(probs, axis=0), grad_ctx)
            store_window(sz, which, proj, columns[0], dot_first(grad_scores, keys) * scale)
            store_window(sz, which, proj, columns[1], jnp.where(first, grad_keys[:length], grad_keys[length:]))
            store_window(sz, which, proj, columns[2], jnp.where(first, grad_values[:length], grad_values[length:]))


def attend_backward(sz, me, h_ref, normed, grad_ref, ctx_ref, proj, gain, triple, dh_ref, scratch, pack, small):
    total, turned, blocks = scratch
    width = sz.width
    grad = grad_ref[...]
    out_rows = 3 * sz.tiles * sz.cut
    turned_blocks(sz, ctx_ref[...], me, turned, blocks)
    output_grad = dot(blocks[...], grad)
    for j in range(sz.sections):
        put_tiles(pack, j, out_rows, output_grad[j * sz.cut : (j + 1) * sz.cut, :])
    turned_blocks(sz, normed[...], me, turned, blocks)
    after = 2 * sz.tiles
    for part in range(3):
        columns = slice(part * width, (part + 1) * width)
        grad_part = proj[:, columns]
        triple_grad = dot(blocks[...], grad_part)
        for j in range(sz.sections):
            put_tiles(pack, j, part * sz.tiles * sz.cut, triple_grad[j * sz.cut : (j + 1) * sz.cut, :])
        if part != 1:
            after = put_vector(small, after, jnp.sum(grad_part.astype(f32), axis=0, keepdims=True))
    total[...] = dot_last(proj[...], triple[...])
    gain_sum, shift_sum = norm_backward(sz, h_ref, grad_ref, total, gain, dh_ref)
    put_vector(small, 0, gain_sum)
    put_vector(small, sz.tiles, shift_sum)
    return put_vector(small, after, jnp.sum(grad.astype(f32), axis=0, keepdims=True))


def put_rows(sz, value, me, turned, blocks, keep, send):
    turned_blocks(sz, value, me, turned, blocks)
    for j in range(sz.sections):
        for tile in range(sz.rows // LANES):
            (keep, send)[j % 2][j // 2, tile * sz.cut : (tile + 1) * sz.cut, :] = blocks[
                j * sz.cut : (j + 1) * sz.cut, tile * LANES : (tile + 1) * LANES
            ]


def ship(exchange, me, replica, pack, rows, keep, send):
    size = rows // exchange.shards
    for shard in range(exchange.shards):
        offset = exchange.shard_of(replica) ^ shard
        for core in range(2):
            for across in range(2):
                options = [exchange.place(c, across, offset) for c in range(2)]
                place = jnp.where(me & 1 ^ core == 0, options[0], options[1])
                target = (keep, send)[core]
                target[pl.ds(pl.multiple_of(place * size, 16), size), :] = pack[
                    2 * across + core, shard * size : (shard + 1) * size, :
                ]


def put_small(pack, start, rows, small):
    held = small.shape[0]
    for j in range(pack.shape[0]):
        pack[j, start : start + held, :] = small[...].astype(bf16)
        if start + held < rows:
            pack[j, start + held : rows, :] = jnp.zeros((rows - start - held, LANES), bf16)


class Moves:
    def __init__(self, pairs, sems):
        self.copies = [pltpu.make_async_copy(source, target, sems.at[i]) for i, (source, target) in enumerate(pairs)]

    def start(self, *which):
        for i in which:
            self.copies[i].start()

    def wait(self, *which):
        for i in which:
            self.copies[i].wait()


def row_of(ref, layer):
    return ref[layer : layer + 1, :].astype(f32)


def pick_row(block, which):
    value = block[:, 0, :].astype(f32)
    for other in range(1, block.shape[1]):
        value = jnp.where(which == other, block[:, other, :].astype(f32), value)
    return value


def gather_rows(sz, of_global, of_local, crop, image, wide):
    wide[: sz.global_len, :] = pick_row(of_global, crop)
    for at in range(sz.locals):
        start = sz.global_len + at * sz.local_len
        wide[start : start + sz.local_len, :] = pick_row(of_local.at[at], image)
    wide[sz.used :, :] = jnp.zeros((sz.rows - sz.used, sz.width), f32)


def front_kernel(sz, *refs):
    rows_in, smalls_in, ratio_ref, weights_in, refs = refs[:4], refs[4:14], refs[14], refs[15:19], refs[19:]
    (
        s0, s1, s2, s3, n0, n1, n2, qkv0, qkv1, lse0, lse1, ctx0, ctx1, act0, act1, slope0, masked_ref, grad,
        triple0, triple1, output0, output1, up0, down0, down1, gain_a, gain_e, down_b, keep, send,
    ) = refs[:30]
    (
        up1, rank_ref, token_ref, shift_a, pair, output_b, shift_e, up_b, own_global, own_local, own_global_back,
        own_local_back, n3, slope1, wide, bias0, bias1, turned, blocks, pack, small, first_grad, load_sems,
    ) = refs[30:]
    own = (own_global, own_local, own_global_back, own_local_back)
    smalls = (rank_ref, token_ref, gain_a, shift_a, pair, output_b, gain_e, shift_e, up_b, down_b)
    weights = ((triple0, output0, up0, down0), (triple1, output1, up1, down1))
    me, replica = lax.axis_index("section"), lax.axis_index("dp")
    per_image = sz.sections // sz.images
    image, crop = me // per_image, me % per_image
    several = pl.ds(crop * sz.locals, sz.locals)
    places = [image, several, image, several]
    pairs = [(source.at[place], target) for source, place, target in zip(rows_in, places, own)]
    pairs += list(zip(smalls_in, smalls))
    pairs += [(weights_in[k].at[layer], weights[layer][k]) for layer in range(2) for k in range(4)]
    loads = Moves(pairs, load_sems)
    loads.start(0, 1, *range(4, 16))
    bias0[...] = window_bias(sz, 0)
    bias1[...] = window_bias(sz, 1)
    biases = (bias0, bias1)
    patches = sz.global_len - 1
    loads.wait(0, 1, *range(4, 14))
    loads.start(2, 3, *range(16, 22))
    limit = lax.div((ratio_ref[image] + 1) * patches, jnp.int32(10))
    both = rank_ref[image]
    entry = lax.broadcasted_iota(jnp.int32, both.shape, 0)
    ranks = jnp.sum(jnp.where(entry == crop, both, 0), axis=0, keepdims=True)
    shape = (sz.rows, patches)
    row = lax.broadcasted_iota(jnp.int32, shape, 0)
    column = lax.broadcasted_iota(jnp.int32, shape, 1)
    chosen = jnp.where((row == column + 1) & (ranks < limit), 1.0, 0.0)
    chosen = jnp.max(chosen, axis=-1, keepdims=True)
    masked_ref[...] = jnp.broadcast_to(chosen, masked_ref.shape)
    gather_rows(sz, own[0], own[1], crop, image, wide)
    s0[...] = jnp.where(chosen > 0.5, token_ref[...].astype(f32), wide[...]).astype(bf16)

    def attend_weights(layer):
        triple, output, _, _ = weights[layer]
        return (
            row_of(gain_a, layer), row_of(shift_a, layer), triple, row_of(pair, layer), output, row_of(output_b, layer),
        )

    def expand_weights(layer):
        return row_of(gain_e, layer), row_of(shift_e, layer), weights[layer][2], row_of(up_b, layer)

    loads.wait(14, 15)
    attend_forward(sz, s0, attend_weights(0), s1, n0, qkv0, lse0, ctx0, biases)
    loads.wait(16, 17)
    expand_hidden(sz, s1, expand_weights(0), n1, act0, slope0)
    s2[...] = expand_output(s1, act0, down0, row_of(down_b, 0)).astype(bf16)
    loads.wait(18, 19)
    attend_forward(sz, s2, attend_weights(1), s3, n2, qkv1, lse1, ctx1, biases)
    loads.wait(20, 21)
    expand_hidden(sz, s3, expand_weights(1), n3, act1, slope1)
    loads.wait(2, 3)
    gather_rows(sz, own[2], own[3], crop, image, wide)
    first_grad[...] = wide[...].astype(bf16)
    small[...] = jnp.zeros_like(small)
    expand_backward(
        sz, me, s3, n3, first_grad, act1, slope1, row_of(gain_e, 1), up1, down1, grad, (wide, turned, blocks), pack, small
    )
    rows = sz.packed(sz.expand_full)
    put_small(pack, sz.expand_full, rows, small)
    ship(sz.exchanges["A"], me, replica, pack, rows, keep, send)


def output_kernel(sz, h_ref, act_ref, down, down_b, out_keep, out_send, turned, blocks):
    me = lax.axis_index("section")
    last = expand_output(h_ref, act_ref, down, row_of(down_b, 1)).astype(bf16)
    put_rows(sz, last, me, turned, blocks, out_keep, out_send)


def expand_kernel(sz, h, normed, grad, act, slope, up, down, gain, dh_ref, keep, send, total, turned, blocks, pack, small):
    me, replica = lax.axis_index("section"), lax.axis_index("dp")
    small[...] = jnp.zeros_like(small)
    expand_backward(
        sz, me, h, normed, grad, act, slope, row_of(gain, 0), up, down, dh_ref, (total, turned, blocks), pack, small
    )
    rows = sz.packed(sz.expand_full)
    put_small(pack, sz.expand_full, rows, small)
    ship(sz.exchanges["C"], me, replica, pack, rows, keep, send)


def attend_core_kernel(sz, grad, output, qkv, lse, proj, dctx, bias0, bias1):
    bias0[...] = window_bias(sz, 0)
    bias1[...] = window_bias(sz, 1)
    attend_core_backward(sz, grad, output, qkv, lse, proj, dctx, (bias0, bias1))


def attend_kernel(sz, layer, *refs):
    h, normed, grad, ctx, proj, triple, gain, flags = refs[:8]
    if layer == 0:
        in_keep, in_send, keep, send, total, turned, blocks, pack, small = refs[8:]
        target = total
    else:
        target, keep, send, total, turned, blocks, pack, small = refs[8:]
    me, replica = lax.axis_index("section"), lax.axis_index("dp")
    small[...] = jnp.zeros_like(small)
    rows = sz.packed(sz.attend_full)
    after = attend_backward(
        sz, me, h, normed, grad, ctx, proj, row_of(gain, layer), triple, target, (total, turned, blocks), pack, small
    )
    if layer == 0:
        masked = flags[:, :1] > 0.5
        put_vector(small, after, jnp.sum(jnp.where(masked, total[...], 0.0), axis=0, keepdims=True))
        put_rows(sz, jnp.where(masked, 0.0, total[...]).astype(bf16), me, turned, blocks, in_keep, in_send)
    put_small(pack, sz.attend_full, rows, small)
    ship(sz.exchanges["DB"[layer]], me, replica, pack, rows, keep, send)


def unpack(exchange, me, replica, source, target):
    shard = target.shape[0] // exchange.shards
    for place in range(exchange.shards):
        options = [exchange.offset(core, place) for core in range(2)]
        offset = jnp.where(me & 1 == 0, options[0], options[1])
        at = pl.multiple_of((exchange.shard_of(replica) ^ offset) * shard, 16)
        target[pl.ds(at, shard), :] = source[place * shard : (place + 1) * shard, :]


def widen_tiles(source, base, target):
    r, columns = target.shape
    for tile in range(columns // LANES):
        target[:, tile * LANES : (tile + 1) * LANES] = source[base + tile * r : base + (tile + 1) * r, :].astype(f32)


def widen_expand(sz, source, targets, moves):
    _, _, up, down = targets
    widen_tiles(source, 0, up)
    moves[2].start()
    widen_tiles(source, sz.hidden // LANES * sz.cut, down)
    moves[3].start()


def widen_attend(sz, source, targets, moves):
    triple, output, _, _ = targets
    widen_tiles(source, 0, triple)
    moves[0].start()
    widen_tiles(source, 3 * sz.tiles * sz.cut, output)
    moves[1].start()


def early_kernel(sz, *refs):
    (expand_in, attend_in), (out_own, out_core, in_own, in_core, across) = refs[:2], refs[2:7]
    (out_global, out_local, in_global, in_local), outs, vectors = refs[7:11], refs[11:15], refs[15]
    expand, attend, targets, wide, sems = refs[16], refs[17], refs[18:22], refs[22], refs[23]
    me, replica = lax.axis_index("section"), lax.axis_index("dp")
    moves = [pltpu.make_async_copy(target, out.at[1], sems.at[i]) for i, (target, out) in enumerate(zip(targets, outs))]
    unpack(sz.exchanges["A"], me, replica, expand_in, expand)
    widen_expand(sz, expand, targets, moves)
    unpack(sz.exchanges["B"], me, replica, attend_in, attend)
    widen_attend(sz, attend, targets, moves)
    vectors[: sz.small_rows, :] = attend[sz.attend_full : sz.attend_full + sz.small_rows, :].astype(f32)
    vectors[sz.small_rows :, :] = expand[sz.expand_full : sz.expand_full + sz.small_rows, :].astype(f32)
    row_parts = (
        (out_own.at[0], out_core.at[0], across.at[0], across.at[1]),
        (in_own.at[0], in_core.at[0], across.at[2], across.at[3]),
    )
    per_image = sz.sections // sz.images
    for which, (to_global, to_local) in enumerate(((out_global, out_local), (in_global, in_local))):
        for k in range(4):
            section = me ^ k
            image, crop = section // per_image, section % per_image
            turned = jnp.concatenate(
                [
                    row_parts[which][k][tile * sz.cut : (tile + 1) * sz.cut, :].astype(f32)
                    for tile in range(sz.rows // LANES)
                ],
                axis=1,
            )
            to_global[section] = turned[:, : sz.global_len]
            turned = jnp.concatenate([turned, jnp.zeros((LANES - sz.cut, sz.rows), f32)], axis=0)
            wide[...] = turned.T
            for at in range(sz.locals):
                start = sz.global_len + at * sz.local_len
                to_local[crop * sz.locals + at, :, pl.ds(image, 1), :] = wide[
                    start : start + sz.local_len, : sz.cut
                ].reshape(sz.local_len, 1, sz.cut)
    for move in moves:
        move.wait()


def finish_kernel(sz, *refs):
    expand_in, attend_in, later_vectors = refs[:3]
    (token, gain_a, shift_a, pair, output_b, gain_e, shift_e, up_b, down_b), outs = refs[7:16], refs[16:20]
    expand, attend, targets, vectors, sems = refs[20], refs[21], refs[22:26], refs[26], refs[27]
    me, replica = lax.axis_index("section"), lax.axis_index("dp")
    moves = [pltpu.make_async_copy(target, out.at[0], sems.at[i]) for i, (target, out) in enumerate(zip(targets, outs))]
    unpack(sz.exchanges["C"], me, replica, expand_in, expand)
    widen_expand(sz, expand, targets, moves)
    unpack(sz.exchanges["D"], me, replica, attend_in, attend)
    widen_attend(sz, attend, targets, moves)
    width, tiles, cut = sz.width, sz.tiles, sz.cut
    row = lax.broadcasted_iota(jnp.int32, (width, cut), 0)
    column = lax.broadcasted_iota(jnp.int32, (width, cut), 1)
    pick = jnp.where(row == column + me * cut, 1.0, 0.0).astype(bf16)
    row = lax.broadcasted_iota(jnp.int32, (2 * width, 2 * cut), 0)
    column = lax.broadcasted_iota(jnp.int32, (2 * width, 2 * cut), 1)
    pick_pair = jnp.where(row == column + me * 2 * cut, 1.0, 0.0).astype(bf16)
    hidden_tiles, up_tiles = sz.hidden // LANES, sz.hidden_cut // LANES
    vectors[: sz.small_rows, :] = attend[sz.attend_full : sz.attend_full + sz.small_rows, :].astype(f32)
    vectors[sz.small_rows :, :] = expand[sz.expand_full : sz.expand_full + sz.small_rows, :].astype(f32)
    for layer, held in enumerate((vectors, later_vectors)):
        one = slice(layer, layer + 1)

        def vector(at, tiles_in):
            return jnp.concatenate([held[at + t : at + t + 1, :] for t in range(tiles_in)], axis=1)

        def picked(at):
            return dot(vector(at, tiles).astype(bf16), pick)

        gain_a[one, :] = picked(0)
        shift_a[one, :] = picked(tiles)
        pair[one, :] = dot(vector(2 * tiles, 2 * tiles).astype(bf16), pick_pair)
        output_b[one, :] = picked(4 * tiles)
        if layer == 0:
            token[...] = picked(5 * tiles)
        base = sz.small_rows
        gain_e[one, :] = picked(base)
        shift_e[one, :] = picked(base + tiles)
        for tile in range(up_tiles):
            up_b[one, tile * LANES : (tile + 1) * LANES] = held[pl.ds(base + 2 * tiles + me * up_tiles + tile, 1), :]
        down_b[one, :] = picked(base + 2 * tiles + hidden_tiles)
    for move in moves:
        move.wait()


VMEM = pl.BlockSpec(memory_space=pltpu.VMEM)
ANY = pl.BlockSpec(memory_space=pl.ANY)
HBM = pl.BlockSpec(memory_space=pltpu.HBM)
SMEM = pl.BlockSpec(memory_space=pltpu.SMEM)
DMA = pltpu.SemaphoreType.DMA


def call(body, name, outs, in_specs, scratch, args, flops, aliases=()):
    args = [
        pltpu.with_memory_space_constraint(arg, pltpu.HBM) if spec is HBM else arg for arg, spec in zip(args, in_specs)
    ]
    return pl.pallas_call(
        body,
        name=name,
        out_shape=tuple(jax.ShapeDtypeStruct(shape, kind) for shape, kind, _ in outs),
        in_specs=in_specs,
        out_specs=tuple(memory for _, _, memory in outs),
        scratch_shapes=[pltpu.VMEM(*item) if isinstance(item, tuple) else item for item in scratch],
        input_output_aliases=dict(aliases),
        compiler_params=pltpu.CompilerParams(vmem_limit_bytes=VMEM_MIB.get(name, 14) << 20),
        cost_estimate=pl.CostEstimate(flops=flops, bytes_accessed=1 << 20, transcendentals=0),
    )(*args)


def add(first, *others):
    total = first.astype(f32)
    for other in others:
        total = total + other.astype(f32)
    return lax.reduce_precision(total, 8, 7).astype(bf16)


def swap(value, partner_of):
    sections, replicas = lax.axis_size("section"), lax.axis_size("dp")
    route = []
    for section in range(sections):
        for replica in range(replicas):
            to_section, to_replica = partner_of(section, replica)
            route.append((section * replicas + replica, to_section * replicas + to_replica))
    return lax.ppermute(value, ("section", "dp"), route)


def other_core(section, replica):
    return section ^ 1, replica


def other_x(section, replica):
    return section ^ 2, replica


def along(orders, step):
    def partner_of(section, replica):
        axis = orders[section & 1][step]
        return (section ^ 2, replica) if axis == X_AXIS else (section, replica ^ (1 << axis))

    return partner_of


class Sequence:
    def __init__(self):
        self.last = None

    def after(self, value):
        return value if self.last is None else lax.optimization_barrier((value, self.last))[0]

    def mark(self, value):
        self.last = value
        return value


def reduce_steps(exchange, order, keep, send):
    orders = exchange.orders
    core = swap(send, other_core)
    yield
    core = order.after(core)
    half = keep.shape[0] // 2
    moved = swap(order.mark(add(keep[half:], core[half:])), along(orders, 0))
    yield
    moved = order.after(moved)
    mine = add(keep[:half], core[:half], moved)
    for step in range(1, len(orders[0])):
        half = mine.shape[0] // 2
        moved = swap(order.mark(mine[half:]), along(orders, step))
        yield
        mine = add(mine[:half], order.after(moved))
    for axis in exchange.rest:
        moved = swap(order.mark(mine), along(([axis], [axis]), 0))
        yield
        mine = add(mine, order.after(moved))
    back = [[axis for axis in order_of if axis != X_AXIS] for order_of in orders]
    for step in reversed(range(len(back[0]))):
        moved = swap(order.mark(mine), along(back, step))
        yield
        mine = jnp.concatenate([mine, order.after(moved)], axis=0)
    yield mine


def row_steps(order, out_rows, in_rows):
    cores = [swap(send, other_core) for _, send in (out_rows, in_rows)]
    yield
    cores[0] = order.after(cores[0])
    across = swap(order.mark(jnp.stack([out_rows[0][1], cores[0][1], in_rows[0][1], cores[1][1]])), other_x)
    yield
    yield out_rows[0], cores[0], in_rows[0], cores[1], order.after(across)


def per_device(
    global_rows, local_rows, patch_rank, ratio_bin, mask_token, attend_gain, attend_shift, triple_weight,
    pair_bias, output_weight, output_bias, expand_gain, expand_shift, up_weight, up_bias, down_weight,
    down_bias, grad_global, grad_local,
):
    sections, replicas = lax.axis_size("section"), lax.axis_size("dp")
    sz = Sizes(global_rows, local_rows, up_weight, sections, replicas)
    width, rows, hidden = sz.width, sz.rows, sz.hidden
    sets = [rows_of.transpose(0, 2, 1, 3) for rows_of in (global_rows, grad_global)]
    many = [rows_of.transpose(1, 2, 0, 3) for rows_of in (local_rows, grad_local)]
    weights = (triple_weight, output_weight, up_weight, down_weight)
    smalls = (
        patch_rank, mask_token, attend_gain, attend_shift, pair_bias, output_bias, expand_gain, expand_shift, up_bias,
        down_bias,
    )
    wide = ((rows, width), bf16)
    triple_rows = ((rows, 3 * width), bf16)
    hidden_rows = ((rows, hidden), bf16)
    lse = ((16, up_to(max(length for _, length in sz.windows), LANES)), f32)
    flags = ((rows, LANES), f32)
    wide_f32 = ((rows, width), f32)
    turned = ((width, rows), bf16)
    small = ((sz.small_rows, LANES), f32)
    share = ((2, sz.extra, LANES), bf16)
    stage = ((sections, sz.extra, LANES), bf16)
    windows = [((length, length), f32) for _, length in sz.windows]
    totals = [sz.packed(full) for full in (sz.expand_full, sz.attend_full)]
    packs = [((sections, total, LANES), bf16) for total in totals]
    parts = [((2 * total, LANES), bf16) for total in totals]
    vectors = ((2, width), bf16)
    blocks = [(weight.shape[1:], bf16) for weight in weights]
    shared = [wide_f32, turned, turned]

    def run_kernel(body, name, outs, scratch, args):
        return call(
            lambda *refs: body(sz, *refs), name, [out + (VMEM,) for out in outs], [VMEM] * len(args), scratch, args, 4 << 30
        )

    (
        s0, s1, s2, s3, n0, n1, n2, qkv0, qkv1, lse0, lse1, ctx0, ctx1, act0, act1, slope0, masked, grad,
        triple0, triple1, output0, output1, up0, down0, down1, gain_a, gain_e, down_b, keep, send,
    ) = call(
        lambda *refs: front_kernel(sz, *refs),
        "front",
        [
            out + (VMEM,)
            for out in [wide] * 7 + [triple_rows] * 2 + [lse] * 2 + [wide] * 2 + [hidden_rows] * 3 + [flags, wide]
            + [blocks[0]] * 2 + [blocks[1]] * 2 + [blocks[2]] + [blocks[3]] * 2 + [vectors] * 3 + [parts[0]] * 2
        ],
        [HBM] * 14 + [SMEM] + [HBM] * 4,
        [blocks[2]]
        + [(one.shape, one.dtype) for one in (patch_rank, mask_token, attend_shift, pair_bias, output_bias)]
        + [(one.shape, one.dtype) for one in (expand_shift, up_bias)]
        + [(sets[0].shape[1:], bf16), ((sz.locals,) + many[0].shape[1:], bf16)] * 2
        + [wide, hidden_rows, wide_f32] + windows + [turned] * 2 + [packs[0], small, wide, DMA((22,))],
        (sets[0], many[0], sets[1], many[1], *smalls, ratio_bin, *weights),
        8 << 30,
    )
    order = Sequence()
    chains, results = {}, {}
    chains["A"] = reduce_steps(sz.exchanges["A"], order, keep, send)
    core_scratch = [wide] + windows
    flow = {"grad": grad}

    def core_kernel(name, output, qkv, lse_of):
        proj, = run_kernel(
            attend_core_kernel, name, [triple_rows], core_scratch, (order.after(flow["grad"]), output, qkv, lse_of)
        )
        flow["proj"] = order.mark(proj)

    def later_core():
        core_kernel("later_core", output1, qkv1, lse1)

    def later_attend():
        dh, keep, send = run_kernel(
            lambda sz, *refs: attend_kernel(sz, 1, *refs), "later_attend", [wide] + [parts[1]] * 2,
            shared + [packs[1], small],
            (s2, n2, flow["grad"], ctx1, order.after(flow["proj"]), triple1, gain_a, masked),
        )
        flow["grad"] = order.mark(dh)
        chains["B"] = reduce_steps(sz.exchanges["B"], order, keep, send)

    def expand():
        dh, keep, send = run_kernel(
            expand_kernel, "expand_back", [wide] + [parts[0]] * 2, shared + [packs[0], small],
            (s1, n1, order.after(flow["grad"]), act0, slope0, up0, down0, gain_e),
        )
        flow["grad"] = order.mark(dh)
        chains["C"] = reduce_steps(sz.exchanges["C"], order, keep, send)

    def core():
        core_kernel("attend_core", output0, qkv0, lse0)

    def attend():
        in_keep, in_send, keep, send = run_kernel(
            lambda sz, *refs: attend_kernel(sz, 0, *refs), "attend_back", [share] * 2 + [parts[1]] * 2,
            shared + [packs[1], small],
            (s0, n0, flow["grad"], ctx0, order.after(flow["proj"]), triple0, gain_a, masked),
        )
        flow["in"] = (order.mark(in_keep), in_send)
        chains["D"] = reduce_steps(sz.exchanges["D"], order, keep, send)

    def output_rows():
        out_rows = run_kernel(
            output_kernel, "output_rows", [share] * 2, [turned, turned], (s3, order.after(act1), down1, down_b)
        )
        order.mark(out_rows[0])
        chains["R"] = row_steps(order, out_rows, flow["in"])

    cut = sz.cut
    weight_outs = [(2, cut, 3 * width), (2, cut, width), (2, cut, hidden), (2, sz.hidden_cut, width)]
    row_outs = [(sz.all_globals, cut, sz.global_len), local_rows.shape[1:3] + (sz.images, cut)] * 2
    both_small = ((2 * sz.small_rows, LANES), f32)
    finish_scratch = [((total, LANES), bf16) for total in totals] + [(shape[1:], f32) for shape in weight_outs]

    def early():
        expand_of, attend_of = (order.after(results[step]) for step in "AB")
        flow["early"] = call(
            lambda *refs: early_kernel(sz, *refs), "early",
            [(shape, f32, VMEM) for shape in row_outs] + [(shape, f32, ANY) for shape in weight_outs] + [both_small + (VMEM,)],
            [VMEM] * 7, finish_scratch + [flags, DMA((4,))], (expand_of, attend_of, *results["R"]), 1 << 28,
        )
        order.mark(flow["early"][-1])

    kernels = {
        "later_core": later_core, "later_attend": later_attend, "expand": expand, "core": core, "attend": attend,
        "output": output_rows, "early": early,
    }
    for plan in PLAN:
        for step in plan.split():
            if step == "early":
                for _ in range(3, len(sz.exchanges["A"].rest) + len(sz.exchanges["A"].axes)):
                    for name in "ABCD":
                        results[name] = next(chains[name], results.get(name))
            if step in kernels:
                kernels[step]()
            else:
                results[step] = next(chains[step], results.get(step))
    *row_values, triple, output, up, down, late_vectors = flow["early"]
    vector_outs = [(1, cut), (2, cut), (2, cut), (2, 2 * cut)] + [(2, cut)] * 3 + [(2, sz.hidden_cut), (2, cut)]
    final = call(
        lambda *refs: finish_kernel(sz, *refs), "finish",
        [(shape, f32, VMEM) for shape in vector_outs] + [(shape, f32, ANY) for shape in weight_outs],
        [VMEM] * 3 + [ANY] * 4, finish_scratch + [both_small, DMA((4,))],
        (order.after(results["C"]), results["D"], late_vectors, triple, output, up, down), 1 << 28,
        [(3 + i, len(vector_outs) + i) for i in range(4)],
    )
    token, gain_a, shift_a, pair, output_b, gain_e, shift_e, up_b, down_b, triple, output, up, down = final
    shape = global_rows.shape[:2] + (cut, sz.global_len)
    return (
        row_values[0].reshape(shape).transpose(0, 1, 3, 2), row_values[1].transpose(2, 0, 1, 3),
        row_values[2].reshape(shape).transpose(0, 1, 3, 2), row_values[3].transpose(2, 0, 1, 3),
        token, gain_a, shift_a, triple, pair, output, output_b, gain_e, shift_e, up, up_b, down, down_b,
    )


def solution(mesh):
    rows, copied = P("dp", None, None, None), P()
    in_specs = (rows, rows, P("dp", None, None), P("dp")) + (copied,) * 13 + (rows, rows)
    wide, flat, deep = P("dp", None, None, "section"), P(None, "section"), P(None, "section", None)
    out_specs = (
        wide, wide, wide, wide, flat, flat, flat, deep, flat, deep, flat, flat, flat, deep, flat, deep, flat,
    )
    return jax.shard_map(per_device, mesh=mesh, in_specs=in_specs, out_specs=out_specs, check_vma=False)
```
